256 devices in a mesh: img: 32 (over z, x_lo, core), row: 8 (over x_hi, y).
Axes of the slice: x: 4 (x_hi: 2, x_lo: 2; x = x_hi * 2 + x_lo), y: 4, z: 8, core: 2. Of those that a mesh axis runs over, the one named last changes fastest.
Arguments:
- llm_hidden: bfloat16 [16384, 6656], P('img', 'row'), may hold values from -96 to 96
- slot_start: int32 [32], P('img'), may hold values from 0 to 448
- image_group: int32 [32], replicated, may hold values from 0 to 31, each once
- timesteps: int32 [32], P('img'), may hold values from 0 to 999
- latents: float32 [32, 4, 64, 128], P('img', None, 'row'), may hold values from -6 to 6
- noise: float32 [32, 4, 64, 128], P('img', None, 'row'), may hold values from -6 to 6
- kv_weight: bfloat16 [6656, 640], P('row'), may hold values from -0.078125 to 0.078125
- in_weight: bfloat16 [3, 3, 320, 4], replicated, may hold values from -1 to 1
- res_weight: bfloat16 [3, 3, 320, 320], replicated, may hold values from -0.109375 to 0.109375
- query_weight: bfloat16 [320, 320], replicated, may hold values from -0.3125 to 0.3125
- out_weight: bfloat16 [320, 320], replicated, may hold values from -0.3125 to 0.3125
- cotangent: bfloat16 [32, 320, 64, 128], P('img', None, 'row'), may hold values from -6 to 6
Outputs:
- block_out: bfloat16 [32, 320, 64, 128], P('img', None, 'row')
- grad_hidden: bfloat16 [16384, 6656], P('img', 'row')
- grad_kv_weight: bfloat16 [6656, 640], P('row')
- grad_res_weight: bfloat16 [3, 3, 320, 320], replicated
- grad_query_weight: bfloat16 [320, 320], replicated
- grad_out_weight: bfloat16 [320, 320], replicated
The draws below stay inside these ranges and needn't reach their ends.
Inputs may be any that keep to these rules, and one draw needn't show every extreme that they name: `slot_start`: each image's 64 condition rows lie inside its own sequence of 512 tokens. `image_group`: every group denoises exactly one image.
All inputs are finite; a program needn't handle non-finite values.
Results may differ from the reference program's by a relative error of at most 0.035.
The reference program's roundings to bfloat16 on the way count: a program that leaves them out, or rounds other values in their place, can miss the bound.
Values may be sent and summed in bfloat16 or wider, within the bound.
A program may use at most 128 MiB of HBM per device.

```python
import math
import jax
import jax.numpy as jnp
from jax import lax

COND = 6656
CHANNELS = 320
HEAD_DIM = 64
LAT_CH = 4
SLOTS = 64
WIDTH = 128
SEQ_DEV = 512
IMAGES = 32
TOKENS = 16384
HEIGHT = 64


def draw_llm_hidden(key, part):
    base_key = jax.random.fold_in(jax.random.fold_in(key, 11), 0)
    entries = jax.random.normal(base_key, (TOKENS, COND), jnp.float32)
    entries = jnp.clip(entries, -6.0, 6.0)
    return entries.astype(jnp.bfloat16)


def place_ends(array, own_key, smallest, top_value):
    extent = array.shape
    index_at = [jax.random.randint(jax.random.fold_in(own_key, axis), (), 0, extent[axis]) for axis in range(len(extent))]
    array = array.at[tuple(index_at)].set(smallest)
    longest = extent.index(max(extent))
    index_at[longest] = (index_at[longest] + 1) % extent[longest]
    return array.at[tuple(index_at)].set(top_value)


def strengthened(array, own_key, source, target, parts, factor):
    owner, partner = [(jnp.arange(array.shape[dim]) // (array.shape[dim] // parts)).reshape([-1 if axis == dim else 1 for axis in range(array.ndim)]) for dim in (source, target)]
    chosen = jax.random.permutation(own_key, parts)[partner]
    strong = (owner == chosen) | (owner == (partner + parts // 2) % parts)
    return jnp.where(strong, factor * array, array)


def level_of(key, extent, shards, smallest, largest):
    loudness, own = 1.0, jax.random.fold_in(key, 6)
    for position, parts in shards:
        draws = jnp.exp(jax.random.uniform(jax.random.fold_in(own, position), (parts,), jnp.float32, smallest / len(shards), largest / len(shards)))
        loudness = loudness * jnp.repeat(draws, extent[position] // parts).reshape([-1 if axis == position else 1 for axis in range(len(extent))])
    return loudness


def scatter_about(rng, extent, width, limit, shards=(), kind=jnp.bfloat16):
    result = width * jax.random.normal(rng, extent, jnp.float32)
    if shards:
        result = result * level_of(rng, extent, shards, -0.22, 0.18)
    return jnp.clip(result, -limit, limit).astype(kind)


def noise_with(rng, dims, deviation, limit, pieces, heavy, kind=jnp.bfloat16):
    array = deviation * jax.random.normal(rng, dims, jnp.float32)
    if pieces:
        array = array * level_of(rng, dims, pieces, -0.22, 0.18)
    return jnp.clip(strengthened(array, jax.random.fold_in(rng, 3), *heavy), -limit, limit).astype(kind)


def setup_inputs(seed: int = 0) -> dict:
    seeds = jax.random.split(jax.random.key(seed), 13)
    llm_hidden = draw_llm_hidden(jax.random.fold_in(seeds[12], 71), 0)
    slot_start = place_ends(jax.random.randint(seeds[1], (IMAGES,), 0, SEQ_DEV - SLOTS + 1), jax.random.fold_in(seeds[1], 1), 0, SEQ_DEV - SLOTS).astype(jnp.int32)
    image_group = jax.random.permutation(seeds[2], IMAGES).astype(jnp.int32)
    timesteps = place_ends(jax.random.randint(seeds[3], (IMAGES,), 0, 1000), jax.random.fold_in(seeds[3], 1), 0, 999).astype(jnp.int32)
    latents = scatter_about(seeds[4], (IMAGES, LAT_CH, HEIGHT, WIDTH), 1.0, 6.0, ((0, 32), (2, 8)), jnp.float32)
    noise = scatter_about(seeds[5], (IMAGES, LAT_CH, HEIGHT, WIDTH), 1.0, 6.0, ((0, 32), (2, 8)), jnp.float32)
    kv_weight = scatter_about(seeds[6], (COND, 2 * CHANNELS), COND ** -0.5, 0.078125, ((0, 8),))
    in_weight = scatter_about(seeds[7], (3, 3, CHANNELS, LAT_CH), (9 * LAT_CH) ** -0.5, 1.0)
    res_weight = scatter_about(seeds[8], (3, 3, CHANNELS, CHANNELS), (9 * CHANNELS) ** -0.5, 0.109375)
    query_weight = scatter_about(seeds[9], (CHANNELS, CHANNELS), CHANNELS ** -0.5, 0.3125)
    out_weight = scatter_about(seeds[10], (CHANNELS, CHANNELS), CHANNELS ** -0.5, 0.3125)
    cotangent = noise_with(seeds[11], (IMAGES, CHANNELS, HEIGHT, WIDTH), 1.0, 6.0, ((0, 32), (2, 8)), (0, 1, 32, 2.75))
    return {"llm_hidden": llm_hidden, "slot_start": slot_start, "image_group": image_group, "timesteps": timesteps, "latents": latents, "noise": noise, "kv_weight": kv_weight, "in_weight": in_weight, "res_weight": res_weight, "query_weight": query_weight, "out_weight": out_weight, "cotangent": cotangent}


def weighted_product(form, left, right):
    return jnp.einsum(form, left.astype(jnp.float32), right.astype(jnp.float32))

def noise_levels():
    plan = jnp.linspace(0.00085 ** 0.5, 0.012 ** 0.5, 1000, dtype=jnp.float32) ** 2
    return jnp.exp(jnp.cumsum(jnp.log(1.0 - plan)))

def noisy_input(latent, noise_one, timestep):
    levels = noise_levels()
    picked = jnp.sum(jnp.where(jnp.arange(levels.shape[0]) == timestep, levels, 0.0))
    return (jnp.sqrt(picked) * latent + jnp.sqrt(1.0 - picked) * noise_one).astype(jnp.bfloat16)

def time_shift(timestep, channel_total):
    half_count = channel_total // 2
    frequency = jnp.exp(-math.log(10000.0) * jnp.arange(half_count, dtype=jnp.float32) / half_count)
    angles = timestep.astype(jnp.float32) * frequency
    return jnp.concatenate([jnp.cos(angles), jnp.sin(angles)])

def pad_columns(field):
    return jnp.pad(field, ((0, 0), (0, 0), (1, 1)))

def convolve(padded, weight, row_count, col_count):
    running = jnp.zeros((weight.shape[2], row_count * col_count), jnp.float32)
    for row_tap in range(3):
        for col_tap in range(3):
            window = padded[:, row_tap:row_tap + row_count, col_tap:col_tap + col_count].reshape(padded.shape[0], row_count * col_count)
            running = running + jnp.dot(weight[row_tap, col_tap], window, preferred_element_type=jnp.float32)
    return running

def filter_grad(padded, upstream, row_count, col_count):
    tap_list = []
    for row_tap in range(3):
        for col_tap in range(3):
            window = padded[:, row_tap:row_tap + row_count, col_tap:col_tap + col_count].reshape(padded.shape[0], row_count * col_count)
            tap_list.append(lax.dot_general(upstream, window, (((1,), (1,)), ((), ())), preferred_element_type=jnp.float32))
    return jnp.stack(tap_list).reshape(3, 3, upstream.shape[0], padded.shape[0])

def block_pass(noisy, timestep, group_kv, upstream, in_weight, res_weight, query_weight, out_weight):
    channel_total = in_weight.shape[2]
    row_count, col_count = (noisy.shape[1], noisy.shape[2])
    latent_cell_count = row_count * col_count
    condition_slot_count = group_kv.shape[0]
    head_count = channel_total // HEAD_DIM
    logit_scale = HEAD_DIM ** (-0.5)
    noisy_pad = pad_columns(jnp.pad(noisy, ((0, 0), (1, 1), (0, 0))))
    first = convolve(noisy_pad, in_weight, row_count, col_count)
    hidden_act = jax.nn.silu(first + time_shift(timestep, channel_total)[:, None]).astype(jnp.bfloat16)
    act_pad = pad_columns(jnp.pad(hidden_act.reshape(channel_total, row_count, col_count), ((0, 0), (1, 1), (0, 0))))
    residual = (first + convolve(act_pad, res_weight, row_count, col_count)).astype(jnp.bfloat16)
    query = jnp.dot(query_weight, residual, preferred_element_type=jnp.float32).astype(jnp.bfloat16)
    query_per_head = query.reshape(head_count, HEAD_DIM, latent_cell_count)
    key_matrix = group_kv[:, :channel_total].reshape(condition_slot_count, head_count, HEAD_DIM)
    value_matrix = group_kv[:, channel_total:].reshape(condition_slot_count, head_count, HEAD_DIM)
    score_matrix = weighted_product('isf,tis->itf', query_per_head, key_matrix) * logit_scale
    softmax_full = jax.nn.softmax(score_matrix, axis=1)
    softmax_reduced_precision = softmax_full.astype(jnp.bfloat16)
    attention_output = weighted_product('cuo,ucb->cbo', softmax_reduced_precision, value_matrix).astype(jnp.bfloat16).reshape(channel_total, latent_cell_count)
    block_out = (residual.astype(jnp.float32) + jnp.dot(out_weight, attention_output, preferred_element_type=jnp.float32)).astype(jnp.bfloat16)
    upstream = upstream.reshape(channel_total, latent_cell_count)
    out_grad = lax.dot_general(upstream, attention_output, (((1,), (1,)), ((), ())), preferred_element_type=jnp.float32)
    grad_att = lax.dot_general(out_weight, upstream, (((0,), (0,)), ((), ())), preferred_element_type=jnp.float32).astype(jnp.bfloat16)
    head_gradient = grad_att.reshape(head_count, HEAD_DIM, latent_cell_count)
    probability_gradient = weighted_product('isf,tis->itf', head_gradient, value_matrix)
    score_gradient = (logit_scale * softmax_full * (probability_gradient - lax.optimization_barrier(jnp.sum(softmax_full * probability_gradient, axis=1, keepdims=True)))).astype(jnp.bfloat16)
    query_gradient = weighted_product('cuo,ucb->cbo', score_gradient, key_matrix).astype(jnp.bfloat16).reshape(channel_total, latent_cell_count)
    key_gradient = weighted_product('exv,ewv->xew', score_gradient, query_per_head).reshape(condition_slot_count, channel_total)
    value_gradient = weighted_product('exv,ewv->xew', softmax_reduced_precision, head_gradient).reshape(condition_slot_count, channel_total)
    grad_kv = jnp.concatenate([key_gradient, value_gradient], axis=1)
    query_grad = lax.dot_general(query_gradient, residual, (((1,), (1,)), ((), ())), preferred_element_type=jnp.float32)
    grad_resid = (upstream.astype(jnp.float32) + lax.dot_general(query_weight, query_gradient, (((0,), (0,)), ((), ())), preferred_element_type=jnp.float32)).astype(jnp.bfloat16)
    res_grad = filter_grad(act_pad, grad_resid, row_count, col_count)
    return (block_out.reshape(channel_total, row_count, col_count), grad_kv, res_grad, query_grad, out_grad)

def reference(llm_hidden, slot_start, image_group, timesteps, latents, noise, kv_weight, in_weight, res_weight, query_weight, out_weight, cotangent):
    image_count = slot_start.shape[0]
    seq_tokens = llm_hidden.shape[0] // image_count
    offsets = jnp.arange(image_count, dtype=jnp.int32) * seq_tokens + slot_start.astype(jnp.int32)

    def select_rows(first_row):
        return lax.dynamic_slice_in_dim(llm_hidden, first_row, SLOTS, 0)
    condition = jax.vmap(select_rows)(offsets)
    kv_rows = weighted_product('isf,fk->isk', condition, kv_weight).astype(jnp.bfloat16)
    group_kv = jnp.zeros_like(kv_rows).at[image_group].set(kv_rows)
    channel_total = in_weight.shape[2]
    zero_res = jnp.zeros((3, 3, channel_total, channel_total), jnp.float32)
    zero_square = jnp.zeros((channel_total, channel_total), jnp.float32)

    def per_group(running, scan_items):
        latent, noise_one, timestep, kv_one, upstream = scan_items
        noisy = noisy_input(latent, noise_one, timestep)
        block_out, grad_kv, res_grad, query_grad, out_grad = block_pass(noisy, timestep, kv_one, upstream, in_weight, res_weight, query_weight, out_weight)
        return ((running[0] + res_grad, running[1] + query_grad, running[2] + out_grad), (block_out, grad_kv.astype(jnp.bfloat16)))
    running, (block_outs, grad_groups) = lax.scan(per_group, (zero_res, zero_square, zero_square), (latents, noise, timesteps, group_kv, cotangent))
    grad_images = grad_groups[image_group]
    grad_condition = weighted_product('isk,fk->isf', grad_images, kv_weight).astype(jnp.bfloat16)
    positions = (offsets[:, None] + jnp.arange(SLOTS, dtype=jnp.int32)[None, :]).reshape(-1)
    grad_hidden = jnp.zeros_like(llm_hidden).at[positions].set(grad_condition.reshape(-1, llm_hidden.shape[1]))
    grad_kv_weight = (weighted_product('isf,isk->fk', condition, grad_images) * (image_count * SLOTS) ** (-0.5)).astype(jnp.bfloat16)
    weight_scale = (image_count * latents.shape[2] * latents.shape[3]) ** (-0.5)
    return (block_outs, grad_hidden, grad_kv_weight, (running[0] * weight_scale).astype(jnp.bfloat16), (running[1] * weight_scale).astype(jnp.bfloat16), (running[2] * weight_scale).astype(jnp.bfloat16))
```

```python
import functools
import math

import jax
import jax.numpy as jnp
from jax import lax
from jax.experimental import pallas as pl
from jax.experimental.pallas import tpu as pltpu
from jax.sharding import PartitionSpec as P

HEAD_DIM = 64
SLOTS = 64
MESH = pl.DeviceIdType.MESH
CHANNELS = 320
IMGS, ROWS = 32, 8
F32, BF16 = jnp.float32, jnp.bfloat16


def extended(cells, sides, width):
    for axis, dim in sides:
        count = lax.axis_size(axis)
        ends = count - 1
        head = lax.slice_in_dim(cells, 0, width, axis=dim)
        tail = lax.slice_in_dim(cells, cells.shape[dim] - width, cells.shape[dim], axis=dim)
        cells = jnp.concatenate(
            [
                lax.ppermute(tail, axis, [(i, (i + 1) % count) for i in range(ends)]),
                cells,
                lax.ppermute(head, axis, [((i + 1) % count, i) for i in range(ends)]),
            ],
            axis=dim,
        )
    return cells


def weighted_product(form, left, right):
    return jnp.einsum(form, left, right, preferred_element_type=jnp.float32)


def noisy_input(latent, noise_one, timestep):
    plan = jnp.linspace(0.00085**0.5, 0.012**0.5, 1000, dtype=jnp.float32) ** 2
    picked = jnp.exp(jnp.sum(jnp.where(jnp.arange(1000) <= timestep, jnp.log(1.0 - plan), 0.0)))
    return (jnp.sqrt(picked) * latent + jnp.sqrt(1.0 - picked) * noise_one).astype(jnp.bfloat16)


def time_shift(timestep, channel_total):
    half_count = channel_total // 2
    frequency = jnp.exp(-math.log(10000.0) * jnp.arange(half_count, dtype=jnp.float32) / half_count)
    angles = timestep.astype(jnp.float32) * frequency
    return jnp.concatenate([jnp.cos(angles), jnp.sin(angles)])


def pad_columns(field):
    return jnp.pad(field, ((0, 0), (0, 0), (1, 1)))


def convolve(padded, weight, row_count, col_count):
    running = jnp.zeros((weight.shape[2], row_count * col_count), jnp.float32)
    for row_tap in range(3):
        for col_tap in range(3):
            window = padded[
                :, row_tap : row_tap + row_count, col_tap : col_tap + col_count
            ].reshape(padded.shape[0], row_count * col_count)
            running = running + jnp.dot(
                weight[row_tap, col_tap], window, preferred_element_type=jnp.float32
            )
    return running


def filter_grad(padded, upstream, row_count, col_count):
    tap_list = []
    for row_tap in range(3):
        for col_tap in range(3):
            window = padded[
                :, row_tap : row_tap + row_count, col_tap : col_tap + col_count
            ].reshape(padded.shape[0], row_count * col_count)
            tap_list.append(
                lax.dot_general(
                    upstream, window, (((1,), (1,)), ((), ())), preferred_element_type=jnp.float32
                )
            )
    return jnp.stack(tap_list).reshape(3, 3, upstream.shape[0], padded.shape[0])


def block_pass(
    noisy, timestep, group_kv, upstream, in_weight, res_weight, query_weight, out_weight
):
    channel_total = in_weight.shape[2]
    row_count, col_count = (noisy.shape[1], noisy.shape[2])
    latent_cell_count = row_count * col_count
    condition_slot_count = group_kv.shape[0]
    head_count = channel_total // HEAD_DIM
    logit_scale = HEAD_DIM ** (-0.5)
    noisy_pad = pad_columns(extended(noisy, (("row", 1),), 1))
    first = convolve(noisy_pad, in_weight, row_count, col_count)
    hidden_act = jax.nn.silu(first + time_shift(timestep, channel_total)[:, None]).astype(
        jnp.bfloat16
    )
    act_pad = pad_columns(
        extended(hidden_act.reshape(channel_total, row_count, col_count), (("row", 1),), 1)
    )
    residual = (first + convolve(act_pad, res_weight, row_count, col_count)).astype(jnp.bfloat16)
    query = jnp.dot(query_weight, residual, preferred_element_type=jnp.float32).astype(jnp.bfloat16)
    query_per_head = query.reshape(head_count, HEAD_DIM, latent_cell_count)
    key_matrix = group_kv[:, :channel_total].reshape(condition_slot_count, head_count, HEAD_DIM)
    value_matrix = group_kv[:, channel_total:].reshape(condition_slot_count, head_count, HEAD_DIM)
    score_matrix = weighted_product("isf,tis->itf", query_per_head, key_matrix) * logit_scale
    softmax_full = jax.nn.softmax(score_matrix, axis=1)
    softmax_reduced_precision = softmax_full.astype(jnp.bfloat16)
    attention_output = (
        weighted_product("cuo,ucb->cbo", softmax_reduced_precision, value_matrix)
        .astype(jnp.bfloat16)
        .reshape(channel_total, latent_cell_count)
    )
    block_out = (
        residual.astype(jnp.float32)
        + jnp.dot(out_weight, attention_output, preferred_element_type=jnp.float32)
    ).astype(jnp.bfloat16)
    upstream = upstream.reshape(channel_total, latent_cell_count)
    out_grad = lax.dot_general(
        upstream, attention_output, (((1,), (1,)), ((), ())), preferred_element_type=jnp.float32
    )
    grad_att = lax.dot_general(
        out_weight, upstream, (((0,), (0,)), ((), ())), preferred_element_type=jnp.float32
    ).astype(jnp.bfloat16)
    head_gradient = grad_att.reshape(head_count, HEAD_DIM, latent_cell_count)
    probability_gradient = weighted_product("isf,tis->itf", head_gradient, value_matrix)
    score_gradient = (
        logit_scale
        * softmax_full
        * (
            probability_gradient
            - jnp.sum(softmax_full * probability_gradient, axis=1, keepdims=True)
        )
    ).astype(jnp.bfloat16)
    query_gradient = (
        weighted_product("cuo,ucb->cbo", score_gradient, key_matrix)
        .astype(jnp.bfloat16)
        .reshape(channel_total, latent_cell_count)
    )
    key_gradient = weighted_product("exv,ewv->xew", score_gradient, query_per_head).reshape(
        condition_slot_count, channel_total
    )
    value_gradient = weighted_product(
        "exv,ewv->xew", softmax_reduced_precision, head_gradient
    ).reshape(condition_slot_count, channel_total)
    grad_kv = jnp.concatenate([key_gradient, value_gradient], axis=1)
    query_grad = lax.dot_general(
        query_gradient, residual, (((1,), (1,)), ((), ())), preferred_element_type=jnp.float32
    )
    grad_resid = (
        upstream.astype(jnp.float32)
        + lax.dot_general(
            query_weight,
            query_gradient,
            (((0,), (0,)), ((), ())),
            preferred_element_type=jnp.float32,
        )
    ).astype(jnp.bfloat16)
    res_grad = filter_grad(act_pad, grad_resid, row_count, col_count)
    return (
        block_out.reshape(channel_total, row_count, col_count),
        grad_kv,
        res_grad,
        query_grad,
        out_grad,
    )


def place():
    img, row = lax.axis_index("img"), lax.axis_index("row")
    return img, row


def coords(img, row):
    z, low, core = lax.div(img, 4), lax.rem(lax.div(img, 2), 2), lax.rem(img, 2)
    return z, lax.div(row, 4) * 2 + low, lax.rem(row, 4), core


def device(z, x, y, core):
    return (z * 4 + lax.rem(x, 2) * 2 + core, lax.div(x, 2) * 4 + y)


def remote(src, dst, sems, slot, where):
    return pltpu.make_async_remote_copy(
        src_ref=src,
        dst_ref=dst,
        send_sem=sems.at[0, slot],
        recv_sem=sems.at[1, slot],
        device_id=where,
        device_id_type=MESH,
    )


def each(count, act, first=1):
    def body(k, carry):
        act(k)
        return carry

    lax.fori_loop(first, count, body, 0)


def rows16(index, count=16):
    return pl.ds(pl.multiple_of(index * 16, 16), count)


def greet(img, row, plane):
    barrier = pltpu.get_barrier_semaphore()

    def call(where):
        pl.semaphore_signal(barrier, inc=1, device_id=where, device_id_type=MESH)

    each(ROWS, lambda k: call((img, lax.rem(row + k, ROWS))))
    each(IMGS, lambda k: call((lax.rem(img + k, IMGS), row)))
    if plane:
        z, x, y, core = coords(img, row)
        other = 2 * (1 - lax.div(x, 2)) + (1 - lax.rem(x, 2))
        call(device(z, other, y, core))
    pl.semaphore_wait(barrier, ROWS - 1 + IMGS - 1 + int(plane))


class RowSum:
    def __init__(self, img, row, part, inbox, sems):
        self.img, self.row, self.part, self.inbox, self.sems = img, row, part, inbox, sems

    def copy(self, k):
        r = lax.rem(self.row + k, ROWS)
        src = self.part.at[lax.rem(r, 2), rows16(lax.div(r, 2))]
        return remote(src, self.inbox.at[k - 1], self.sems, k - 1, (self.img, r))

    def start(self):
        each(ROWS, lambda k: self.copy(k).start())

    def total(self):
        own = self.part[lax.rem(self.row, 2), rows16(lax.div(self.row, 2))].astype(F32)

        def body(k, acc):
            self.copy(k).wait_recv()
            return acc + self.inbox[k - 1].astype(F32)

        return lax.fori_loop(1, ROWS, body, own)

    def finish(self):
        each(ROWS, lambda k: self.copy(k).wait_send())


class Gather:
    def __init__(self, count, me, where, target, sems):
        self.count, self.me, self.where, self.target, self.sems = count, me, where, target, sems

    def copy(self, k):
        to = lax.rem(self.me + k, self.count)
        return remote(
            self.target(self.me), self.target(self.me), self.sems, k - 1, self.where(to)
        )

    def start(self):
        each(self.count, lambda k: self.copy(k).start())

    def wait(self):
        each(self.count, lambda k: self.copy(k).wait_recv())

    def finish(self):
        each(self.count, lambda k: self.copy(k).wait_send())


def front_kernel(
    group_ref, slot_ref, hidden_ref, kvw_ref, cond_ref, kv_ref,
    part, inbox, everyone, whole, sum_sems, img_sems, row_sems,
):
    img, row = place()
    greet(img, row, False)
    token = lax.broadcasted_iota(jnp.int32, (SLOTS, hidden_ref.shape[0]), 1)
    wanted = lax.broadcasted_iota(jnp.int32, (SLOTS, hidden_ref.shape[0]), 0) + slot_ref[0]
    pick = (token == wanted).astype(BF16)
    cond_ref[...] = jnp.dot(pick, hidden_ref[...], preferred_element_type=F32).astype(BF16)
    product = jnp.dot(cond_ref[...], kvw_ref[...], preferred_element_type=F32)
    part[0] = product[:, :CHANNELS]
    part[1] = product[:, CHANNELS:]
    row_sum = RowSum(img, row, part, inbox, sum_sems)
    row_sum.start()
    everyone[img] = row_sum.total().astype(BF16)
    gather = Gather(IMGS, img, lambda j: (j, row), lambda j: everyone.at[j], img_sems)
    gather.start()
    source = lax.fori_loop(
        0, IMGS, lambda i, s: jnp.maximum(s, jnp.where(group_ref[i] == img, i, 0)), jnp.int32(0)
    )
    gather.wait()
    whole[lax.rem(row, 2), rows16(lax.div(row, 2))] = everyone[source]
    share = Gather(
        ROWS, row, lambda j: (img, j),
        lambda j: whole.at[lax.rem(j, 2), rows16(lax.div(j, 2))], row_sems,
    )
    share.start()
    share.wait()
    kv_ref[...] = whole[...]
    row_sum.finish()
    gather.finish()
    share.finish()


def front(llm_hidden, slot_start, image_group, kv_weight):
    vmem, smem = pl.BlockSpec(memory_space=pltpu.VMEM), pl.BlockSpec(memory_space=pltpu.SMEM)
    return pl.pallas_call(
        front_kernel,
        out_shape=(
            jax.ShapeDtypeStruct((SLOTS, llm_hidden.shape[1]), BF16),
            jax.ShapeDtypeStruct((2, SLOTS, CHANNELS), BF16),
        ),
        in_specs=[smem, smem, vmem, vmem],
        out_specs=(vmem, vmem),
        scratch_shapes=[
            pltpu.VMEM((2, SLOTS, CHANNELS), F32),
            pltpu.VMEM((ROWS - 1, 16, CHANNELS), F32),
            pltpu.VMEM((IMGS, 16, CHANNELS), BF16),
            pltpu.VMEM((2, SLOTS, CHANNELS), BF16),
            pltpu.SemaphoreType.DMA((2, ROWS - 1)),
            pltpu.SemaphoreType.DMA((2, IMGS - 1)),
            pltpu.SemaphoreType.DMA((2, ROWS - 1)),
        ],
        compiler_params=pltpu.CompilerParams(
            collective_id=0, has_side_effects=True, vmem_limit_bytes=32 * 2**20
        ),
        name="front",
    )(image_group, slot_start, llm_hidden, kv_weight)


A_ROWS, B_ROWS = 64, 48


def total_of(count, base, piece):
    return lax.fori_loop(1, count, lambda k, acc: acc + piece(k).astype(F32), base.astype(F32))


def tail_kernel(
    group_ref, slot_ref, grads_ref, gkv_ref, cond_ref, kvw_ref,
    res_ref, query_ref, out_ref, hidden_ref, kvout_ref,
    s_inbox, s_all, s_image,
    in_core, half, in_a1, in_b1, sum_a, sum_b, in_a2, in_b2, sum_f, in_z, final,
    k_part, k_core, k_half, k_low, k_quarter, k_z, k_final,
    s_sum_sems, s_img_sems, s_row_sems,
    core_sems, a1_sems, b1_sems, a2_sems, b2_sems, z_sems,
    gz_sems, ga1_sems, gb1_sems, ga2_sems, gb2_sems, gcore_sems,
    kc_sems, kx_sems, kz_sems, kgz_sems, kgx_sems, kgc_sems,
    *, weight_scale, kv_scale,
):
    img, row = place()
    z, x, y, core = coords(img, row)
    partner = device(z, x, y, 1 - core)
    low = lax.rem(x, 2)
    across = device(z, x + 1 - 2 * low, y, core)
    greet(img, row, True)

    def at_x(k):
        return lax.rem(x + k, 4)

    def at_y(k):
        return lax.rem(y + k, 4)

    def at_z(k):
        return lax.rem(z + k, 8)

    row_sum = RowSum(img, row, gkv_ref, s_inbox, s_sum_sems)
    row_sum.start()

    def core_copy(k):
        return remote(
            grads_ref.at[1 - core, at_x(k)], in_core.at[at_x(k)], core_sems, k - 1, partner
        )

    each(5, lambda k: core_copy(k).start())

    s_all[img] = row_sum.total().astype(BF16)
    gather = Gather(IMGS, img, lambda j: (j, row), lambda j: s_all.at[j], s_img_sems)
    gather.start()

    def a1_copy(k):
        return remote(
            half.at[at_x(k), :, pl.ds(0, A_ROWS)], in_a1.at[k - 1], a1_sems, k - 1,
            device(z, at_x(k), y, core),
        )

    def b1_copy(k):
        return remote(
            half.at[:, at_y(k), pl.ds(A_ROWS, B_ROWS)], in_b1.at[k - 1], b1_sems, k - 1,
            device(z, x, at_y(k), core),
        )

    def add_core(k):
        core_copy(k).wait_recv()
        to = at_x(k)

        def add(j):
            half[to, j] = (
                grads_ref[core, to, j].astype(F32) + in_core[to, j].astype(F32)
            ).astype(BF16)

        each(4, add, 0)

    def add_and_send(k):
        add_core(k)
        a1_copy(k).start()

    each(4, add_and_send)
    add_core(4)
    each(4, lambda k: b1_copy(k).start())

    source = group_ref[img]
    gather.wait()
    s_image[lax.rem(row, 2), rows16(lax.div(row, 2))] = s_all[source]
    share = Gather(
        ROWS, row, lambda j: (img, j),
        lambda j: s_image.at[lax.rem(j, 2), rows16(lax.div(j, 2))], s_row_sems,
    )
    share.start()

    def a2_copy(k):
        return remote(
            sum_a.at[at_y(k)], in_a2.at[k - 1], a2_sems, k - 1, device(z, x, at_y(k), core)
        )

    def b2_copy(k):
        return remote(
            sum_b.at[at_x(k)], in_b2.at[k - 1], b2_sems, k - 1, device(z, at_x(k), y, core)
        )

    each(4, lambda k: a1_copy(k).wait_recv())

    def add_a(j):
        base = half[x, j, pl.ds(0, A_ROWS)]
        sum_a[j] = total_of(4, base, lambda k: in_a1[k - 1, j]).astype(BF16)

    each(4, add_a, 0)
    each(4, lambda k: a2_copy(k).start())

    share.wait()
    feature_count = cond_ref.shape[1]
    part = jnp.concatenate(
        [
            lax.dot_general(
                cond_ref[...], s_image[side], (((0,), (0,)), ((), ())), preferred_element_type=F32
            )
            for side in range(2)
        ],
        axis=1,
    ).astype(BF16)
    k_part[pl.ds(0, feature_count)] = part
    k_part[pl.ds(feature_count, 64)] = jnp.zeros((64, 2 * CHANNELS), BF16)

    def kc_copy():
        return remote(k_part.at[rows16((1 - core) * 28, 448)], k_core, kc_sems, 0, partner)

    kc_copy().start()

    each(4, lambda k: b1_copy(k).wait_recv())

    def add_b(j):
        base = half[j, y, pl.ds(A_ROWS, B_ROWS)]
        sum_b[j] = total_of(4, base, lambda k: in_b1[k - 1, j]).astype(BF16)

    each(4, add_b, 0)
    each(4, lambda k: b2_copy(k).start())

    each(4, lambda k: a2_copy(k).wait_recv())
    sum_f[pl.ds(0, A_ROWS)] = total_of(4, sum_a[y], lambda k: in_a2[k - 1]).astype(BF16)
    each(4, lambda k: b2_copy(k).wait_recv())
    sum_f[pl.ds(A_ROWS, B_ROWS)] = total_of(4, sum_b[x], lambda k: in_b2[k - 1]).astype(BF16)

    def z_copy(k):
        to = at_z(k)
        return remote(
            sum_f.at[rows16(lax.rem(to, 7))], in_z.at[k - 1], z_sems, k - 1, device(to, x, y, core)
        )

    def to_owner(k, act):
        pl.when(at_z(k) < 7)(lambda: act(k))

    each(8, lambda k: to_owner(k, lambda j: z_copy(j).start()))

    kc_copy().wait_recv()
    each(
        14,
        lambda j: k_half.__setitem__(
            rows16(2 * j, 32),
            (
                k_part[rows16(core * 28 + 2 * j, 32)].astype(F32) + k_core[rows16(2 * j, 32)].astype(F32)
            ).astype(BF16),
        ),
        0,
    )

    def kx_copy():
        return remote(k_half.at[rows16((1 - low) * 14, 224)], k_low, kx_sems, 0, across)

    kx_copy().start()

    @pl.when(z < 7)
    def _():
        each(8, lambda k: z_copy(k).wait_recv())
        done = total_of(8, sum_f[rows16(z)], lambda k: in_z[k - 1]) * weight_scale
        final[core, x, y, rows16(z)] = done.astype(BF16)

    def gz_copy(k):
        mine = final.at[core, x, y, rows16(lax.rem(z, 7))]
        return remote(mine, mine, gz_sems, k - 1, device(at_z(k), x, y, core))

    @pl.when(z < 7)
    def _():
        each(8, lambda k: gz_copy(k).start())

    kx_copy().wait_recv()
    each(
        7,
        lambda j: k_quarter.__setitem__(
            rows16(2 * j, 32),
            (
                k_half[rows16(low * 14 + 2 * j, 32)].astype(F32) + k_low[rows16(2 * j, 32)].astype(F32)
            ).astype(BF16),
        ),
        0,
    )

    def kz_copy(k):
        to = at_z(k)
        return remote(
            k_quarter.at[rows16(2 * lax.rem(to, 7), 32)], k_z.at[k - 1], kz_sems, k - 1,
            device(to, x, y, core),
        )

    each(8, lambda k: to_owner(k, lambda j: kz_copy(j).start()))

    grad_condition = lax.dot_general(
        jnp.concatenate([s_image[0], s_image[1]], axis=1), kvw_ref[...],
        (((1,), (1,)), ((), ())), preferred_element_type=F32,
    ).astype(BF16)
    token = lax.broadcasted_iota(jnp.int32, (hidden_ref.shape[0], SLOTS), 0)
    wanted = lax.broadcasted_iota(jnp.int32, (hidden_ref.shape[0], SLOTS), 1) + slot_ref[0]
    put = (token == wanted).astype(BF16)
    hidden_ref[...] = jnp.dot(put, grad_condition, preferred_element_type=F32).astype(BF16)

    def from_owner(k, act):
        pl.when(lax.rem(z + 8 - k, 8) < 7)(lambda: act(k))

    each(8, lambda k: from_owner(k, lambda j: gz_copy(j).wait_recv()))

    def ga1_copy(k):
        mine = final.at[core, x, y, pl.ds(0, A_ROWS)]
        return remote(mine, mine, ga1_sems, k - 1, device(z, x, at_y(k), core))

    def gb1_copy(k):
        mine = final.at[core, x, y, pl.ds(A_ROWS, B_ROWS)]
        return remote(mine, mine, gb1_sems, k - 1, device(z, at_x(k), y, core))

    each(4, lambda k: ga1_copy(k).start())
    each(4, lambda k: gb1_copy(k).start())

    @pl.when(z < 7)
    def _():
        each(8, lambda k: kz_copy(k).wait_recv())
        done = total_of(8, k_quarter[rows16(2 * z, 32)], lambda k: k_z[k - 1]) * kv_scale
        k_final[core, low, z] = done.astype(BF16)

    def kgz_copy(k):
        mine = k_final.at[core, low, lax.rem(z, 7)]
        return remote(mine, mine, kgz_sems, k - 1, device(at_z(k), x, y, core))

    @pl.when(z < 7)
    def _():
        each(8, lambda k: kgz_copy(k).start())

    def ga2_copy(k):
        mine = final.at[core, x, :, pl.ds(0, A_ROWS)]
        return remote(mine, mine, ga2_sems, k - 1, device(z, at_x(k), y, core))

    def gb2_copy(k):
        mine = final.at[core, :, y, pl.ds(A_ROWS, B_ROWS)]
        return remote(mine, mine, gb2_sems, k - 1, device(z, x, at_y(k), core))

    def core_a(k):
        mine = final.at[core, lax.rem(x + 4 - k, 4), :, pl.ds(0, A_ROWS)]
        return remote(mine, mine, gcore_sems, k, partner)

    def core_b(k):
        mine = final.at[core, :, lax.rem(y + 4 - k, 4), pl.ds(A_ROWS, B_ROWS)]
        return remote(mine, mine, gcore_sems, 4 + k, partner)

    each(4, lambda k: ga1_copy(k).wait_recv())
    each(4, lambda k: ga2_copy(k).start())
    core_a(0).start()
    each(4, lambda k: gb1_copy(k).wait_recv())
    each(4, lambda k: gb2_copy(k).start())
    core_b(0).start()

    each(8, lambda k: from_owner(k, lambda j: kgz_copy(j).wait_recv()))

    def kgx_copy():
        mine = k_final.at[core, low]
        return remote(mine, mine, kgx_sems, 0, across)

    def kgc_copy(k):
        mine = k_final.at[core, lax.rem(low + k, 2)]
        return remote(mine, mine, kgc_sems, k, partner)

    kgx_copy().start()
    kgc_copy(0).start()

    def pass_on_a(k):
        ga2_copy(k).wait_recv()
        core_a(k).start()

    def pass_on_b(k):
        gb2_copy(k).wait_recv()
        core_b(k).start()

    each(4, pass_on_a)
    each(4, pass_on_b)
    kgx_copy().wait_recv()
    kgc_copy(1).start()

    each(4, lambda k: core_a(k).wait_recv(), 0)
    each(4, lambda k: core_b(k).wait_recv(), 0)

    def write(target, begin, count):
        for start in range(begin, begin + count, 16):
            block, inside = divmod(start, 112)
            c, rest = divmod(block, 16)
            target[pl.ds(start - begin, 16)] = final[c, rest // 4, rest % 4, pl.ds(inside, 16)]

    write(res_ref, 0, 2880)
    write(query_ref, 2880, 320)
    write(out_ref, 3200, 320)
    each(2, lambda k: kgc_copy(k).wait_recv(), 0)
    for block in range(26):
        c, rest = divmod(block, 14)
        kvout_ref[pl.ds(32 * block, 32)] = k_final[c, rest // 7, rest % 7]

    row_sum.finish()
    gather.finish()
    share.finish()
    each(5, lambda k: core_copy(k).wait_send())
    for copy in (a1_copy, b1_copy, a2_copy, b2_copy, ga1_copy, gb1_copy, ga2_copy, gb2_copy):
        each(4, lambda k, copy=copy: copy(k).wait_send())
    each(8, lambda k: to_owner(k, lambda j: z_copy(j).wait_send()))
    each(8, lambda k: to_owner(k, lambda j: kz_copy(j).wait_send()))

    @pl.when(z < 7)
    def _():
        each(8, lambda k: gz_copy(k).wait_send())
        each(8, lambda k: kgz_copy(k).wait_send())

    each(4, lambda k: core_a(k).wait_send(), 0)
    each(4, lambda k: core_b(k).wait_send(), 0)
    kc_copy().wait_send()
    kx_copy().wait_send()
    kgx_copy().wait_send()
    each(2, lambda k: kgc_copy(k).wait_send(), 0)


def tail(image_group, slot_start, grads, grad_kv, condition, kv_weight, weight_scale, kv_scale):
    vmem, smem = pl.BlockSpec(memory_space=pltpu.VMEM), pl.BlockSpec(memory_space=pltpu.SMEM)
    width = CHANNELS
    dma = lambda n: pltpu.SemaphoreType.DMA((2, n))
    tokens = 512
    return pl.pallas_call(
        functools.partial(tail_kernel, weight_scale=weight_scale, kv_scale=kv_scale),
        out_shape=(
            jax.ShapeDtypeStruct((9 * width, width), BF16),
            jax.ShapeDtypeStruct((width, width), BF16),
            jax.ShapeDtypeStruct((width, width), BF16),
            jax.ShapeDtypeStruct((tokens, condition.shape[1]), BF16),
            jax.ShapeDtypeStruct(kv_weight.shape, BF16),
        ),
        in_specs=[smem, smem, vmem, vmem, vmem, vmem],
        out_specs=(vmem,) * 5,
        scratch_shapes=[
            pltpu.VMEM((ROWS - 1, 16, width), BF16),
            pltpu.VMEM((IMGS, 16, width), BF16),
            pltpu.VMEM((2, SLOTS, width), BF16),
            pltpu.VMEM((4, 4, 112, width), BF16),
            pltpu.VMEM((4, 4, 112, width), BF16),
            pltpu.VMEM((3, 4, A_ROWS, width), BF16),
            pltpu.VMEM((3, 4, B_ROWS, width), BF16),
            pltpu.VMEM((4, A_ROWS, width), BF16),
            pltpu.VMEM((4, B_ROWS, width), BF16),
            pltpu.VMEM((3, A_ROWS, width), BF16),
            pltpu.VMEM((3, B_ROWS, width), BF16),
            pltpu.VMEM((112, width), BF16),
            pltpu.VMEM((7, 16, width), BF16),
            pltpu.VMEM((2, 4, 4, 112, width), BF16),
            pltpu.VMEM((896, 2 * width), BF16),
            pltpu.VMEM((448, 2 * width), BF16),
            pltpu.VMEM((448, 2 * width), BF16),
            pltpu.VMEM((224, 2 * width), BF16),
            pltpu.VMEM((224, 2 * width), BF16),
            pltpu.VMEM((7, 32, 2 * width), BF16),
            pltpu.VMEM((2, 2, 7, 32, 2 * width), BF16),
            dma(7), dma(31), dma(7),
            dma(4), dma(3), dma(3), dma(3), dma(3), dma(7),
            dma(7), dma(3), dma(3), dma(3), dma(3), dma(8),
            dma(1), dma(1), dma(7), dma(7), dma(1), dma(2),
        ],
        compiler_params=pltpu.CompilerParams(
            collective_id=1, has_side_effects=True, vmem_limit_bytes=48 * 2**20
        ),
        name="tail",
    )(image_group, slot_start, grads, grad_kv, condition, kv_weight)


def shards(
    llm_hidden,
    slot_start,
    image_group,
    timesteps,
    latents,
    noise,
    kv_weight,
    in_weight,
    res_weight,
    query_weight,
    out_weight,
    cotangent,
):
    condition, kv = front(llm_hidden, slot_start, image_group, kv_weight)
    group_kv = jnp.concatenate([kv[0], kv[1]], axis=1)
    noisy = noisy_input(latents[0], noise[0], timesteps[0])
    block_out, grad_kv, res_grad, query_grad, out_grad = block_pass(
        noisy, timesteps[0], group_kv, cotangent[0], in_weight, res_weight, query_weight, out_weight
    )
    grads = jnp.concatenate(
        [
            res_grad.reshape(-1, CHANNELS).astype(BF16),
            query_grad.astype(BF16),
            out_grad.astype(BF16),
            jnp.zeros((64, CHANNELS), BF16),
        ]
    ).reshape(2, 4, 4, 112, CHANNELS)
    grad_kv = grad_kv.astype(BF16)
    grad_kv = jnp.stack([grad_kv[:, :CHANNELS], grad_kv[:, CHANNELS:]])
    cells = IMGS * ROWS * latents.shape[2] * latents.shape[3]
    res, query, out, grad_hidden, grad_kv_weight = tail(
        image_group, slot_start, grads, grad_kv, condition, kv_weight,
        cells ** (-0.5), (IMGS * SLOTS) ** (-0.5),
    )
    return (block_out[None], grad_hidden, grad_kv_weight, res.reshape(3, 3, CHANNELS, CHANNELS), query, out)


def solution(mesh):
    return jax.shard_map(
        shards,
        mesh=mesh,
        in_specs=(
            P("img", "row"),
            P("img"),
            P(),
            P("img"),
            P("img", None, "row", None),
            P("img", None, "row", None),
            P("row", None),
            P(),
            P(),
            P(),
            P(),
            P("img", None, "row", None),
        ),
        out_specs=(P("img", None, "row", None), P("img", "row"), P("row", None), P(), P(), P()),
        check_vma=False,
    )
```

```python
import functools
import math

import jax
import jax.numpy as jnp
from jax import lax
from jax.experimental import pallas as pl
from jax.experimental.pallas import tpu as pltpu
from jax.sharding import PartitionSpec as P

HEAD_DIM = 64
SLOTS = 64
MESH = pl.DeviceIdType.MESH
CHANNELS = 320
HEADS = 5
IMGS, ROWS = 32, 8
TAPS = 11
F32, BF16 = jnp.float32, jnp.bfloat16


def place():
    img, row = lax.axis_index("img"), lax.axis_index("row")
    return img, row


def coords(img, row):
    z, low, core = lax.div(img, 4), lax.rem(lax.div(img, 2), 2), lax.rem(img, 2)
    return z, lax.div(row, 4) * 2 + low, lax.rem(row, 4), core


def device(z, x, y, core):
    return (z * 4 + lax.rem(x, 2) * 2 + core, lax.div(x, 2) * 4 + y)


def remote(src, dst, sems, slot, where):
    return pltpu.make_async_remote_copy(
        src_ref=src,
        dst_ref=dst,
        send_sem=sems.at[0, slot],
        recv_sem=sems.at[1, slot],
        device_id=where,
        device_id_type=MESH,
    )


def each(count, act, first=1):
    def body(k, carry):
        act(k)
        return carry

    lax.fori_loop(first, count, body, 0)


def rows16(index, count=16):
    return pl.ds(pl.multiple_of(index * 16, 16), count)


def greet(img, row):
    barrier = pltpu.get_barrier_semaphore()

    def call(where):
        pl.semaphore_signal(barrier, inc=1, device_id=where, device_id_type=MESH)

    each(ROWS, lambda k: call((img, lax.rem(row + k, ROWS))))
    each(IMGS, lambda k: call((lax.rem(img + k, IMGS), row)))
    z, x, y, core = coords(img, row)
    other = 2 * (1 - lax.div(x, 2)) + (1 - lax.rem(x, 2))
    call(device(z, other, y, core))
    return ROWS - 1 + IMGS - 1 + 1


class RowSum:
    def __init__(self, img, row, part, inbox, sems):
        self.img, self.row, self.part, self.inbox, self.sems = img, row, part, inbox, sems

    def copy(self, k):
        r = lax.rem(self.row + k, ROWS)
        src = self.part.at[lax.rem(r, 2), rows16(lax.div(r, 2))]
        return remote(src, self.inbox.at[k - 1], self.sems, k - 1, (self.img, r))

    def start(self):
        each(ROWS, lambda k: self.copy(k).start())

    def total(self):
        own = self.part[lax.rem(self.row, 2), rows16(lax.div(self.row, 2))].astype(F32)

        def body(k, acc):
            self.copy(k).wait_recv()
            return acc + self.inbox[k - 1].astype(F32)

        return lax.fori_loop(1, ROWS, body, own)

    def finish(self):
        each(ROWS, lambda k: self.copy(k).wait_send())


class Gather:
    def __init__(self, count, me, where, target, sems):
        self.count, self.me, self.where, self.target, self.sems = count, me, where, target, sems

    def copy(self, k):
        to = lax.rem(self.me + k, self.count)
        return remote(
            self.target(self.me), self.target(self.me), self.sems, k - 1, self.where(to)
        )

    def start(self):
        each(self.count, lambda k: self.copy(k).start())

    def wait(self):
        each(self.count, lambda k: self.copy(k).wait_recv())

    def finish(self):
        each(self.count, lambda k: self.copy(k).wait_send())


def total_of(count, base, piece):
    return lax.fori_loop(1, count, lambda k, acc: acc + piece(k).astype(F32), base.astype(F32))


def matmul(left, right):
    return jnp.dot(left, right, preferred_element_type=F32)


def against(left, right):
    return lax.dot_general(left, right, (((1,), (1,)), ((), ())), preferred_element_type=F32)


def shifted(field, step):
    lane = lax.broadcasted_iota(jnp.int32, (field.shape[0], 128), 1)
    edge = 127 if step > 0 else 0
    parts = []
    for start in range(0, field.shape[1], 128):
        turned = pltpu.roll(field[:, start : start + 128], (-step) % 128, 1)
        parts.append(jnp.where(lane == edge, 0.0, turned))
    return parts[0] if len(parts) == 1 else jnp.concatenate(parts, axis=1)


def spread(rows, target, flip):
    lane = lax.div(lax.broadcasted_iota(jnp.int32, rows.shape, 1), HEAD_DIM)
    wide = rows.astype(F32)
    full = jnp.concatenate([jnp.where(lane == h, wide, 0.0) for h in range(HEADS)], axis=0)
    target[...] = full.astype(BF16)
    flip[...] = full.T.astype(BF16)


def diagonal(full):
    lane = lax.div(lax.broadcasted_iota(jnp.int32, (SLOTS, CHANNELS), 1), HEAD_DIM)
    total = jnp.zeros((SLOTS, CHANNELS), F32)
    for h in range(HEADS):
        total = jnp.where(lane == h, full[h * SLOTS : (h + 1) * SLOTS], total)
    return total


def kernel(
    group_ref, slot_ref, time_ref,
    hidden_ref, kvw_ref, latent_ref, noise_ref, emb_ref, inw_ref, resw_ref, qw_ref, ow_ref, up_ref,
    block_ref, res_ref, query_ref, out_ref, ghidden_ref, kvout_ref,
    noisy, band, cond, part, f_inbox, f_all, f_kv, wcat, qw_t, ow_t, taps, first,
    hid, query, att, prob, gatt, gscore, gquery, ghid, bk, bk_t, bv, bv_t,
    gkv, s_inbox, s_all, s_image,
    grads, in_core, half, in_a1, in_b1, sum_a, sum_b, in_a2, in_b2, sum_f, in_z, final,
    k_part, k_core, k_half, k_low, k_quarter, k_z, k_final,
    halo_sems, f_sum_sems, f_img_sems, f_row_sems,
    s_sum_sems, s_img_sems, s_row_sems,
    core_sems, a1_sems, b1_sems, a2_sems, b2_sems, z_sems,
    gz_sems, ga1_sems, gb1_sems, ga2_sems, gb2_sems, gcore_sems,
    kc_sems, kx_sems, kz_sems, kgz_sems, kgx_sems, kgc_sems,
    *, weight_scale, kv_scale,
):
    img, row = place()
    z, x, y, core = coords(img, row)
    partner = device(z, x, y, 1 - core)
    low = lax.rem(x, 2)
    across = device(z, x + 1 - 2 * low, y, core)

    band[...] = jnp.zeros_like(band)
    signals = greet(img, row)

    def at_x(k):
        return lax.rem(x + k, 4)

    def at_y(k):
        return lax.rem(y + k, 4)

    def at_z(k):
        return lax.rem(z + k, 8)

    index = lax.broadcasted_iota(jnp.int32, (8, 128), 0) * 128 + lax.broadcasted_iota(
        jnp.int32, (8, 128), 1
    )
    share_of = index.astype(F32) / 999.0
    beta = (0.00085**0.5 * (1.0 - share_of) + 0.012**0.5 * share_of) ** 2
    logs = jnp.where(index <= time_ref[0], jnp.log(1.0 - jnp.where(index < 1000, beta, 0.0)), 0.0)
    level = jnp.exp(jnp.sum(logs, axis=(0, 1), keepdims=True))
    keep, add = jnp.sqrt(level), jnp.sqrt(1.0 - level)
    for c in range(4):
        noisy[c] = (keep * latent_ref[c] + add * noise_ref[c]).astype(BF16).astype(F32)
    for r in range(8):
        band[2 + r, pl.ds(0, 4)] = noisy[:, r, :]

    token = lax.broadcasted_iota(jnp.int32, (SLOTS, hidden_ref.shape[0]), 1)
    wanted = lax.broadcasted_iota(jnp.int32, (SLOTS, hidden_ref.shape[0]), 0) + slot_ref[0]
    cond[...] = matmul((token == wanted).astype(BF16), hidden_ref[...]).astype(BF16)
    product = matmul(cond[...], kvw_ref[...])
    part[0] = product[:, :CHANNELS]
    part[1] = product[:, CHANNELS:]

    pl.semaphore_wait(pltpu.get_barrier_semaphore(), signals)

    def halo_up():
        return remote(band.at[pl.ds(8, 2)], band.at[pl.ds(0, 2)], halo_sems, 0, (img, lax.rem(row + 1, ROWS)))

    def halo_down():
        return remote(band.at[pl.ds(2, 2)], band.at[pl.ds(10, 2)], halo_sems, 1, (img, lax.rem(row + ROWS - 1, ROWS)))

    above, below = row > 0, row < ROWS - 1
    pl.when(below)(lambda: halo_up().start())
    pl.when(above)(lambda: halo_down().start())
    f_sum = RowSum(img, row, part, f_inbox, f_sum_sems)
    f_sum.start()

    for a in range(3):
        for b in range(3):
            wcat[a, :, b * CHANNELS : (b + 1) * CHANNELS] = resw_ref[3 * a + b]
    qw_t[...] = qw_ref[...].astype(F32).T.astype(BF16)
    ow_t[...] = ow_ref[...].astype(F32).T.astype(BF16)

    pl.when(above)(lambda: halo_up().wait_recv())
    pl.when(below)(lambda: halo_down().wait_recv())

    def first_rows(j):
        fields = []
        for r in range(2):
            pieces = []
            for a in range(3):
                n = band[2 * j + r + a]
                pieces += [shifted(n, -1), n, shifted(n, 1)]
            fields.append(jnp.concatenate(pieces, axis=0))
        field = jnp.concatenate(fields, axis=1).astype(BF16)
        value = matmul(inw_ref[...], field)
        lanes = pl.ds(pl.multiple_of(j * 256, 256), 256)
        first[:, lanes] = value
        v = value + emb_ref[...]
        line = row * 8 - 1 + 2 * j + lax.div(lax.broadcasted_iota(jnp.int32, v.shape, 1), 128)
        act = jnp.where((line >= 0) & (line < 64), v / (1.0 + jnp.exp(-v)), 0.0)
        act = act.astype(BF16).astype(F32)
        taps[pl.ds(0, CHANNELS), lanes] = shifted(act, -1).astype(BF16)
        taps[pl.ds(CHANNELS, CHANNELS), lanes] = act.astype(BF16)
        taps[pl.ds(2 * CHANNELS, CHANNELS), lanes] = shifted(act, 1).astype(BF16)

    each(5, first_rows, 0)

    f_all[img] = f_sum.total().astype(BF16)
    f_gather = Gather(IMGS, img, lambda j: (j, row), lambda j: f_all.at[j], f_img_sems)
    f_gather.start()

    def cells(n, more=0):
        return pl.ds(pl.multiple_of(n * 256 + more, 128), 256)

    def residual(n):
        acc = first[:, cells(n, 128)]
        for a in range(3):
            acc = acc + matmul(wcat[a], taps[:, cells(n, 128 * a)])
        hid[:, cells(n)] = acc.astype(BF16)

    each(4, residual, 0)

    source = lax.fori_loop(
        0, IMGS, lambda i, s: jnp.maximum(s, jnp.where(group_ref[i] == img, i, 0)), jnp.int32(0)
    )
    f_gather.wait()
    f_kv[lax.rem(row, 2), rows16(lax.div(row, 2))] = f_all[source]
    f_share = Gather(
        ROWS, row, lambda j: (img, j),
        lambda j: f_kv.at[lax.rem(j, 2), rows16(lax.div(j, 2))], f_row_sems,
    )
    f_share.start()

    def projections(n):
        query[:, cells(n)] = matmul(qw_ref[...], hid[:, cells(n)]).astype(BF16)
        gatt[:, cells(n)] = matmul(ow_t[...], up_ref[:, cells(n)]).astype(BF16)

    each(4, projections, 0)
    f_share.wait()
    spread(f_kv[0], bk, bk_t)
    spread(f_kv[1], bv, bv_t)

    def attend(n):
        here = cells(n)
        score = matmul(bk[...], query[:, here]) * HEAD_DIM**-0.5
        score = score.reshape(HEADS, SLOTS, 256)
        top = jnp.max(score, axis=1, keepdims=True)
        grown = jnp.exp(score - top)
        soft = grown / jnp.sum(grown, axis=1, keepdims=True)
        soft_low = soft.reshape(CHANNELS, 256).astype(BF16)
        prob[:, here] = soft_low
        attended = matmul(bv_t[...], soft_low).astype(BF16)
        att[:, here] = attended
        block_ref[:, here] = (
            hid[:, here].astype(F32) + matmul(ow_ref[...], attended)
        ).astype(BF16)
        gprob = matmul(bv[...], gatt[:, here]).reshape(HEADS, SLOTS, 256)
        mean = jnp.sum(soft * gprob, axis=1, keepdims=True)
        gs = (HEAD_DIM**-0.5 * soft * (gprob - mean)).reshape(CHANNELS, 256).astype(BF16)
        gscore[:, here] = gs
        gq = matmul(bk_t[...], gs).astype(BF16)
        gquery[:, here] = gq
        ghid[:, here] = (up_ref[:, here].astype(F32) + matmul(qw_t[...], gq)).astype(BF16)

    each(4, attend, 0)

    gkv[0] = diagonal(against(gscore[...], query[...])).astype(BF16)
    gkv[1] = diagonal(against(prob[...], gatt[...])).astype(BF16)
    row_sum = RowSum(img, row, gkv, s_inbox, s_sum_sems)
    row_sum.start()

    def core_copy(t):
        return remote(
            grads.at[t, rows16((1 - core) * 10, 160)], in_core.at[t], core_sems, t, partner
        )

    grads[0] = against(gquery[...], hid[...]).astype(BF16)
    core_copy(0).start()
    grads[1] = against(up_ref[...], att[...]).astype(BF16)
    core_copy(1).start()

    def tap(t):
        a, b = lax.div(t - 2, 3), lax.rem(t - 2, 3)
        field = taps[
            pl.ds(pl.multiple_of(b * CHANNELS, CHANNELS), CHANNELS),
            pl.ds(pl.multiple_of(a * 128, 128), 1024),
        ]
        grads[t] = against(ghid[...], field).astype(BF16)
        core_copy(t).start()

    def a1_copy(k):
        return remote(
            half.at[at_x(k), :, pl.ds(0, 4)], in_a1.at[k - 1], a1_sems, k - 1,
            device(z, at_x(k), y, core),
        )

    def b1_copy(k):
        return remote(
            half.at[:, at_y(k), pl.ds(4, 3)], in_b1.at[k - 1], b1_sems, k - 1,
            device(z, x, at_y(k), core),
        )

    def add_block(to, begin, end):
        each(end, lambda t: core_copy(t).wait_recv(), begin)

        def add(u):
            unit = to * 28 + u
            t, j = lax.div(unit, 10), lax.rem(unit, 10)
            half[to, lax.div(u, 7), lax.rem(u, 7)] = (
                grads[t, rows16(core * 10 + j)].astype(F32) + in_core[t, rows16(j)].astype(F32)
            ).astype(BF16)

        each(26 if to == 3 else 28, add, 0)

        @pl.when(x != to)
        def _():
            a1_copy(lax.rem(to + 4 - x, 4)).start()

    half[3, 3, pl.ds(5, 2)] = jnp.zeros((2, 16, CHANNELS), BF16)
    each(5, tap, 2)
    add_block(0, 0, 3)
    s_all[img] = row_sum.total().astype(BF16)
    gather = Gather(IMGS, img, lambda j: (j, row), lambda j: s_all.at[j], s_img_sems)
    gather.start()
    each(8, tap, 5)
    add_block(1, 3, 6)
    each(11, tap, 8)
    add_block(2, 6, 9)
    add_block(3, 9, 11)
    each(4, lambda k: b1_copy(k).start())

    gather.wait()
    s_image[lax.rem(row, 2), rows16(lax.div(row, 2))] = s_all[group_ref[img]]
    share = Gather(
        ROWS, row, lambda j: (img, j),
        lambda j: s_image.at[lax.rem(j, 2), rows16(lax.div(j, 2))], s_row_sems,
    )
    share.start()

    def a2_copy(k):
        return remote(
            sum_a.at[at_y(k)], in_a2.at[k - 1], a2_sems, k - 1, device(z, x, at_y(k), core)
        )

    def b2_copy(k):
        return remote(
            sum_b.at[at_x(k)], in_b2.at[k - 1], b2_sems, k - 1, device(z, at_x(k), y, core)
        )

    each(4, lambda k: a1_copy(k).wait_recv())

    def add_a(j):
        sum_a[j] = total_of(4, half[x, j, pl.ds(0, 4)], lambda k: in_a1[k - 1, j]).astype(BF16)

    each(4, add_a, 0)
    each(4, lambda k: a2_copy(k).start())

    share.wait()
    features = cond.shape[1]
    for side in range(2):
        k_part[pl.ds(0, features), side * CHANNELS : (side + 1) * CHANNELS] = lax.dot_general(
            cond[...], s_image[side], (((0,), (0,)), ((), ())), preferred_element_type=F32
        ).astype(BF16)
    k_part[pl.ds(features, 64)] = jnp.zeros((64, 2 * CHANNELS), BF16)

    def kc_copy():
        return remote(k_part.at[rows16((1 - core) * 28, 448)], k_core, kc_sems, 0, partner)

    kc_copy().start()

    each(4, lambda k: b1_copy(k).wait_recv())

    def add_b(j):
        sum_b[j] = total_of(4, half[j, y, pl.ds(4, 3)], lambda k: in_b1[k - 1, j]).astype(BF16)

    each(4, add_b, 0)
    each(4, lambda k: b2_copy(k).start())

    each(4, lambda k: a2_copy(k).wait_recv())
    sum_f[pl.ds(0, 4)] = total_of(4, sum_a[y], lambda k: in_a2[k - 1]).astype(BF16)
    each(4, lambda k: b2_copy(k).wait_recv())
    sum_f[pl.ds(4, 3)] = total_of(4, sum_b[x], lambda k: in_b2[k - 1]).astype(BF16)

    def z_copy(k):
        to = at_z(k)
        return remote(
            sum_f.at[lax.rem(to, 7)], in_z.at[k - 1], z_sems, k - 1, device(to, x, y, core)
        )

    def to_owner(k, act):
        pl.when(at_z(k) < 7)(lambda: act(k))

    def from_owner(k, act):
        pl.when(lax.rem(z + 8 - k, 8) < 7)(lambda: act(k))

    each(8, lambda k: to_owner(k, lambda j: z_copy(j).start()))

    kc_copy().wait_recv()

    def add_kc(j):
        k_half[rows16(2 * j, 32)] = (
            k_part[rows16(core * 28 + 2 * j, 32)].astype(F32) + k_core[rows16(2 * j, 32)].astype(F32)
        ).astype(BF16)

    each(14, add_kc, 0)

    def kx_copy():
        return remote(k_half.at[rows16((1 - low) * 14, 224)], k_low, kx_sems, 0, across)

    kx_copy().start()

    @pl.when(z < 7)
    def _():
        each(8, lambda k: z_copy(k).wait_recv())
        done = total_of(8, sum_f[lax.rem(z, 7)], lambda k: in_z[k - 1]) * weight_scale
        final[core, x, y, lax.rem(z, 7)] = done.astype(BF16)

    def gz_copy(k):
        mine = final.at[core, x, y, lax.rem(z, 7)]
        return remote(mine, mine, gz_sems, k - 1, device(at_z(k), x, y, core))

    @pl.when(z < 7)
    def _():
        each(8, lambda k: gz_copy(k).start())

    kx_copy().wait_recv()

    def add_kx(j):
        k_quarter[rows16(2 * j, 32)] = (
            k_half[rows16(low * 14 + 2 * j, 32)].astype(F32) + k_low[rows16(2 * j, 32)].astype(F32)
        ).astype(BF16)

    each(7, add_kx, 0)

    def kz_copy(k):
        to = at_z(k)
        return remote(
            k_quarter.at[rows16(2 * lax.rem(to, 7), 32)], k_z.at[k - 1], kz_sems, k - 1,
            device(to, x, y, core),
        )

    each(8, lambda k: to_owner(k, lambda j: kz_copy(j).start()))

    gcond = against(jnp.concatenate([s_image[0], s_image[1]], axis=1), kvw_ref[...]).astype(BF16)
    spot = lax.broadcasted_iota(jnp.int32, (hidden_ref.shape[0], SLOTS), 0)
    slot = lax.broadcasted_iota(jnp.int32, (hidden_ref.shape[0], SLOTS), 1) + slot_ref[0]
    ghidden_ref[...] = matmul((spot == slot).astype(BF16), gcond).astype(BF16)

    each(8, lambda k: from_owner(k, lambda j: gz_copy(j).wait_recv()))

    def ga1_copy(k):
        mine = final.at[core, x, y, pl.ds(0, 4)]
        return remote(mine, mine, ga1_sems, k - 1, device(z, x, at_y(k), core))

    def gb1_copy(k):
        mine = final.at[core, x, y, pl.ds(4, 3)]
        return remote(mine, mine, gb1_sems, k - 1, device(z, at_x(k), y, core))

    each(4, lambda k: ga1_copy(k).start())
    each(4, lambda k: gb1_copy(k).start())

    @pl.when(z < 7)
    def _():
        each(8, lambda k: kz_copy(k).wait_recv())
        own = k_quarter[rows16(2 * lax.rem(z, 7), 32)]
        k_final[core, low, lax.rem(z, 7)] = (
            total_of(8, own, lambda k: k_z[k - 1]) * kv_scale
        ).astype(BF16)

    def kgz_copy(k):
        mine = k_final.at[core, low, lax.rem(z, 7)]
        return remote(mine, mine, kgz_sems, k - 1, device(at_z(k), x, y, core))

    @pl.when(z < 7)
    def _():
        each(8, lambda k: kgz_copy(k).start())

    def ga2_copy(k):
        mine = final.at[core, x, :, pl.ds(0, 4)]
        return remote(mine, mine, ga2_sems, k - 1, device(z, at_x(k), y, core))

    def gb2_copy(k):
        mine = final.at[core, :, y, pl.ds(4, 3)]
        return remote(mine, mine, gb2_sems, k - 1, device(z, x, at_y(k), core))

    def core_a(k):
        mine = final.at[core, lax.rem(x + 4 - k, 4), :, pl.ds(0, 4)]
        return remote(mine, mine, gcore_sems, k, partner)

    def core_b(k):
        mine = final.at[core, :, lax.rem(y + 4 - k, 4), pl.ds(4, 3)]
        return remote(mine, mine, gcore_sems, 4 + k, partner)

    each(4, lambda k: ga1_copy(k).wait_recv())
    each(4, lambda k: ga2_copy(k).start())
    core_a(0).start()
    each(4, lambda k: gb1_copy(k).wait_recv())
    each(4, lambda k: gb2_copy(k).start())
    core_b(0).start()

    each(8, lambda k: from_owner(k, lambda j: kgz_copy(j).wait_recv()))

    def kgx_copy():
        mine = k_final.at[core, low]
        return remote(mine, mine, kgx_sems, 0, across)

    def kgc_copy(k):
        mine = k_final.at[core, lax.rem(low + k, 2)]
        return remote(mine, mine, kgc_sems, k, partner)

    kgx_copy().start()
    kgc_copy(0).start()

    def pass_on_a(k):
        ga2_copy(k).wait_recv()
        core_a(k).start()

    def pass_on_b(k):
        gb2_copy(k).wait_recv()
        core_b(k).start()

    each(4, pass_on_a)
    each(4, pass_on_b)
    kgx_copy().wait_recv()
    kgc_copy(1).start()

    each(4, lambda k: core_a(k).wait_recv(), 0)
    each(4, lambda k: core_b(k).wait_recv(), 0)

    for t in range(TAPS):
        target, base = ((query_ref, 0), (out_ref, 0))[t] if t < 2 else (res_ref, (t - 2) * CHANNELS)
        for c in range(2):
            for j in range(10):
                block, inside = divmod(t * 10 + j, 7)
                target[pl.ds(base + c * 160 + j * 16, 16)] = final[c, block // 4, block % 4, inside]
    each(2, lambda k: kgc_copy(k).wait_recv(), 0)
    for block in range(26):
        c, rest = divmod(block, 14)
        kvout_ref[pl.ds(32 * block, 32)] = k_final[c, rest // 7, rest % 7]

    pl.when(below)(lambda: halo_up().wait_send())
    pl.when(above)(lambda: halo_down().wait_send())
    for one in (f_sum, f_gather, f_share, row_sum, gather, share):
        one.finish()
    each(TAPS, lambda t: core_copy(t).wait_send(), 0)
    for copy in (a1_copy, b1_copy, a2_copy, b2_copy, ga1_copy, gb1_copy, ga2_copy, gb2_copy):
        each(4, lambda k, copy=copy: copy(k).wait_send())
    each(8, lambda k: to_owner(k, lambda j: z_copy(j).wait_send()))
    each(8, lambda k: to_owner(k, lambda j: kz_copy(j).wait_send()))

    @pl.when(z < 7)
    def _():
        each(8, lambda k: gz_copy(k).wait_send())
        each(8, lambda k: kgz_copy(k).wait_send())

    each(4, lambda k: core_a(k).wait_send(), 0)
    each(4, lambda k: core_b(k).wait_send(), 0)
    kc_copy().wait_send()
    kx_copy().wait_send()
    kgx_copy().wait_send()
    each(2, lambda k: kgc_copy(k).wait_send(), 0)


def shards(
    llm_hidden,
    slot_start,
    image_group,
    timesteps,
    latents,
    noise,
    kv_weight,
    in_weight,
    res_weight,
    query_weight,
    out_weight,
    cotangent,
):
    width, features = CHANNELS, llm_hidden.shape[1]
    frequency = jnp.exp(-math.log(10000.0) * jnp.arange(width // 2, dtype=F32) / (width // 2))
    angles = timesteps[0].astype(F32) * frequency
    emb = jnp.concatenate([jnp.cos(angles), jnp.sin(angles)])[:, None]
    in_matrix = jnp.pad(in_weight.transpose(2, 0, 1, 3), ((0, 0), (0, 0), (0, 0), (0, 4)))
    vmem, smem = pl.BlockSpec(memory_space=pltpu.VMEM), pl.BlockSpec(memory_space=pltpu.SMEM)
    dma = lambda n: pltpu.SemaphoreType.DMA((2, n))
    low = lambda *shape: pltpu.VMEM(shape, BF16)
    field, square = low(width, 1024), low(width, width)
    out = lambda *shape: jax.ShapeDtypeStruct(shape, BF16)
    block, res, query, projection, grad_hidden, grad_kv_weight = pl.pallas_call(
        functools.partial(
            kernel,
            weight_scale=(IMGS * ROWS * 1024) ** (-0.5),
            kv_scale=(IMGS * SLOTS) ** (-0.5),
        ),
        out_shape=(
            out(width, 1024), out(9 * width, width), out(width, width), out(width, width),
            out(*llm_hidden.shape), out(*kv_weight.shape),
        ),
        in_specs=[smem] * 3 + [vmem] * 10,
        out_specs=(vmem,) * 6,
        scratch_shapes=[
            pltpu.VMEM((4, 8, 128), F32), pltpu.VMEM((12, 8, 128), F32),
            low(SLOTS, features), pltpu.VMEM((2, SLOTS, width), F32),
            pltpu.VMEM((ROWS - 1, 16, width), F32), low(IMGS, 16, width), low(2, SLOTS, width),
            low(3, width, 3 * width), square, square,
            low(3 * width, 1280), pltpu.VMEM((width, 1280), F32),
            field, field, field, field, field, field, field, field, square, square, square, square,
            low(2, SLOTS, width), low(ROWS - 1, 16, width), low(IMGS, 16, width), low(2, SLOTS, width),
            low(TAPS, width, width), low(TAPS, 160, width), low(4, 4, 7, 16, width),
            low(3, 4, 4, 16, width), low(3, 4, 3, 16, width),
            low(4, 4, 16, width), low(4, 3, 16, width), low(3, 4, 16, width), low(3, 3, 16, width),
            low(7, 16, width), low(7, 16, width), low(2, 4, 4, 7, 16, width),
            low(896, 2 * width), low(448, 2 * width), low(448, 2 * width), low(224, 2 * width),
            low(224, 2 * width), low(7, 32, 2 * width), low(2, 2, 7, 32, 2 * width),
            dma(2), dma(7), dma(31), dma(7), dma(7), dma(31), dma(7),
            dma(TAPS), dma(3), dma(3), dma(3), dma(3), dma(7),
            dma(7), dma(3), dma(3), dma(3), dma(3), dma(8),
            dma(1), dma(1), dma(7), dma(7), dma(1), dma(2),
        ],
        compiler_params=pltpu.CompilerParams(
            collective_id=0, has_side_effects=True, vmem_limit_bytes=60 * 2**20
        ),
        name="block",
    )(
        image_group, slot_start, timesteps, llm_hidden, kv_weight, latents[0], noise[0], emb,
        in_matrix.reshape(width, 72).astype(BF16), res_weight.reshape(9, width, width),
        query_weight, out_weight, cotangent.reshape(width, 1024),
    )
    return (
        block.reshape(1, width, 8, 128), grad_hidden, grad_kv_weight,
        res.reshape(3, 3, width, width), query, projection,
    )


def solution(mesh):
    return jax.shard_map(
        shards,
        mesh=mesh,
        in_specs=(
            P("img", "row"),
            P("img"),
            P(),
            P("img"),
            P("img", None, "row", None),
            P("img", None, "row", None),
            P("row", None),
            P(),
            P(),
            P(),
            P(),
            P("img", None, "row", None),
        ),
        out_specs=(P("img", None, "row", None), P("img", "row"), P("row", None), P(), P(), P()),
        check_vma=False,
    )
```

```python
import functools
import math

import jax
import jax.numpy as jnp
from jax import lax
from jax.experimental import pallas as pl
from jax.experimental.pallas import tpu as pltpu
from jax.sharding import PartitionSpec as P

HEAD_DIM = 64
SLOTS = 64
MESH = pl.DeviceIdType.MESH
CHANNELS = 320
HEADS = 5
IMGS, ROWS = 32, 8
TAPS = 11
SLICES = 7
F32, BF16 = jnp.float32, jnp.bfloat16


def place():
    img, row = lax.axis_index("img"), lax.axis_index("row")
    return img, row


def coords(img, row):
    z, low, core = lax.div(img, 4), lax.rem(lax.div(img, 2), 2), lax.rem(img, 2)
    return z, lax.div(row, 4) * 2 + low, lax.rem(row, 4), core


def device(z, x, y, core):
    return (z * 4 + lax.rem(x, 2) * 2 + core, lax.div(x, 2) * 4 + y)


def remote(src, dst, sems, slot, where):
    return pltpu.make_async_remote_copy(
        src_ref=src,
        dst_ref=dst,
        send_sem=sems.at[0, slot],
        recv_sem=sems.at[1, slot],
        device_id=where,
        device_id_type=MESH,
    )


def each(count, act, first=1):
    def body(k, carry):
        act(k)
        return carry

    lax.fori_loop(first, count, body, 0)


def rows16(index, count=16):
    return pl.ds(pl.multiple_of(index * 16, 16), count)


def greet(img, row):
    barrier = pltpu.get_barrier_semaphore()

    def call(where):
        pl.semaphore_signal(barrier, inc=1, device_id=where, device_id_type=MESH)

    each(ROWS, lambda k: call((img, lax.rem(row + k, ROWS))))
    each(IMGS // 2, lambda k: call((lax.rem(img + 2 * k, IMGS), row)))
    call((img + 1 - 2 * lax.rem(img, 2), row))
    z, x, y, core = coords(img, row)
    other = 2 * (1 - lax.div(x, 2)) + (1 - lax.rem(x, 2))
    call(device(z, other, y, core))
    return ROWS - 1 + IMGS // 2 - 1 + 1 + 1


class RowSum:
    def __init__(self, img, row, part, inbox, sems):
        self.img, self.row, self.part, self.inbox, self.sems = img, row, part, inbox, sems

    def copy(self, k):
        r = lax.rem(self.row + k, ROWS)
        src = self.part.at[lax.rem(r, 2), rows16(lax.div(r, 2))]
        return remote(src, self.inbox.at[k - 1], self.sems, k - 1, (self.img, r))

    def start(self):
        each(ROWS, lambda k: self.copy(k).start())

    def total(self):
        own = self.part[lax.rem(self.row, 2), rows16(lax.div(self.row, 2))].astype(F32)

        def body(k, acc):
            self.copy(k).wait_recv()
            return acc + self.inbox[k - 1].astype(F32)

        return lax.fori_loop(1, ROWS, body, own)

    def finish(self):
        each(ROWS, lambda k: self.copy(k).wait_send())


class Gather:
    def __init__(self, count, me, where, target, sems):
        self.count, self.me, self.where, self.target, self.sems = count, me, where, target, sems

    def copy(self, k):
        to = lax.rem(self.me + k, self.count)
        return remote(
            self.target(self.me), self.target(self.me), self.sems, k - 1, self.where(to)
        )

    def start(self):
        each(self.count, lambda k: self.copy(k).start())

    def wait(self):
        each(self.count, lambda k: self.copy(k).wait_recv())

    def finish(self):
        each(self.count, lambda k: self.copy(k).wait_send())


class Pick:
    def __init__(self, img, row, everyone, give, got, sems, pair_sems):
        self.img, self.row, self.core = img, row, lax.rem(img, 2)
        self.everyone, self.give, self.got, self.pair_sems = everyone, give, got, pair_sems
        self.gather = Gather(
            IMGS // 2, lax.div(img, 2), lambda j: (2 * j + self.core, row),
            lambda j: everyone.at[j], sems,
        )

    def start(self, own):
        self.everyone[lax.div(self.img, 2)] = own
        self.gather.start()

    def pair(self):
        where = (self.img + 1 - 2 * self.core, self.row)
        return remote(self.give, self.got, self.pair_sems, 0, where)

    def relay(self, wanted):
        self.gather.wait()
        self.give[...] = self.everyone[lax.div(wanted, 2)]
        self.pair().start()

    def result(self, source):
        self.pair().wait_recv()
        own = self.everyone[lax.div(source, 2)].astype(F32)
        return jnp.where(lax.rem(source, 2) == self.core, own, self.got[...].astype(F32)).astype(BF16)

    def finish(self):
        self.gather.finish()
        self.pair().wait_send()


def total_of(count, base, piece):
    return lax.fori_loop(1, count, lambda k, acc: acc + piece(k).astype(F32), base.astype(F32))


def matmul(left, right):
    return jnp.dot(left, right, preferred_element_type=F32)


def against(left, right):
    return lax.dot_general(left, right, (((1,), (1,)), ((), ())), preferred_element_type=F32)


def shifted(field, step):
    lane = lax.broadcasted_iota(jnp.int32, (field.shape[0], 128), 1)
    edge = 127 if step > 0 else 0
    parts = []
    for start in range(0, field.shape[1], 128):
        turned = pltpu.roll(field[:, start : start + 128], (-step) % 128, 1)
        parts.append(jnp.where(lane == edge, 0.0, turned))
    return parts[0] if len(parts) == 1 else jnp.concatenate(parts, axis=1)


def spread(rows, target, flip):
    lane = lax.div(lax.broadcasted_iota(jnp.int32, rows.shape, 1), HEAD_DIM)
    wide = rows.astype(F32)
    full = jnp.concatenate([jnp.where(lane == h, wide, 0.0) for h in range(HEADS)], axis=0)
    target[...] = full.astype(BF16)
    flip[...] = full.T.astype(BF16)


def diagonal(full):
    lane = lax.div(lax.broadcasted_iota(jnp.int32, (SLOTS, CHANNELS), 1), HEAD_DIM)
    total = jnp.zeros((SLOTS, CHANNELS), F32)
    for h in range(HEADS):
        total = jnp.where(lane == h, full[h * SLOTS : (h + 1) * SLOTS], total)
    return total


def kernel(
    group_ref, slot_ref, time_ref,
    hidden_ref, kvw_ref, latent_ref, noise_ref, emb_ref, inw_ref, qw_ref, ow_ref, resw_hbm, up_hbm,
    block3_ref, res_ref, query_ref, out_ref, ghidden_ref, kvout_ref,
    resw_ref, up3_ref, load_sems, turn, up_ref, block_ref,
    noisy, band, cond, part, f_inbox, f_all, f_give, f_got, f_kv, wcat, qw_t, ow_t, taps, first,
    hid, query, att, prob, gatt, gscore, gquery, ghid, bk, bk_t, bv, bv_t,
    gkv, s_inbox, s_all, s_give, s_got, s_image,
    grads, in_core, half, in_1, mid, in_2, sum_f, in_z, final,
    k_part, k_core, k_half, k_low1, k_z1, k_sum1, k_sum2, k_z2, k_low2, k_final,
    halo_sems, f_sum_sems, f_img_sems, f_pair_sems, f_row_sems,
    s_sum_sems, s_img_sems, s_pair_sems, s_row_sems,
    core_sems, s1_sems, s2_sems, z_sems,
    gz_sems, g1_sems, g2_sems, gcore_sems,
    kc_sems, kx1_sems, kz1_sems, kx2_sems, kz2_sems,
    kgx1_sems, kgz1_sems, kgx2_sems, kgz2_sems, kgc_sems,
    *, weight_scale, kv_scale,
):
    loads = [
        pltpu.make_async_copy(resw_hbm, resw_ref, load_sems.at[0]),
        pltpu.make_async_copy(up_hbm, up3_ref, load_sems.at[1]),
    ]
    for load in loads:
        load.start()
    img, row = place()
    z, x, y, core = coords(img, row)
    partner = device(z, x, y, 1 - core)
    low = lax.rem(x, 2)
    across = device(z, x + 1 - 2 * low, y, core)

    band[...] = jnp.zeros_like(band)
    signals = greet(img, row)

    def at_x(k):
        return lax.rem(x + k, 4)

    def at_y(k):
        return lax.rem(y + k, 4)

    def at_z(k):
        return lax.rem(z + k, 8)

    token = lax.broadcasted_iota(jnp.int32, (SLOTS, hidden_ref.shape[0]), 1)
    wanted = lax.broadcasted_iota(jnp.int32, (SLOTS, hidden_ref.shape[0]), 0) + slot_ref[0]
    cond[...] = matmul((token == wanted).astype(BF16), hidden_ref[...]).astype(BF16)
    product = matmul(cond[...], kvw_ref[...])
    part[0] = product[:, :CHANNELS]
    part[1] = product[:, CHANNELS:]

    index = lax.broadcasted_iota(jnp.int32, (8, 128), 0) * 128 + lax.broadcasted_iota(
        jnp.int32, (8, 128), 1
    )
    share_of = index.astype(F32) / 999.0
    beta = (0.00085**0.5 * (1.0 - share_of) + 0.012**0.5 * share_of) ** 2
    logs = jnp.where(index <= time_ref[0], jnp.log(1.0 - jnp.where(index < 1000, beta, 0.0)), 0.0)
    level = jnp.exp(jnp.sum(logs, axis=(0, 1), keepdims=True))
    keep, add = jnp.sqrt(level), jnp.sqrt(1.0 - level)
    for c in range(4):
        noisy[c] = (keep * latent_ref[c] + add * noise_ref[c]).astype(BF16).astype(F32)
    for r in range(8):
        band[2 + r, pl.ds(0, 4)] = noisy[:, r, :]

    pl.semaphore_wait(pltpu.get_barrier_semaphore(), signals)

    def halo_up():
        return remote(band.at[pl.ds(8, 2)], band.at[pl.ds(0, 2)], halo_sems, 0, (img, lax.rem(row + 1, ROWS)))

    def halo_down():
        return remote(band.at[pl.ds(2, 2)], band.at[pl.ds(10, 2)], halo_sems, 1, (img, lax.rem(row + ROWS - 1, ROWS)))

    above, below = row > 0, row < ROWS - 1
    pl.when(below)(lambda: halo_up().start())
    pl.when(above)(lambda: halo_down().start())
    f_sum = RowSum(img, row, part, f_inbox, f_sum_sems)
    f_sum.start()

    loads[0].wait()
    for a in range(3):
        for b in range(3):
            wcat[a, :, b * CHANNELS : (b + 1) * CHANNELS] = resw_ref[3 * a + b]
    qw_t[...] = qw_ref[...].astype(F32).T.astype(BF16)
    ow_t[...] = ow_ref[...].astype(F32).T.astype(BF16)

    def source_of(which):
        return lax.fori_loop(
            0, IMGS, lambda i, s: jnp.maximum(s, jnp.where(group_ref[i] == which, i, 0)), jnp.int32(0)
        )

    other = img + 1 - 2 * core
    source, other_source = source_of(img), source_of(other)
    f_pick = Pick(img, row, f_all, f_give, f_got, f_img_sems, f_pair_sems)
    f_pick.start(f_sum.total().astype(BF16))

    pl.when(above)(lambda: halo_up().wait_recv())
    pl.when(below)(lambda: halo_down().wait_recv())

    def first_rows(j):
        fields = []
        for r in range(2):
            pieces = []
            for a in range(3):
                n = band[2 * j + r + a]
                pieces += [shifted(n, -1), n, shifted(n, 1)]
            fields.append(jnp.concatenate(pieces, axis=0))
        field = jnp.concatenate(fields, axis=1).astype(BF16)
        value = matmul(inw_ref[...], field)
        lanes = pl.ds(pl.multiple_of(j * 256, 256), 256)
        first[:, lanes] = value
        v = value + emb_ref[...]
        line = row * 8 - 1 + 2 * j + lax.div(lax.broadcasted_iota(jnp.int32, v.shape, 1), 128)
        act = jnp.where((line >= 0) & (line < 64), v / (1.0 + jnp.exp(-v)), 0.0)
        act = act.astype(BF16).astype(F32)
        taps[pl.ds(0, CHANNELS), lanes] = shifted(act, -1).astype(BF16)
        taps[pl.ds(CHANNELS, CHANNELS), lanes] = act.astype(BF16)
        taps[pl.ds(2 * CHANNELS, CHANNELS), lanes] = shifted(act, 1).astype(BF16)

    each(5, first_rows, 0)

    def cells(n, more=0):
        return pl.ds(pl.multiple_of(n * 256 + more, 128), 256)

    def residual(n):
        acc = first[:, cells(n, 128)]
        for a in range(3):
            acc = acc + matmul(wcat[a], taps[:, cells(n, 128 * a)])
        hid[:, cells(n)] = acc.astype(BF16)

    each(2, residual, 0)
    f_pick.relay(other_source)
    each(4, residual, 2)

    f_kv[lax.rem(row, 2), rows16(lax.div(row, 2))] = f_pick.result(source)
    f_share = Gather(
        ROWS, row, lambda j: (img, j),
        lambda j: f_kv.at[lax.rem(j, 2), rows16(lax.div(j, 2))], f_row_sems,
    )
    f_share.start()

    loads[1].wait()

    def flatten(c):
        channels = rows16(4 * c, 64)
        turn[...] = up3_ref[channels].astype(F32)
        for r in range(8):
            up_ref[channels, r * 128 : (r + 1) * 128] = turn[:, r, :].astype(BF16)

    each(5, flatten, 0)

    def unflatten(c):
        channels = rows16(4 * c, 64)
        for r in range(8):
            turn[:, r, :] = block_ref[channels, r * 128 : (r + 1) * 128].astype(F32)
        block3_ref[channels] = turn[...].astype(BF16)

    def projections(n):
        query[:, cells(n)] = matmul(qw_ref[...], hid[:, cells(n)]).astype(BF16)
        gatt[:, cells(n)] = matmul(ow_t[...], up_ref[:, cells(n)]).astype(BF16)

    each(4, projections, 0)
    f_share.wait()
    spread(f_kv[0], bk, bk_t)
    spread(f_kv[1], bv, bv_t)

    def attend(n):
        here = cells(n)
        score = matmul(bk[...], query[:, here]) * HEAD_DIM**-0.5
        score = score.reshape(HEADS, SLOTS, 256)
        top = jnp.max(score, axis=1, keepdims=True)
        grown = jnp.exp(score - top)
        soft = grown / jnp.sum(grown, axis=1, keepdims=True)
        soft_low = soft.reshape(CHANNELS, 256).astype(BF16)
        prob[:, here] = soft_low
        gprob = matmul(bv[...], gatt[:, here]).reshape(HEADS, SLOTS, 256)
        mean = jnp.sum(soft * gprob, axis=1, keepdims=True)
        gs = (HEAD_DIM**-0.5 * soft * (gprob - mean)).reshape(CHANNELS, 256).astype(BF16)
        gscore[:, here] = gs

    def attend_more(n):
        here = cells(n)
        attended = matmul(bv_t[...], prob[:, here]).astype(BF16)
        att[:, here] = attended
        block_ref[:, here] = (
            hid[:, here].astype(F32) + matmul(ow_ref[...], attended)
        ).astype(BF16)
        gq = matmul(bk_t[...], gscore[:, here]).astype(BF16)
        gquery[:, here] = gq
        ghid[:, here] = (up_ref[:, here].astype(F32) + matmul(qw_t[...], gq)).astype(BF16)

    each(4, attend, 0)

    gkv[0] = diagonal(against(gscore[...], query[...])).astype(BF16)
    gkv[1] = diagonal(against(prob[...], gatt[...])).astype(BF16)
    row_sum = RowSum(img, row, gkv, s_inbox, s_sum_sems)
    row_sum.start()

    each(4, attend_more, 0)

    def core_copy(t):
        return remote(
            grads.at[t, rows16((1 - core) * 10, 160)], in_core.at[t], core_sems, t, partner
        )

    grads[0] = against(gquery[...], hid[...]).astype(BF16)
    core_copy(0).start()
    grads[1] = against(up_ref[...], att[...]).astype(BF16)
    core_copy(1).start()

    def tap(t):
        a, b = lax.div(t - 2, 3), lax.rem(t - 2, 3)
        field = taps[
            pl.ds(pl.multiple_of(b * CHANNELS, CHANNELS), CHANNELS),
            pl.ds(pl.multiple_of(a * 128, 128), 1024),
        ]
        grads[t] = against(ghid[...], field).astype(BF16)
        core_copy(t).start()

    def x_first(j):
        return j % 2 == 1 or j == SLICES - 1

    def at(axis_x, k):
        return device(z, at_x(k), y, core) if axis_x else device(z, x, at_y(k), core)

    def s1_copy(j, k):
        src = half.at[j, at_x(k)] if x_first(j) else half.at[j, :, at_y(k)]
        return remote(src, in_1.at[j, k - 1], s1_sems, 3 * j + k - 1, at(x_first(j), k))

    def s2_copy(j, k):
        src = mid.at[j, at_y(k) if x_first(j) else at_x(k)]
        return remote(src, in_2.at[j, k - 1], s2_sems, 3 * j + k - 1, at(not x_first(j), k))

    def z_copy(k):
        to = at_z(k)
        return remote(
            sum_f.at[lax.rem(to, 7)], in_z.at[k - 1], z_sems, k - 1, device(to, x, y, core)
        )

    def to_owner(k, act):
        pl.when(at_z(k) < 7)(lambda: act(k))

    def from_owner(k, act):
        pl.when(lax.rem(z + 8 - k, 8) < 7)(lambda: act(k))

    def across_cores(j, begin, end):
        each(end, lambda t: core_copy(t).wait_recv(), begin)

        def add(u):
            unit = 16 * j + u
            t, i = lax.div(unit, 10), lax.rem(unit, 10)
            half[j, lax.div(u, 4), lax.rem(u, 4)] = (
                grads[t, rows16(core * 10 + i)].astype(F32) + in_core[t, rows16(i)].astype(F32)
            ).astype(BF16)

        each(min(16, TAPS * 10 - 16 * j), add, 0)
        each(4, lambda k: s1_copy(j, k).start())

    def across_first(j):
        each(4, lambda k: s1_copy(j, k).wait_recv())
        own = half[j, x] if x_first(j) else half[j, :, y]
        mid[j] = total_of(4, own, lambda k: in_1[j, k - 1]).astype(BF16)
        each(4, lambda k: s2_copy(j, k).start())

    def across_second(j):
        each(4, lambda k: s2_copy(j, k).wait_recv())
        own = mid[j, y if x_first(j) else x]
        sum_f[j] = total_of(4, own, lambda k: in_2[j, k - 1]).astype(BF16)
        pl.when(z != j)(lambda: z_copy(lax.rem(j + 8 - z, 8)).start())

    half[SLICES - 1, 3, pl.ds(2, 2)] = jnp.zeros((2, 16, CHANNELS), BF16)
    pick = Pick(img, row, s_all, s_give, s_got, s_img_sems, s_pair_sems)
    each(3, tap, 2)
    pick.start(row_sum.total().astype(BF16))
    across_cores(0, 0, 2)
    each(5, tap, 3)
    across_cores(1, 2, 4)
    each(6, tap, 5)
    across_cores(2, 4, 5)
    each(8, tap, 6)
    across_cores(3, 5, 7)
    each(9, tap, 8)
    across_cores(4, 7, 8)
    across_first(0)
    each(11, tap, 9)
    across_cores(5, 8, 10)
    across_cores(6, 10, 11)
    across_first(1)
    across_first(2)
    across_second(0)

    pick.relay(group_ref[other])
    across_first(3)
    across_second(1)
    s_image[lax.rem(row, 2), rows16(lax.div(row, 2))] = pick.result(group_ref[img])
    share = Gather(
        ROWS, row, lambda j: (img, j),
        lambda j: s_image.at[lax.rem(j, 2), rows16(lax.div(j, 2))], s_row_sems,
    )
    share.start()
    across_first(4)
    across_second(2)
    across_first(5)
    across_second(3)
    across_first(6)
    across_second(4)

    share.wait()
    features = cond.shape[1]
    for side in range(2):
        k_part[
            pl.ds(0, features // 16), :, side * CHANNELS : (side + 1) * CHANNELS
        ] = (
            lax.dot_general(
                cond[...], s_image[side], (((0,), (0,)), ((), ())), preferred_element_type=F32
            )
            .astype(BF16)
            .reshape(features // 16, 16, CHANNELS)
        )
    k_part[pl.ds(features // 16, 4)] = jnp.zeros((4, 16, 2 * CHANNELS), BF16)

    def kc_copy():
        return remote(k_part.at[pl.ds((1 - core) * 28, 28)], k_core, kc_sems, 0, partner)

    kc_copy().start()
    across_second(5)
    across_second(6)

    def kx1_copy():
        return remote(k_half.at[pl.ds((1 - low) * 7, 7)], k_low1, kx1_sems, 0, across)

    def kz1_copy(k):
        to = at_z(k)
        return remote(
            k_sum1.at[lax.rem(to, 7)], k_z1.at[k - 1], kz1_sems, k - 1, device(to, x, y, core)
        )

    def kz2_copy(k):
        to = at_z(k)
        return remote(
            k_half.at[pl.ds(14 + 2 * lax.rem(to, 7), 2)], k_z2.at[k - 1], kz2_sems, k - 1,
            device(to, x, y, core),
        )

    def kx2_copy():
        return remote(k_sum2.at[1 - low], k_low2, kx2_sems, 0, across)

    kc_copy().wait_recv()

    def add_kc(j):
        k_half[j] = (k_part[core * 28 + j].astype(F32) + k_core[j].astype(F32)).astype(BF16)

    each(28, add_kc, 14)
    each(8, lambda k: to_owner(k, lambda i: kz2_copy(i).start()))
    each(14, add_kc, 0)
    kx1_copy().start()

    zi = lax.rem(z, 7)

    @pl.when(z < 7)
    def _():
        each(8, lambda k: z_copy(k).wait_recv())
        done = total_of(8, sum_f[zi], lambda k: in_z[k - 1]) * weight_scale
        final[core, zi, x, y] = done.astype(BF16)

    def gz_copy(k):
        mine = final.at[core, zi, x, y]
        return remote(mine, mine, gz_sems, k - 1, device(at_z(k), x, y, core))

    @pl.when(z < 7)
    def _():
        each(8, lambda k: gz_copy(k).start())

    gcond = against(jnp.concatenate([s_image[0], s_image[1]], axis=1), kvw_ref[...]).astype(BF16)
    spot = lax.broadcasted_iota(jnp.int32, (hidden_ref.shape[0], SLOTS), 0)
    slot = lax.broadcasted_iota(jnp.int32, (hidden_ref.shape[0], SLOTS), 1) + slot_ref[0]
    ghidden_ref[...] = matmul((spot == slot).astype(BF16), gcond).astype(BF16)

    kx1_copy().wait_recv()

    def add_kx1(j):
        k_sum1[j] = (k_half[low * 7 + j].astype(F32) + k_low1[j].astype(F32)).astype(BF16)

    each(7, add_kx1, 0)
    each(8, lambda k: to_owner(k, lambda i: kz1_copy(i).start()))

    each(5, unflatten, 0)

    def g1_copy(j, k):
        mine = final.at[core, j, x, y]
        return remote(mine, mine, g1_sems, 3 * j + k - 1, at(not x_first(j), k))

    def g2_copy(j, k):
        mine = final.at[core, j, x] if x_first(j) else final.at[core, j, :, y]
        return remote(mine, mine, g2_sems, 3 * j + k - 1, at(x_first(j), k))

    def core_pass(j, k):
        mine = (
            final.at[core, j, lax.rem(x + 4 - k, 4)]
            if x_first(j)
            else final.at[core, j, :, lax.rem(y + 4 - k, 4)]
        )
        return remote(mine, mine, gcore_sems, 4 * j + k, partner)

    def spread_second(j):
        @pl.when(z != j)
        def _():
            gz_copy(lax.rem(z + 8 - j, 8)).wait_recv()

        each(4, lambda k: g1_copy(j, k).start())

    def spread_first(j):
        each(4, lambda k: g1_copy(j, k).wait_recv())
        each(4, lambda k: g2_copy(j, k).start())
        core_pass(j, 0).start()

    def spread_core(j):
        def go(k):
            g2_copy(j, k).wait_recv()
            core_pass(j, k).start()

        each(4, go)

    for j in range(SLICES):
        spread_second(j)

    @pl.when(z < 7)
    def _():
        each(8, lambda k: kz2_copy(k).wait_recv())
        own = k_half[pl.ds(14 + 2 * zi, 2)]
        k_sum2[...] = total_of(8, own, lambda k: k_z2[k - 1]).astype(BF16)
        kx2_copy().start()

    for j in range(SLICES):
        spread_first(j)

    def kgz1_copy(k):
        mine = k_final.at[core, low * 7 + zi]
        return remote(mine, mine, kgz1_sems, k - 1, device(at_z(k), x, y, core))

    def kgx1_copy():
        mine = k_final.at[core, pl.ds(low * 7, 7)]
        return remote(mine, mine, kgx1_sems, 0, across)

    def kgx2_copy():
        mine = k_final.at[core, 14 + 2 * zi + low]
        return remote(mine, mine, kgx2_sems, 0, across)

    def kgz2_copy(k):
        mine = k_final.at[core, pl.ds(14 + 2 * zi, 2)]
        return remote(mine, mine, kgz2_sems, k - 1, device(at_z(k), x, y, core))

    @pl.when(z < 7)
    def _():
        kx2_copy().wait_recv()
        done = (k_sum2[low].astype(F32) + k_low2[...].astype(F32)) * kv_scale
        k_final[core, 14 + 2 * zi + low] = done.astype(BF16)
        kgx2_copy().start()
        each(8, lambda k: kz1_copy(k).wait_recv())
        done = total_of(8, k_sum1[zi], lambda k: k_z1[k - 1]) * kv_scale
        k_final[core, low * 7 + zi] = done.astype(BF16)
        each(8, lambda k: kgz1_copy(k).start())
        kgx2_copy().wait_recv()
        each(8, lambda k: kgz2_copy(k).start())

    for j in range(0, 3):
        spread_core(j)
    each(8, lambda k: from_owner(k, lambda i: kgz1_copy(i).wait_recv()))
    kgx1_copy().start()

    def kgc_copy(k):
        begin, count = ((low * 7, 7), (14, 7), (21, 7), ((1 - low) * 7, 7))[k]
        mine = k_final.at[core, pl.ds(begin, count)]
        return remote(mine, mine, kgc_sems, k, partner)

    kgc_copy(0).start()
    for j in range(3, SLICES):
        spread_core(j)
    each(8, lambda k: from_owner(k, lambda i: kgz2_copy(i).wait_recv()))
    kgc_copy(1).start()
    kgc_copy(2).start()
    kgx1_copy().wait_recv()
    kgc_copy(3).start()

    for j in range(SLICES):
        each(4, lambda k, j=j: core_pass(j, k).wait_recv(), 0)

    for t in range(TAPS):
        target, base = ((query_ref, 0), (out_ref, 0))[t] if t < 2 else (res_ref, (t - 2) * CHANNELS)
        for c in range(2):
            for i in range(10):
                j, rest = divmod(t * 10 + i, 16)
                target[pl.ds(base + c * 160 + i * 16, 16)] = final[c, j, rest // 4, rest % 4]
    for k in range(4):
        kgc_copy(k).wait_recv()
    for unit in range(52):
        kvout_ref[pl.ds(16 * unit, 16)] = k_final[unit // 28, unit % 28]

    pl.when(below)(lambda: halo_up().wait_send())
    pl.when(above)(lambda: halo_down().wait_send())
    for one in (f_sum, f_pick, f_share, row_sum, pick, share):
        one.finish()
    each(TAPS, lambda t: core_copy(t).wait_send(), 0)
    for j in range(SLICES):
        for copy in (s1_copy, s2_copy, g1_copy, g2_copy):
            each(4, lambda k, copy=copy, j=j: copy(j, k).wait_send())
        each(4, lambda k, j=j: core_pass(j, k).wait_send(), 0)
    each(8, lambda k: to_owner(k, lambda i: z_copy(i).wait_send()))
    each(8, lambda k: to_owner(k, lambda i: kz1_copy(i).wait_send()))
    each(8, lambda k: to_owner(k, lambda i: kz2_copy(i).wait_send()))

    @pl.when(z < 7)
    def _():
        for copy in (gz_copy, kgz1_copy, kgz2_copy):
            each(8, lambda k, copy=copy: copy(k).wait_send())
        kx2_copy().wait_send()
        kgx2_copy().wait_send()

    kc_copy().wait_send()
    kx1_copy().wait_send()
    kgx1_copy().wait_send()
    for k in range(4):
        kgc_copy(k).wait_send()


def finish_kernel(*refs):
    count = (len(refs) - 1) // 3
    sems = refs[-1]
    loads = [pltpu.make_async_copy(refs[i], refs[2 * count + i], sems.at[0, i]) for i in range(count)]
    stores = [pltpu.make_async_copy(refs[2 * count + i], refs[count + i], sems.at[1, i]) for i in range(count)]
    for load in loads:
        load.start()
    for load, store in zip(loads, stores):
        load.wait()
        store.start()
    for store in stores:
        store.wait()


def finish(arrays):
    anywhere = pl.BlockSpec(memory_space=pl.ANY)
    return pl.pallas_call(
        finish_kernel,
        out_shape=tuple(jax.ShapeDtypeStruct(a.shape, a.dtype) for a in arrays),
        in_specs=[anywhere] * len(arrays),
        out_specs=(anywhere,) * len(arrays),
        scratch_shapes=[pltpu.VMEM(a.shape, a.dtype) for a in arrays]
        + [pltpu.SemaphoreType.DMA((2, len(arrays)))],
        compiler_params=pltpu.CompilerParams(vmem_limit_bytes=32 * 2**20),
        name="finish",
    )(*arrays)


def shards(
    llm_hidden,
    slot_start,
    image_group,
    timesteps,
    latents,
    noise,
    kv_weight,
    in_weight,
    res_weight,
    query_weight,
    out_weight,
    cotangent,
):
    width, features = CHANNELS, llm_hidden.shape[1]
    frequency = jnp.exp(-math.log(10000.0) * jnp.arange(width // 2, dtype=F32) / (width // 2))
    angles = timesteps[0].astype(F32) * frequency
    emb = jnp.concatenate([jnp.cos(angles), jnp.sin(angles)])[:, None]
    in_matrix = jnp.pad(in_weight.transpose(2, 0, 1, 3), ((0, 0), (0, 0), (0, 0), (0, 4)))
    vmem, smem = pl.BlockSpec(memory_space=pltpu.VMEM), pl.BlockSpec(memory_space=pltpu.SMEM)
    anywhere = pl.BlockSpec(memory_space=pl.ANY)
    dma = lambda n: pltpu.SemaphoreType.DMA((2, n))
    low = lambda *shape: pltpu.VMEM(shape, BF16)
    field, square = low(width, 1024), low(width, width)
    out = lambda *shape: jax.ShapeDtypeStruct(shape, BF16)
    block, res, query, projection, grad_hidden, grad_kv_weight = pl.pallas_call(
        functools.partial(
            kernel,
            weight_scale=(IMGS * ROWS * 1024) ** (-0.5),
            kv_scale=(IMGS * SLOTS) ** (-0.5),
        ),
        out_shape=(
            out(width, 8, 128), out(9 * width, width), out(width, width), out(width, width),
            out(*llm_hidden.shape), out(*kv_weight.shape),
        ),
        in_specs=[smem] * 3 + [vmem] * 8 + [anywhere] * 2,
        out_specs=(vmem,) * 6,
        scratch_shapes=[
            low(9, width, width), low(width, 8, 128), pltpu.SemaphoreType.DMA((2,)),
            pltpu.VMEM((64, 8, 128), F32), field, field,
            pltpu.VMEM((4, 8, 128), F32), pltpu.VMEM((12, 8, 128), F32),
            low(SLOTS, features), pltpu.VMEM((2, SLOTS, width), F32),
            pltpu.VMEM((ROWS - 1, 16, width), F32), low(IMGS // 2, 16, width),
            low(16, width), low(16, width), low(2, SLOTS, width),
            low(3, width, 3 * width), square, square,
            low(3 * width, 1280), pltpu.VMEM((width, 1280), F32),
            field, field, field, field, field, field, field, field, square, square, square, square,
            low(2, SLOTS, width), low(ROWS - 1, 16, width), low(IMGS // 2, 16, width),
            low(16, width), low(16, width), low(2, SLOTS, width),
            low(TAPS, width, width), low(TAPS, 160, width), low(SLICES, 4, 4, 16, width),
            low(SLICES, 3, 4, 16, width), low(SLICES, 4, 16, width), low(SLICES, 3, 16, width),
            low(SLICES, 16, width), low(7, 16, width), low(2, SLICES, 4, 4, 16, width),
            low(56, 16, 2 * width), low(28, 16, 2 * width), low(28, 16, 2 * width),
            low(7, 16, 2 * width), low(7, 16, 2 * width), low(7, 16, 2 * width),
            low(2, 16, 2 * width), low(7, 2, 16, 2 * width), low(16, 2 * width),
            low(2, 28, 16, 2 * width),
            dma(2), dma(7), dma(15), dma(1), dma(7),
            dma(7), dma(15), dma(1), dma(7),
            dma(TAPS), dma(3 * SLICES), dma(3 * SLICES), dma(7),
            dma(7), dma(3 * SLICES), dma(3 * SLICES), dma(4 * SLICES),
            dma(1), dma(1), dma(7), dma(1), dma(7),
            dma(1), dma(7), dma(1), dma(7), dma(4),
        ],
        compiler_params=pltpu.CompilerParams(
            collective_id=0, has_side_effects=True, vmem_limit_bytes=60 * 2**20
        ),
        name="block",
    )(
        image_group, slot_start, timesteps, llm_hidden, kv_weight, latents[0], noise[0], emb,
        in_matrix.reshape(width, 72).astype(BF16), query_weight, out_weight,
        res_weight.reshape(9, width, width), cotangent[0],
    )
    query, projection, block, grad_hidden, grad_kv_weight, res = finish(
        (query, projection, block, grad_hidden, grad_kv_weight, res.reshape(3, 3, width, width))
    )
    return block[None], grad_hidden, grad_kv_weight, res, query, projection


def solution(mesh):
    return jax.shard_map(
        shards,
        mesh=mesh,
        in_specs=(
            P("img", "row"),
            P("img"),
            P(),
            P("img"),
            P("img", None, "row", None),
            P("img", None, "row", None),
            P("row", None),
            P(),
            P(),
            P(),
            P(),
            P("img", None, "row", None),
        ),
        out_specs=(P("img", None, "row", None), P("img", "row"), P("row", None), P(), P(), P()),
        check_vma=False,
    )
```

```python
import functools
import math

import jax
import jax.numpy as jnp
from jax import lax
from jax.experimental import pallas as pl
from jax.experimental.pallas import tpu as pltpu
from jax.sharding import PartitionSpec as P

HEAD_DIM = 64
SLOTS = 64
MESH = pl.DeviceIdType.MESH
CHANNELS = 320
HEADS = 5
IMGS, ROWS = 32, 8
TAPS = 11
SLICES = 7
F32, BF16 = jnp.float32, jnp.bfloat16


def place():
    img, row = lax.axis_index("img"), lax.axis_index("row")
    return img, row


def coords(img, row):
    z, low, core = lax.div(img, 4), lax.rem(lax.div(img, 2), 2), lax.rem(img, 2)
    return z, lax.div(row, 4) * 2 + low, lax.rem(row, 4), core


def device(z, x, y, core):
    return (z * 4 + lax.rem(x, 2) * 2 + core, lax.div(x, 2) * 4 + y)


def remote(src, dst, sems, slot, where):
    return pltpu.make_async_remote_copy(
        src_ref=src,
        dst_ref=dst,
        send_sem=sems.at[0, slot],
        recv_sem=sems.at[1, slot],
        device_id=where,
        device_id_type=MESH,
    )


def each(count, act, first=1):
    def body(k, carry):
        act(k)
        return carry

    lax.fori_loop(first, count, body, 0)


def rows16(index, count=16):
    return pl.ds(pl.multiple_of(index * 16, 16), count)


def greet(img, row):
    barrier = pltpu.get_barrier_semaphore()

    def call(where):
        pl.semaphore_signal(barrier, inc=1, device_id=where, device_id_type=MESH)

    each(ROWS, lambda k: call((img, lax.rem(row + k, ROWS))))
    each(IMGS // 2, lambda k: call((lax.rem(img + 2 * k, IMGS), row)))
    call((img + 1 - 2 * lax.rem(img, 2), row))
    z, x, y, core = coords(img, row)
    other = 2 * (1 - lax.div(x, 2)) + (1 - lax.rem(x, 2))
    call(device(z, other, y, core))
    return ROWS - 1 + IMGS // 2 - 1 + 1 + 1


class RowSum:
    def __init__(self, img, row, part, inbox, sems):
        self.img, self.row, self.part, self.inbox, self.sems = img, row, part, inbox, sems

    def copy(self, k):
        r = lax.rem(self.row + k, ROWS)
        src = self.part.at[lax.rem(r, 2), rows16(lax.div(r, 2))]
        return remote(src, self.inbox.at[k - 1], self.sems, k - 1, (self.img, r))

    def start(self):
        each(ROWS, lambda k: self.copy(k).start())

    def total(self):
        own = self.part[lax.rem(self.row, 2), rows16(lax.div(self.row, 2))].astype(F32)

        def body(k, acc):
            self.copy(k).wait_recv()
            return acc + self.inbox[k - 1].astype(F32)

        return lax.fori_loop(1, ROWS, body, own)

    def finish(self):
        each(ROWS, lambda k: self.copy(k).wait_send())


class Gather:
    def __init__(self, count, me, where, target, sems):
        self.count, self.me, self.where, self.target, self.sems = count, me, where, target, sems

    def copy(self, k):
        to = lax.rem(self.me + k, self.count)
        return remote(
            self.target(self.me), self.target(self.me), self.sems, k - 1, self.where(to)
        )

    def start(self):
        each(self.count, lambda k: self.copy(k).start())

    def wait(self):
        each(self.count, lambda k: self.copy(k).wait_recv())

    def finish(self):
        each(self.count, lambda k: self.copy(k).wait_send())


class Pick:
    def __init__(self, img, row, everyone, give, got, sems, pair_sems):
        self.img, self.row, self.core = img, row, lax.rem(img, 2)
        self.everyone, self.give, self.got, self.pair_sems = everyone, give, got, pair_sems
        self.gather = Gather(
            IMGS // 2, lax.div(img, 2), lambda j: (2 * j + self.core, row),
            lambda j: everyone.at[j], sems,
        )

    def start(self, own):
        self.everyone[lax.div(self.img, 2)] = own
        self.gather.start()

    def pair(self):
        where = (self.img + 1 - 2 * self.core, self.row)
        return remote(self.give, self.got, self.pair_sems, 0, where)

    def relay(self, wanted):
        self.gather.wait()
        self.give[...] = self.everyone[lax.div(wanted, 2)]
        self.pair().start()

    def result(self, source):
        self.pair().wait_recv()
        own = self.everyone[lax.div(source, 2)].astype(F32)
        return jnp.where(lax.rem(source, 2) == self.core, own, self.got[...].astype(F32)).astype(BF16)

    def finish(self):
        self.gather.finish()
        self.pair().wait_send()


def total_of(count, base, piece):
    return lax.fori_loop(1, count, lambda k, acc: acc + piece(k).astype(F32), base.astype(F32))


def matmul(left, right):
    return jnp.dot(left, right, preferred_element_type=F32)


def against(left, right):
    return lax.dot_general(left, right, (((1,), (1,)), ((), ())), preferred_element_type=F32)


def against_first(left, right):
    return lax.dot_general(left, right, (((0,), (0,)), ((), ())), preferred_element_type=F32)


def shifted(field, step):
    lane = lax.broadcasted_iota(jnp.int32, (field.shape[0], 128), 1)
    edge = 127 if step > 0 else 0
    parts = []
    for start in range(0, field.shape[1], 128):
        turned = pltpu.roll(field[:, start : start + 128], (-step) % 128, 1)
        parts.append(jnp.where(lane == edge, 0.0, turned))
    return parts[0] if len(parts) == 1 else jnp.concatenate(parts, axis=1)


def spread(rows, target, flip):
    lane = lax.div(lax.broadcasted_iota(jnp.int32, rows.shape, 1), HEAD_DIM)
    wide = rows.astype(F32)
    full = jnp.concatenate([jnp.where(lane == h, wide, 0.0) for h in range(HEADS)], axis=0)
    target[...] = full.astype(BF16)
    flip[...] = full.T.astype(BF16)


def diagonal(full):
    lane = lax.div(lax.broadcasted_iota(jnp.int32, (SLOTS, CHANNELS), 1), HEAD_DIM)
    total = jnp.zeros((SLOTS, CHANNELS), F32)
    for h in range(HEADS):
        total = jnp.where(lane == h, full[h * SLOTS : (h + 1) * SLOTS], total)
    return total


def kernel(
    group_ref, slot_ref, time_ref,
    hidden_ref, kvw_ref, latent_ref, noise_ref, emb_ref, inw_ref, qw_ref, ow_ref, resw_hbm, up_hbm,
    block3_ref, res_ref, query_ref, out_ref, ghidden_ref, kvout_ref,
    resw_ref, up3_ref, load_sems, inw_f, inw_t, turn, up_ref, block_ref,
    noisy, band, cond, part, f_inbox, f_all, f_give, f_got, f_kv, wcat, qw_t, ow_t, taps, first,
    hid, query, att, prob, gatt, gscore, gquery, ghid, bk, bk_t, bv, bv_t,
    gkv, s_inbox, s_all, s_give, s_got, s_image,
    grads, in_core, half, in_1, mid, in_2, sum_f, in_z, final,
    k_part, k_core, k_half, k_low1, k_z1, k_sum1, k_sum2, k_z2, k_low2, k_final,
    halo_sems, f_sum_sems, f_img_sems, f_pair_sems, f_row_sems,
    s_sum_sems, s_img_sems, s_pair_sems, s_row_sems,
    core_sems, s1_sems, s2_sems, z_sems,
    gz_sems, g1_sems, g2_sems, gcore_sems,
    kc_sems, kx1_sems, kz1_sems, kx2_sems, kz2_sems,
    kgx1_sems, kgz1_sems, kgx2_sems, kgz2_sems, kgc_sems,
    *, weight_scale, kv_scale,
):
    loads = [
        pltpu.make_async_copy(resw_hbm, resw_ref, load_sems.at[0]),
        pltpu.make_async_copy(up_hbm, up3_ref, load_sems.at[1]),
    ]
    for load in loads:
        load.start()
    img, row = place()
    z, x, y, core = coords(img, row)
    partner = device(z, x, y, 1 - core)
    low = lax.rem(x, 2)
    across = device(z, x + 1 - 2 * low, y, core)

    band[...] = jnp.zeros_like(band)
    signals = greet(img, row)

    def at_x(k):
        return lax.rem(x + k, 4)

    def at_y(k):
        return lax.rem(y + k, 4)

    def at_z(k):
        return lax.rem(z + k, 8)

    tokens = hidden_ref.shape[1]
    token = lax.broadcasted_iota(jnp.int32, (SLOTS, tokens), 1)
    wanted = lax.broadcasted_iota(jnp.int32, (SLOTS, tokens), 0) + slot_ref[0]
    pick_rows = (token == wanted).astype(BF16)
    cond[...] = against(hidden_ref[...], pick_rows).astype(BF16)
    product = against_first(cond[...], kvw_ref[...])
    part[0] = product[:, :CHANNELS]
    part[1] = product[:, CHANNELS:]

    index = lax.broadcasted_iota(jnp.int32, (8, 128), 0) * 128 + lax.broadcasted_iota(
        jnp.int32, (8, 128), 1
    )
    share_of = index.astype(F32) / 999.0
    beta = (0.00085**0.5 * (1.0 - share_of) + 0.012**0.5 * share_of) ** 2
    logs = jnp.where(index <= time_ref[0], jnp.log(1.0 - jnp.where(index < 1000, beta, 0.0)), 0.0)
    level = jnp.exp(jnp.sum(logs, axis=(0, 1), keepdims=True))
    keep, add = jnp.sqrt(level), jnp.sqrt(1.0 - level)
    for c in range(4):
        noisy[c] = (keep * latent_ref[c] + add * noise_ref[c]).astype(BF16).astype(F32)
    for r in range(8):
        band[2 + r, pl.ds(0, 4)] = noisy[:, r, :]

    pl.semaphore_wait(pltpu.get_barrier_semaphore(), signals)

    def halo_up():
        return remote(band.at[pl.ds(8, 2)], band.at[pl.ds(0, 2)], halo_sems, 0, (img, lax.rem(row + 1, ROWS)))

    def halo_down():
        return remote(band.at[pl.ds(2, 2)], band.at[pl.ds(10, 2)], halo_sems, 1, (img, lax.rem(row + ROWS - 1, ROWS)))

    above, below = row > 0, row < ROWS - 1
    pl.when(below)(lambda: halo_up().start())
    pl.when(above)(lambda: halo_down().start())
    f_sum = RowSum(img, row, part, f_inbox, f_sum_sems)
    f_sum.start()

    inw_f[...] = jnp.zeros_like(inw_f)
    for t in range(9):
        inw_f[pl.ds(8 * t, 4)] = inw_ref[t].astype(F32)
    inw_t[...] = inw_f[...].T.astype(BF16)
    loads[0].wait()
    for a in range(3):
        for b in range(3):
            wcat[a, :, b * CHANNELS : (b + 1) * CHANNELS] = resw_ref[3 * a + b]
    qw_t[...] = qw_ref[...].astype(F32).T.astype(BF16)
    ow_t[...] = ow_ref[...].astype(F32).T.astype(BF16)

    def source_of(which):
        return lax.fori_loop(
            0, IMGS, lambda i, s: jnp.maximum(s, jnp.where(group_ref[i] == which, i, 0)), jnp.int32(0)
        )

    other = img + 1 - 2 * core
    source, other_source = source_of(img), source_of(other)
    f_pick = Pick(img, row, f_all, f_give, f_got, f_img_sems, f_pair_sems)
    f_pick.start(f_sum.total().astype(BF16))

    pl.when(above)(lambda: halo_up().wait_recv())
    pl.when(below)(lambda: halo_down().wait_recv())

    def first_rows(j):
        fields = []
        for r in range(2):
            pieces = []
            for a in range(3):
                n = band[2 * j + r + a]
                pieces += [shifted(n, -1), n, shifted(n, 1)]
            fields.append(jnp.concatenate(pieces, axis=0))
        field = jnp.concatenate(fields, axis=1).astype(BF16)
        value = matmul(inw_t[...], field)
        lanes = pl.ds(pl.multiple_of(j * 256, 256), 256)
        first[:, lanes] = value
        v = value + emb_ref[...]
        line = row * 8 - 1 + 2 * j + lax.div(lax.broadcasted_iota(jnp.int32, v.shape, 1), 128)
        act = jnp.where((line >= 0) & (line < 64), v / (1.0 + jnp.exp(-v)), 0.0)
        act = act.astype(BF16).astype(F32)
        taps[pl.ds(0, CHANNELS), lanes] = shifted(act, -1).astype(BF16)
        taps[pl.ds(CHANNELS, CHANNELS), lanes] = act.astype(BF16)
        taps[pl.ds(2 * CHANNELS, CHANNELS), lanes] = shifted(act, 1).astype(BF16)

    each(5, first_rows, 0)

    def cells(n, more=0):
        return pl.ds(pl.multiple_of(n * 256 + more, 128), 256)

    def residual(n):
        acc = first[:, cells(n, 128)]
        for a in range(3):
            acc = acc + matmul(wcat[a], taps[:, cells(n, 128 * a)])
        hid[:, cells(n)] = acc.astype(BF16)

    each(2, residual, 0)
    f_pick.relay(other_source)
    each(4, residual, 2)

    f_kv[lax.rem(row, 2), rows16(lax.div(row, 2))] = f_pick.result(source)
    f_share = Gather(
        ROWS, row, lambda j: (img, j),
        lambda j: f_kv.at[lax.rem(j, 2), rows16(lax.div(j, 2))], f_row_sems,
    )
    f_share.start()

    loads[1].wait()

    def flatten(c):
        channels = rows16(4 * c, 64)
        turn[...] = up3_ref[channels].astype(F32)
        for r in range(8):
            up_ref[channels, r * 128 : (r + 1) * 128] = turn[:, r, :].astype(BF16)

    each(5, flatten, 0)

    def unflatten(c):
        channels = rows16(4 * c, 64)
        for r in range(8):
            turn[:, r, :] = block_ref[channels, r * 128 : (r + 1) * 128].astype(F32)
        block3_ref[channels] = turn[...].astype(BF16)

    def projections(n):
        query[:, cells(n)] = matmul(qw_ref[...], hid[:, cells(n)]).astype(BF16)
        gatt[:, cells(n)] = matmul(ow_t[...], up_ref[:, cells(n)]).astype(BF16)

    each(4, projections, 0)
    f_share.wait()
    spread(f_kv[0], bk, bk_t)
    spread(f_kv[1], bv, bv_t)

    def attend(n):
        here = cells(n)
        score = matmul(bk[...], query[:, here]) * HEAD_DIM**-0.5
        score = score.reshape(HEADS, SLOTS, 256)
        top = jnp.max(score, axis=1, keepdims=True)
        grown = jnp.exp(score - top)
        soft = grown / jnp.sum(grown, axis=1, keepdims=True)
        soft_low = soft.reshape(CHANNELS, 256).astype(BF16)
        prob[:, here] = soft_low
        gprob = matmul(bv[...], gatt[:, here]).reshape(HEADS, SLOTS, 256)
        mean = jnp.sum(soft * gprob, axis=1, keepdims=True)
        gs = (HEAD_DIM**-0.5 * soft * (gprob - mean)).reshape(CHANNELS, 256).astype(BF16)
        gscore[:, here] = gs

    def attend_more(n):
        here = cells(n)
        attended = matmul(bv_t[...], prob[:, here]).astype(BF16)
        att[:, here] = attended
        block_ref[:, here] = (
            hid[:, here].astype(F32) + matmul(ow_ref[...], attended)
        ).astype(BF16)
        gq = matmul(bk_t[...], gscore[:, here]).astype(BF16)
        gquery[:, here] = gq
        ghid[:, here] = (up_ref[:, here].astype(F32) + matmul(qw_t[...], gq)).astype(BF16)

    each(4, attend, 0)

    gkv[0] = diagonal(against(gscore[...], query[...])).astype(BF16)
    gkv[1] = diagonal(against(prob[...], gatt[...])).astype(BF16)
    row_sum = RowSum(img, row, gkv, s_inbox, s_sum_sems)
    row_sum.start()

    each(4, attend_more, 0)

    def core_copy(t):
        return remote(
            grads.at[t, rows16((1 - core) * 10, 160)], in_core.at[t], core_sems, t, partner
        )

    grads[0] = against(gquery[...], hid[...]).astype(BF16)
    core_copy(0).start()
    grads[1] = against(up_ref[...], att[...]).astype(BF16)
    core_copy(1).start()

    def tap(t):
        a, b = lax.div(t - 2, 3), lax.rem(t - 2, 3)
        field = taps[
            pl.ds(pl.multiple_of(b * CHANNELS, CHANNELS), CHANNELS),
            pl.ds(pl.multiple_of(a * 128, 128), 1024),
        ]
        grads[t] = against(ghid[...], field).astype(BF16)
        core_copy(t).start()

    def x_first(j):
        return j % 2 == 1

    def at(axis_x, k):
        return device(z, at_x(k), y, core) if axis_x else device(z, x, at_y(k), core)

    def s1_copy(j, k):
        src = half.at[j, at_x(k)] if x_first(j) else half.at[j, :, at_y(k)]
        return remote(src, in_1.at[j, k - 1], s1_sems, 3 * j + k - 1, at(x_first(j), k))

    def s2_copy(j, k):
        src = mid.at[j, at_y(k) if x_first(j) else at_x(k)]
        return remote(src, in_2.at[j, k - 1], s2_sems, 3 * j + k - 1, at(not x_first(j), k))

    def z_copy(k):
        to = at_z(k)
        return remote(
            sum_f.at[lax.rem(to, 7)], in_z.at[k - 1], z_sems, k - 1, device(to, x, y, core)
        )

    def to_owner(k, act):
        pl.when(at_z(k) < 7)(lambda: act(k))

    def from_owner(k, act):
        pl.when(lax.rem(z + 8 - k, 8) < 7)(lambda: act(k))

    def across_cores(j, begin, end):
        each(end, lambda t: core_copy(t).wait_recv(), begin)

        def add(u):
            unit = 16 * j + u
            t, i = lax.div(unit, 10), lax.rem(unit, 10)
            half[j, lax.div(u, 4), lax.rem(u, 4)] = (
                grads[t, rows16(core * 10 + i)].astype(F32) + in_core[t, rows16(i)].astype(F32)
            ).astype(BF16)

        each(min(16, TAPS * 10 - 16 * j), add, 0)
        each(4, lambda k: s1_copy(j, k).start())

    def across_first(j):
        each(4, lambda k: s1_copy(j, k).wait_recv())
        own = half[j, x] if x_first(j) else half[j, :, y]
        mid[j] = total_of(4, own, lambda k: in_1[j, k - 1]).astype(BF16)
        each(4, lambda k: s2_copy(j, k).start())

    def across_second(j):
        each(4, lambda k: s2_copy(j, k).wait_recv())
        own = mid[j, y if x_first(j) else x]
        sum_f[j] = total_of(4, own, lambda k: in_2[j, k - 1]).astype(BF16)
        pl.when(z != j)(lambda: z_copy(lax.rem(j + 8 - z, 8)).start())

    half[SLICES - 1, 3, pl.ds(2, 2)] = jnp.zeros((2, 16, CHANNELS), BF16)
    pick = Pick(img, row, s_all, s_give, s_got, s_img_sems, s_pair_sems)
    each(3, tap, 2)
    pick.start(row_sum.total().astype(BF16))
    across_cores(0, 0, 2)
    each(5, tap, 3)
    across_cores(1, 2, 4)
    each(6, tap, 5)
    across_cores(2, 4, 5)
    each(8, tap, 6)
    across_cores(3, 5, 7)
    each(9, tap, 8)
    across_cores(4, 7, 8)
    across_first(0)
    each(11, tap, 9)
    across_cores(5, 8, 10)
    across_cores(6, 10, 11)
    zi = lax.rem(z, 7)

    def kx1_copy():
        return remote(k_half.at[pl.ds((1 - low) * 7, 7)], k_low1, kx1_sems, 0, across)

    def kz1_copy(k):
        to = at_z(k)
        return remote(
            k_sum1.at[lax.rem(to, 7)], k_z1.at[k - 1], kz1_sems, k - 1, device(to, x, y, core)
        )

    def kz2_copy(k):
        to = at_z(k)
        return remote(
            k_half.at[pl.ds(14 + 2 * lax.rem(to, 7), 2)], k_z2.at[k - 1], kz2_sems, k - 1,
            device(to, x, y, core),
        )

    def kx2_copy():
        return remote(k_sum2.at[1 - low], k_low2, kx2_sems, 0, across)

    def g1_copy(j, k):
        mine = final.at[core, j, x, y]
        return remote(mine, mine, g1_sems, 3 * j + k - 1, at(not x_first(j), k))

    def g2_copy(j, k):
        mine = final.at[core, j, x] if x_first(j) else final.at[core, j, :, y]
        return remote(mine, mine, g2_sems, 3 * j + k - 1, at(x_first(j), k))

    def core_pass(j, k):
        mine = (
            final.at[core, j, lax.rem(x + 4 - k, 4)]
            if x_first(j)
            else final.at[core, j, :, lax.rem(y + 4 - k, 4)]
        )
        return remote(mine, mine, gcore_sems, 4 * j + k, partner)

    def spread_second(j):
        @pl.when(z != j)
        def _():
            gz_copy(lax.rem(z + 8 - j, 8)).wait_recv()

        each(4, lambda k: g1_copy(j, k).start())

    def spread_first(j):
        each(4, lambda k: g1_copy(j, k).wait_recv())
        each(4, lambda k: g2_copy(j, k).start())
        core_pass(j, 0).start()

    def spread_core(j):
        def go(k):
            g2_copy(j, k).wait_recv()
            core_pass(j, k).start()

        each(4, go)

    def kgz1_copy(k):
        mine = k_final.at[core, low * 7 + zi]
        return remote(mine, mine, kgz1_sems, k - 1, device(at_z(k), x, y, core))

    def kgx1_copy():
        mine = k_final.at[core, pl.ds(low * 7, 7)]
        return remote(mine, mine, kgx1_sems, 0, across)

    def kgx2_copy():
        mine = k_final.at[core, 14 + 2 * zi + low]
        return remote(mine, mine, kgx2_sems, 0, across)

    def kgz2_copy(k):
        mine = k_final.at[core, pl.ds(14 + 2 * zi, 2)]
        return remote(mine, mine, kgz2_sems, k - 1, device(at_z(k), x, y, core))

    def kgc_copy(k):
        begin, count = ((low * 7, 7), (14, 7), (21, 7), ((1 - low) * 7, 7))[k]
        mine = k_final.at[core, pl.ds(begin, count)]
        return remote(mine, mine, kgc_sems, k, partner)

    pick.relay(group_ref[other])
    across_first(1)
    s_image[lax.rem(row, 2), rows16(lax.div(row, 2))] = pick.result(group_ref[img])
    share = Gather(
        ROWS, row, lambda j: (img, j),
        lambda j: s_image.at[lax.rem(j, 2), rows16(lax.div(j, 2))], s_row_sems,
    )
    share.start()
    across_first(2)
    across_second(0)
    across_first(3)
    across_second(1)
    share.wait()
    features = cond.shape[0]
    for side in range(2):
        k_part[
            pl.ds(0, features // 16), :, side * CHANNELS : (side + 1) * CHANNELS
        ] = (
            matmul(cond[...], s_image[side]).astype(BF16).reshape(features // 16, 16, CHANNELS)
        )
    k_part[pl.ds(features // 16, 4)] = jnp.zeros((4, 16, 2 * CHANNELS), BF16)

    def kc_copy():
        return remote(k_part.at[pl.ds((1 - core) * 28, 28)], k_core, kc_sems, 0, partner)

    kc_copy().start()
    across_first(4)
    across_second(2)
    kc_copy().wait_recv()

    def add_kc(j):
        k_half[j] = (k_part[core * 28 + j].astype(F32) + k_core[j].astype(F32)).astype(BF16)

    each(28, add_kc, 14)
    each(8, lambda k: to_owner(k, lambda i: kz2_copy(i).start()))
    each(14, add_kc, 0)
    kx1_copy().start()

    across_first(5)
    across_second(3)
    kx1_copy().wait_recv()

    def add_kx1(j):
        k_sum1[j] = (k_half[low * 7 + j].astype(F32) + k_low1[j].astype(F32)).astype(BF16)

    each(7, add_kx1, 0)
    each(8, lambda k: to_owner(k, lambda i: kz1_copy(i).start()))

    across_first(6)
    across_second(4)
    across_second(5)
    across_second(6)
    @pl.when(z < 7)
    def _():
        each(8, lambda k: z_copy(k).wait_recv())
        done = total_of(8, sum_f[zi], lambda k: in_z[k - 1]) * weight_scale
        final[core, zi, x, y] = done.astype(BF16)

    def gz_copy(k):
        mine = final.at[core, zi, x, y]
        return remote(mine, mine, gz_sems, k - 1, device(at_z(k), x, y, core))

    @pl.when(z < 7)
    def _():
        each(8, lambda k: gz_copy(k).start())

    @pl.when(z < 7)
    def _():
        each(8, lambda k: kz2_copy(k).wait_recv())
        own = k_half[pl.ds(14 + 2 * zi, 2)]
        k_sum2[...] = total_of(8, own, lambda k: k_z2[k - 1]).astype(BF16)
        kx2_copy().start()

    image = jnp.concatenate([s_image[0], s_image[1]], axis=1)
    gcond = against(kvw_ref[...], image).astype(BF16)
    spot = lax.broadcasted_iota(jnp.int32, (SLOTS, tokens), 1)
    slot = lax.broadcasted_iota(jnp.int32, (SLOTS, tokens), 0) + slot_ref[0]
    ghidden_ref[...] = matmul(gcond, (spot == slot).astype(BF16)).astype(BF16)

    @pl.when(z < 7)
    def _():
        kx2_copy().wait_recv()
        done = (k_sum2[low].astype(F32) + k_low2[...].astype(F32)) * kv_scale
        k_final[core, 14 + 2 * zi + low] = done.astype(BF16)
        kgx2_copy().start()
        each(8, lambda k: kz1_copy(k).wait_recv())
        done = total_of(8, k_sum1[zi], lambda k: k_z1[k - 1]) * kv_scale
        k_final[core, low * 7 + zi] = done.astype(BF16)
        each(8, lambda k: kgz1_copy(k).start())
        kgx2_copy().wait_recv()
        each(8, lambda k: kgz2_copy(k).start())

    each(5, unflatten, 0)
    for j in range(SLICES):
        spread_second(j)
    for j in range(SLICES):
        spread_first(j)
    each(8, lambda k: from_owner(k, lambda i: kgz1_copy(i).wait_recv()))
    kgx1_copy().start()
    kgc_copy(0).start()
    for j in range(0, 4):
        spread_core(j)
    each(8, lambda k: from_owner(k, lambda i: kgz2_copy(i).wait_recv()))
    kgc_copy(1).start()
    kgc_copy(2).start()
    for j in range(4, SLICES):
        spread_core(j)
    kgx1_copy().wait_recv()
    kgc_copy(3).start()

    for j in range(SLICES):
        each(4, lambda k, j=j: core_pass(j, k).wait_recv(), 0)

    for t in range(TAPS):
        target, base = ((query_ref, 0), (out_ref, 0))[t] if t < 2 else (res_ref, (t - 2) * CHANNELS)
        for c in range(2):
            for i in range(10):
                j, rest = divmod(t * 10 + i, 16)
                target[pl.ds(base + c * 160 + i * 16, 16)] = final[c, j, rest // 4, rest % 4]
    for k in range(4):
        kgc_copy(k).wait_recv()
    for unit in range(52):
        kvout_ref[pl.ds(16 * unit, 16)] = k_final[unit // 28, unit % 28]

    pl.when(below)(lambda: halo_up().wait_send())
    pl.when(above)(lambda: halo_down().wait_send())
    for one in (f_sum, f_pick, f_share, row_sum, pick, share):
        one.finish()
    each(TAPS, lambda t: core_copy(t).wait_send(), 0)
    for j in range(SLICES):
        for copy in (s1_copy, s2_copy, g1_copy, g2_copy):
            each(4, lambda k, copy=copy, j=j: copy(j, k).wait_send())
        each(4, lambda k, j=j: core_pass(j, k).wait_send(), 0)
    each(8, lambda k: to_owner(k, lambda i: z_copy(i).wait_send()))
    each(8, lambda k: to_owner(k, lambda i: kz1_copy(i).wait_send()))
    each(8, lambda k: to_owner(k, lambda i: kz2_copy(i).wait_send()))

    @pl.when(z < 7)
    def _():
        for copy in (gz_copy, kgz1_copy, kgz2_copy):
            each(8, lambda k, copy=copy: copy(k).wait_send())
        kx2_copy().wait_send()
        kgx2_copy().wait_send()

    kc_copy().wait_send()
    kx1_copy().wait_send()
    kgx1_copy().wait_send()
    for k in range(4):
        kgc_copy(k).wait_send()


def finish_kernel(*refs):
    count = (len(refs) - 1) // 3
    sems = refs[-1]
    loads = [pltpu.make_async_copy(refs[i], refs[2 * count + i], sems.at[0, i]) for i in range(count)]
    stores = [pltpu.make_async_copy(refs[2 * count + i], refs[count + i], sems.at[1, i]) for i in range(count)]
    for load in loads:
        load.start()
    for load, store in zip(loads, stores):
        load.wait()
        store.start()
    for store in stores:
        store.wait()


def finish(arrays):
    anywhere = pl.BlockSpec(memory_space=pl.ANY)
    return pl.pallas_call(
        finish_kernel,
        out_shape=tuple(jax.ShapeDtypeStruct(a.shape, a.dtype) for a in arrays),
        in_specs=[anywhere] * len(arrays),
        out_specs=(anywhere,) * len(arrays),
        scratch_shapes=[pltpu.VMEM(a.shape, a.dtype) for a in arrays]
        + [pltpu.SemaphoreType.DMA((2, len(arrays)))],
        compiler_params=pltpu.CompilerParams(vmem_limit_bytes=62 * 2**20),
        name="finish",
    )(*arrays)


def shards(
    llm_hidden,
    slot_start,
    image_group,
    timesteps,
    latents,
    noise,
    kv_weight,
    in_weight,
    res_weight,
    query_weight,
    out_weight,
    cotangent,
):
    width, features = CHANNELS, llm_hidden.shape[1]
    frequency = jnp.exp(-math.log(10000.0) * jnp.arange(width // 2, dtype=F32) / (width // 2))
    angles = timesteps[0].astype(F32) * frequency
    emb = jnp.concatenate([jnp.cos(angles), jnp.sin(angles)])[:, None]
    vmem, smem = pl.BlockSpec(memory_space=pltpu.VMEM), pl.BlockSpec(memory_space=pltpu.SMEM)
    anywhere = pl.BlockSpec(memory_space=pl.ANY)
    dma = lambda n: pltpu.SemaphoreType.DMA((2, n))
    low = lambda *shape: pltpu.VMEM(shape, BF16)
    field, square = low(width, 1024), low(width, width)
    out = lambda *shape: jax.ShapeDtypeStruct(shape, BF16)
    block, res, query, projection, grad_hidden, grad_kv_weight = pl.pallas_call(
        functools.partial(
            kernel,
            weight_scale=(IMGS * ROWS * 1024) ** (-0.5),
            kv_scale=(IMGS * SLOTS) ** (-0.5),
        ),
        out_shape=(
            out(width, 8, 128), out(9 * width, width), out(width, width), out(width, width),
            out(features, llm_hidden.shape[0]), out(*kv_weight.shape),
        ),
        in_specs=[smem] * 3 + [vmem] * 8 + [anywhere] * 2,
        out_specs=(vmem,) * 6,
        scratch_shapes=[
            low(9, width, width), low(width, 8, 128), pltpu.SemaphoreType.DMA((2,)),
            pltpu.VMEM((72, width), F32), low(width, 72), pltpu.VMEM((64, 8, 128), F32), field, field,
            pltpu.VMEM((4, 8, 128), F32), pltpu.VMEM((12, 8, 128), F32),
            low(features, SLOTS), pltpu.VMEM((2, SLOTS, width), F32),
            pltpu.VMEM((ROWS - 1, 16, width), F32), low(IMGS // 2, 16, width),
            low(16, width), low(16, width), low(2, SLOTS, width),
            low(3, width, 3 * width), square, square,
            low(3 * width, 1280), pltpu.VMEM((width, 1280), F32),
            field, field, field, field, field, field, field, field, square, square, square, square,
            low(2, SLOTS, width), low(ROWS - 1, 16, width), low(IMGS // 2, 16, width),
            low(16, width), low(16, width), low(2, SLOTS, width),
            low(TAPS, width, width), low(TAPS, 160, width), low(SLICES, 4, 4, 16, width),
            low(SLICES, 3, 4, 16, width), low(SLICES, 4, 16, width), low(SLICES, 3, 16, width),
            low(SLICES, 16, width), low(7, 16, width), low(2, SLICES, 4, 4, 16, width),
            low(56, 16, 2 * width), low(28, 16, 2 * width), low(28, 16, 2 * width),
            low(7, 16, 2 * width), low(7, 16, 2 * width), low(7, 16, 2 * width),
            low(2, 16, 2 * width), low(7, 2, 16, 2 * width), low(16, 2 * width),
            low(2, 28, 16, 2 * width),
            dma(2), dma(7), dma(15), dma(1), dma(7),
            dma(7), dma(15), dma(1), dma(7),
            dma(TAPS), dma(3 * SLICES), dma(3 * SLICES), dma(7),
            dma(7), dma(3 * SLICES), dma(3 * SLICES), dma(4 * SLICES),
            dma(1), dma(1), dma(7), dma(1), dma(7),
            dma(1), dma(7), dma(1), dma(7), dma(4),
        ],
        compiler_params=pltpu.CompilerParams(
            collective_id=0, has_side_effects=True, vmem_limit_bytes=60 * 2**20
        ),
        name="block",
    )(
        image_group, slot_start, timesteps, llm_hidden.T, kv_weight, latents[0], noise[0], emb,
        in_weight.transpose(0, 1, 3, 2).reshape(9, 4, width), query_weight, out_weight,
        res_weight.reshape(9, width, width), cotangent[0],
    )
    query, projection, block, grad_hidden, grad_kv_weight, res = finish(
        (query, projection, block, grad_hidden, grad_kv_weight, res.reshape(3, 3, width, width))
    )
    return block[None], grad_hidden.T, grad_kv_weight, res, query, projection


def solution(mesh):
    return jax.shard_map(
        shards,
        mesh=mesh,
        in_specs=(
            P("img", "row"),
            P("img"),
            P(),
            P("img"),
            P("img", None, "row", None),
            P("img", None, "row", None),
            P("row", None),
            P(),
            P(),
            P(),
            P(),
            P("img", None, "row", None),
        ),
        out_specs=(P("img", None, "row", None), P("img", "row"), P("row", None), P(), P(), P()),
        check_vma=False,
    )
```

```python
import functools
import math

import jax
import jax.numpy as jnp
from jax import lax
from jax.experimental import pallas as pl
from jax.experimental.pallas import tpu as pltpu
from jax.sharding import PartitionSpec as P

HEAD_DIM = 64
SLOTS = 64
MESH = pl.DeviceIdType.MESH
CHANNELS = 320
HEADS = 5
IMGS, ROWS = 32, 8
TAPS = 11
SLICES = 7
F32, BF16 = jnp.float32, jnp.bfloat16


def place():
    img, row = lax.axis_index("img"), lax.axis_index("row")
    return img, row


def coords(img, row):
    z, low, core = lax.div(img, 4), lax.rem(lax.div(img, 2), 2), lax.rem(img, 2)
    return z, lax.div(row, 4) * 2 + low, lax.rem(row, 4), core


def device(z, x, y, core):
    return (z * 4 + lax.rem(x, 2) * 2 + core, lax.div(x, 2) * 4 + y)


def remote(src, dst, sems, slot, where):
    return pltpu.make_async_remote_copy(
        src_ref=src,
        dst_ref=dst,
        send_sem=sems.at[0, slot],
        recv_sem=sems.at[1, slot],
        device_id=where,
        device_id_type=MESH,
    )


def each(count, act, first=1):
    def body(k, carry):
        act(k)
        return carry

    lax.fori_loop(first, count, body, 0)


def rows16(index, count=16):
    return pl.ds(pl.multiple_of(index * 16, 16), count)


def greet(img, row):
    barrier = pltpu.get_barrier_semaphore()

    def call(where):
        pl.semaphore_signal(barrier, inc=1, device_id=where, device_id_type=MESH)

    each(ROWS, lambda k: call((img, lax.rem(row + k, ROWS))))
    each(IMGS // 2, lambda k: call((lax.rem(img + 2 * k, IMGS), row)))
    call((img + 1 - 2 * lax.rem(img, 2), row))
    call((img + 3 - 2 * lax.rem(img, 4), row))
    z, x, y, core = coords(img, row)
    other = 2 * (1 - lax.div(x, 2)) + (1 - lax.rem(x, 2))
    call(device(z, other, y, core))
    return ROWS - 1 + IMGS // 2 - 1 + 1 + 1 + 1


class RowSum:
    def __init__(self, img, row, part, inbox, sems):
        self.img, self.row, self.part, self.inbox, self.sems = img, row, part, inbox, sems

    def copy(self, k):
        r = lax.rem(self.row + k, ROWS)
        src = self.part.at[lax.rem(r, 2), rows16(lax.div(r, 2))]
        return remote(src, self.inbox.at[k - 1], self.sems, k - 1, (self.img, r))

    def start(self):
        each(ROWS, lambda k: self.copy(k).start())

    def total(self):
        own = self.part[lax.rem(self.row, 2), rows16(lax.div(self.row, 2))].astype(F32)

        def body(k, acc):
            self.copy(k).wait_recv()
            return acc + self.inbox[k - 1].astype(F32)

        return lax.fori_loop(1, ROWS, body, own)

    def finish(self):
        each(ROWS, lambda k: self.copy(k).wait_send())


class Gather:
    def __init__(self, count, me, where, target, sems):
        self.count, self.me, self.where, self.target, self.sems = count, me, where, target, sems

    def copy(self, k):
        to = lax.rem(self.me + k, self.count)
        return remote(
            self.target(self.me), self.target(self.me), self.sems, k - 1, self.where(to)
        )

    def start(self):
        each(self.count, lambda k: self.copy(k).start())

    def wait(self):
        each(self.count, lambda k: self.copy(k).wait_recv())

    def finish(self):
        each(self.count, lambda k: self.copy(k).wait_send())


class Pick:
    def __init__(self, img, row, everyone, give, got, sems, pair_sems):
        self.img, self.row, self.core = img, row, lax.rem(img, 2)
        self.everyone, self.give, self.got, self.pair_sems = everyone, give, got, pair_sems
        self.gather = Gather(
            IMGS // 2, lax.div(img, 2), lambda j: (2 * j + self.core, row),
            lambda j: everyone.at[j], sems,
        )

    def start(self, own):
        self.everyone[lax.div(self.img, 2)] = own
        self.gather.start()

    def pair(self):
        where = (self.img + 1 - 2 * self.core, self.row)
        return remote(self.give, self.got, self.pair_sems, 0, where)

    def relay(self, wanted):
        self.gather.wait()
        self.give[...] = self.everyone[lax.div(wanted, 2)]
        self.pair().start()

    def result(self, source):
        self.pair().wait_recv()
        own = self.everyone[lax.div(source, 2)].astype(F32)
        return jnp.where(lax.rem(source, 2) == self.core, own, self.got[...].astype(F32)).astype(BF16)

    def finish(self):
        self.gather.finish()
        self.pair().wait_send()


class PickFour(Pick):
    def relay(self, wanted):
        self.gather.wait()
        for m in range(4):
            self.give[m] = self.everyone[lax.div(wanted(m), 2)]
        self.pair().start()

    def result(self, wanted, put):
        self.pair().wait_recv()
        for m in range(4):
            own = self.give[m].astype(F32)
            put(m, jnp.where(lax.rem(wanted(m), 2) == self.core, own, self.got[m].astype(F32)).astype(BF16))


def total_of(count, base, piece):
    return lax.fori_loop(1, count, lambda k, acc: acc + piece(k).astype(F32), base.astype(F32))


def matmul(left, right):
    return jnp.dot(left, right, preferred_element_type=F32)


def against(left, right):
    return lax.dot_general(left, right, (((1,), (1,)), ((), ())), preferred_element_type=F32)


def against_first(left, right):
    return lax.dot_general(left, right, (((0,), (0,)), ((), ())), preferred_element_type=F32)


def shifted(field, step):
    lane = lax.broadcasted_iota(jnp.int32, (field.shape[0], 128), 1)
    edge = 127 if step > 0 else 0
    parts = []
    for start in range(0, field.shape[1], 128):
        turned = pltpu.roll(field[:, start : start + 128], (-step) % 128, 1)
        parts.append(jnp.where(lane == edge, 0.0, turned))
    return parts[0] if len(parts) == 1 else jnp.concatenate(parts, axis=1)


def spread(rows, target, flip):
    lane = lax.div(lax.broadcasted_iota(jnp.int32, rows.shape, 1), HEAD_DIM)
    wide = rows.astype(F32)
    full = jnp.concatenate([jnp.where(lane == h, wide, 0.0) for h in range(HEADS)], axis=0)
    target[...] = full.astype(BF16)
    flip[...] = full.T.astype(BF16)


def diagonal(full):
    lane = lax.div(lax.broadcasted_iota(jnp.int32, (SLOTS, CHANNELS), 1), HEAD_DIM)
    total = jnp.zeros((SLOTS, CHANNELS), F32)
    for h in range(HEADS):
        total = jnp.where(lane == h, full[h * SLOTS : (h + 1) * SLOTS], total)
    return total


def kernel(
    group_ref, slot_ref, time_ref,
    hidden_ref, kvw_ref, latent_ref, noise_ref, emb_ref, inw_ref, qw_ref, ow_ref, resw_hbm, up_hbm,
    block3_ref, res_ref, query_ref, out_ref, ghidden_ref, kvout_ref,
    resw_ref, up3_ref, load_sems, inw_f, inw_t, turn, up_ref, block_ref,
    noisy, band, cond, part, f_inbox, f_all, f_give, f_got, f_kv, wcat, qw_t, ow_t, taps, first,
    hid, query, att, prob, gatt, gscore, gquery, ghid, bk, bk_t, bv, bv_t,
    gkv, s_inbox, s_all, s_give, s_got, s_image,
    grads, in_core, half, in_1, mid, in_2, sum_f, in_z, final,
    quarters, four_cond, k_quarter, k_z, k_final,
    halo_sems, f_sum_sems, f_img_sems, f_pair_sems, f_row_sems,
    s_sum_sems, s_img_sems, s_pair_sems, s_row_sems,
    core_sems, s1_sems, s2_sems, z_sems,
    gz_sems, g1_sems, g2_sems, gcore_sems,
    q_sems, kz_sems,
    kgz1_sems, kgx1_sems, kgx2_sems, kgz2_sems, kgc_sems,
    *, weight_scale, kv_scale,
):
    loads = [
        pltpu.make_async_copy(resw_hbm, resw_ref, load_sems.at[0]),
        pltpu.make_async_copy(up_hbm, up3_ref, load_sems.at[1]),
    ]
    for load in loads:
        load.start()
    img, row = place()
    z, x, y, core = coords(img, row)
    partner = device(z, x, y, 1 - core)
    low = lax.rem(x, 2)
    across = device(z, x + 1 - 2 * low, y, core)

    band[...] = jnp.zeros_like(band)
    signals = greet(img, row)

    def at_x(k):
        return lax.rem(x + k, 4)

    def at_y(k):
        return lax.rem(y + k, 4)

    def at_z(k):
        return lax.rem(z + k, 8)

    tokens = hidden_ref.shape[1]
    token = lax.broadcasted_iota(jnp.int32, (SLOTS, tokens), 1)
    wanted = lax.broadcasted_iota(jnp.int32, (SLOTS, tokens), 0) + slot_ref[0]
    pick_rows = (token == wanted).astype(BF16)
    cond[...] = against(hidden_ref[...], pick_rows).astype(BF16)
    units = cond[...].reshape(cond.shape[0] // 16, 16, SLOTS)
    for q in range(4):
        count = min(14, units.shape[0] - 14 * q)
        quarters[q, pl.ds(0, count)] = units[14 * q : 14 * q + count]
    quarters[3, pl.ds(10, 4)] = jnp.zeros((4, 16, SLOTS), BF16)
    member = lax.rem(img, 4)
    four_cond[member] = quarters[2 * core + low]
    product = against_first(cond[...], kvw_ref[...])
    part[0] = product[:, :CHANNELS]
    part[1] = product[:, CHANNELS:]

    index = lax.broadcasted_iota(jnp.int32, (8, 128), 0) * 128 + lax.broadcasted_iota(
        jnp.int32, (8, 128), 1
    )
    share_of = index.astype(F32) / 999.0
    beta = (0.00085**0.5 * (1.0 - share_of) + 0.012**0.5 * share_of) ** 2
    logs = jnp.where(index <= time_ref[0], jnp.log(1.0 - jnp.where(index < 1000, beta, 0.0)), 0.0)
    level = jnp.exp(jnp.sum(logs, axis=(0, 1), keepdims=True))
    keep, add = jnp.sqrt(level), jnp.sqrt(1.0 - level)
    for c in range(4):
        noisy[c] = (keep * latent_ref[c] + add * noise_ref[c]).astype(BF16).astype(F32)
    for r in range(8):
        band[2 + r, pl.ds(0, 4)] = noisy[:, r, :]

    pl.semaphore_wait(pltpu.get_barrier_semaphore(), signals)

    def halo_up():
        return remote(band.at[pl.ds(8, 2)], band.at[pl.ds(0, 2)], halo_sems, 0, (img, lax.rem(row + 1, ROWS)))

    def halo_down():
        return remote(band.at[pl.ds(2, 2)], band.at[pl.ds(10, 2)], halo_sems, 1, (img, lax.rem(row + ROWS - 1, ROWS)))

    above, below = row > 0, row < ROWS - 1
    pl.when(below)(lambda: halo_up().start())
    pl.when(above)(lambda: halo_down().start())
    f_sum = RowSum(img, row, part, f_inbox, f_sum_sems)
    f_sum.start()

    def quarter_copy(k):
        to = lax.rem(member + k, 4)
        return remote(
            quarters.at[2 * lax.rem(to, 2) + lax.div(to, 2)], four_cond.at[member], q_sems, k - 1,
            (img - member + to, row),
        )

    each(4, lambda k: quarter_copy(k).start())

    inw_f[...] = jnp.zeros_like(inw_f)
    for t in range(9):
        inw_f[pl.ds(8 * t, 4)] = inw_ref[t].astype(F32)
    inw_t[...] = inw_f[...].T.astype(BF16)
    loads[0].wait()
    for a in range(3):
        for b in range(3):
            wcat[a, :, b * CHANNELS : (b + 1) * CHANNELS] = resw_ref[3 * a + b]
    qw_t[...] = qw_ref[...].astype(F32).T.astype(BF16)
    ow_t[...] = ow_ref[...].astype(F32).T.astype(BF16)

    def source_of(which):
        return lax.fori_loop(
            0, IMGS, lambda i, s: jnp.maximum(s, jnp.where(group_ref[i] == which, i, 0)), jnp.int32(0)
        )

    other = img + 1 - 2 * core
    source, other_source = source_of(img), source_of(other)
    f_pick = Pick(img, row, f_all, f_give, f_got, f_img_sems, f_pair_sems)
    f_pick.start(f_sum.total().astype(BF16))

    pl.when(above)(lambda: halo_up().wait_recv())
    pl.when(below)(lambda: halo_down().wait_recv())

    def first_rows(j):
        fields = []
        for r in range(2):
            pieces = []
            for a in range(3):
                n = band[2 * j + r + a]
                pieces += [shifted(n, -1), n, shifted(n, 1)]
            fields.append(jnp.concatenate(pieces, axis=0))
        field = jnp.concatenate(fields, axis=1).astype(BF16)
        value = matmul(inw_t[...], field)
        lanes = pl.ds(pl.multiple_of(j * 256, 256), 256)
        first[:, lanes] = value
        v = value + emb_ref[...]
        line = row * 8 - 1 + 2 * j + lax.div(lax.broadcasted_iota(jnp.int32, v.shape, 1), 128)
        act = jnp.where((line >= 0) & (line < 64), v / (1.0 + jnp.exp(-v)), 0.0)
        act = act.astype(BF16).astype(F32)
        taps[pl.ds(0, CHANNELS), lanes] = shifted(act, -1).astype(BF16)
        taps[pl.ds(CHANNELS, CHANNELS), lanes] = act.astype(BF16)
        taps[pl.ds(2 * CHANNELS, CHANNELS), lanes] = shifted(act, 1).astype(BF16)

    each(5, first_rows, 0)

    def cells(n, more=0):
        return pl.ds(pl.multiple_of(n * 256 + more, 128), 256)

    def residual(n):
        acc = first[:, cells(n, 128)]
        for a in range(3):
            acc = acc + matmul(wcat[a], taps[:, cells(n, 128 * a)])
        hid[:, cells(n)] = acc.astype(BF16)

    each(2, residual, 0)
    f_pick.relay(other_source)
    each(4, residual, 2)

    f_kv[lax.rem(row, 2), rows16(lax.div(row, 2))] = f_pick.result(source)
    f_share = Gather(
        ROWS, row, lambda j: (img, j),
        lambda j: f_kv.at[lax.rem(j, 2), rows16(lax.div(j, 2))], f_row_sems,
    )
    f_share.start()

    loads[1].wait()

    def flatten(c):
        channels = rows16(4 * c, 64)
        turn[...] = up3_ref[channels].astype(F32)
        for r in range(8):
            up_ref[channels, r * 128 : (r + 1) * 128] = turn[:, r, :].astype(BF16)

    each(5, flatten, 0)

    def unflatten(c):
        channels = rows16(4 * c, 64)
        for r in range(8):
            turn[:, r, :] = block_ref[channels, r * 128 : (r + 1) * 128].astype(F32)
        block3_ref[channels] = turn[...].astype(BF16)

    def projections(n):
        query[:, cells(n)] = matmul(qw_ref[...], hid[:, cells(n)]).astype(BF16)
        gatt[:, cells(n)] = matmul(ow_t[...], up_ref[:, cells(n)]).astype(BF16)

    each(4, projections, 0)
    f_share.wait()
    spread(f_kv[0], bk, bk_t)
    spread(f_kv[1], bv, bv_t)

    def attend(n):
        here = cells(n)
        score = matmul(bk[...], query[:, here]) * HEAD_DIM**-0.5
        score = score.reshape(HEADS, SLOTS, 256)
        top = jnp.max(score, axis=1, keepdims=True)
        grown = jnp.exp(score - top)
        soft = grown / jnp.sum(grown, axis=1, keepdims=True)
        soft_low = soft.reshape(CHANNELS, 256).astype(BF16)
        prob[:, here] = soft_low
        gprob = matmul(bv[...], gatt[:, here]).reshape(HEADS, SLOTS, 256)
        mean = jnp.sum(soft * gprob, axis=1, keepdims=True)
        gs = (HEAD_DIM**-0.5 * soft * (gprob - mean)).reshape(CHANNELS, 256).astype(BF16)
        gscore[:, here] = gs

    def attend_more(n):
        here = cells(n)
        attended = matmul(bv_t[...], prob[:, here]).astype(BF16)
        att[:, here] = attended
        block_ref[:, here] = (
            hid[:, here].astype(F32) + matmul(ow_ref[...], attended)
        ).astype(BF16)
        gq = matmul(bk_t[...], gscore[:, here]).astype(BF16)
        gquery[:, here] = gq
        ghid[:, here] = (up_ref[:, here].astype(F32) + matmul(qw_t[...], gq)).astype(BF16)

    each(4, attend, 0)

    gkv[0] = diagonal(against(gscore[...], query[...])).astype(BF16)
    gkv[1] = diagonal(against(prob[...], gatt[...])).astype(BF16)
    row_sum = RowSum(img, row, gkv, s_inbox, s_sum_sems)
    row_sum.start()

    each(4, attend_more, 0)

    def core_copy(t):
        return remote(
            grads.at[t, rows16((1 - core) * 10, 160)], in_core.at[t], core_sems, t, partner
        )

    grads[0] = against(gquery[...], hid[...]).astype(BF16)
    core_copy(0).start()
    grads[1] = against(up_ref[...], att[...]).astype(BF16)
    core_copy(1).start()

    def tap(t):
        a, b = lax.div(t - 2, 3), lax.rem(t - 2, 3)
        field = taps[
            pl.ds(pl.multiple_of(b * CHANNELS, CHANNELS), CHANNELS),
            pl.ds(pl.multiple_of(a * 128, 128), 1024),
        ]
        grads[t] = against(ghid[...], field).astype(BF16)
        core_copy(t).start()

    def x_first(j):
        return j % 2 == 1

    def at(axis_x, k):
        return device(z, at_x(k), y, core) if axis_x else device(z, x, at_y(k), core)

    def s1_copy(j, k):
        src = half.at[j, at_x(k)] if x_first(j) else half.at[j, :, at_y(k)]
        return remote(src, in_1.at[j, k - 1], s1_sems, 3 * j + k - 1, at(x_first(j), k))

    def s2_copy(j, k):
        src = mid.at[j, at_y(k) if x_first(j) else at_x(k)]
        return remote(src, in_2.at[j, k - 1], s2_sems, 3 * j + k - 1, at(not x_first(j), k))

    def z_copy(k):
        to = at_z(k)
        return remote(
            sum_f.at[lax.rem(to, 7)], in_z.at[k - 1], z_sems, k - 1, device(to, x, y, core)
        )

    def to_owner(k, act):
        pl.when(at_z(k) < 7)(lambda: act(k))

    def from_owner(k, act):
        pl.when(lax.rem(z + 8 - k, 8) < 7)(lambda: act(k))

    def across_cores(j, begin, end):
        each(end, lambda t: core_copy(t).wait_recv(), begin)

        def add(u):
            unit = 16 * j + u
            t, i = lax.div(unit, 10), lax.rem(unit, 10)
            half[j, lax.div(u, 4), lax.rem(u, 4)] = (
                grads[t, rows16(core * 10 + i)].astype(F32) + in_core[t, rows16(i)].astype(F32)
            ).astype(BF16)

        each(min(16, TAPS * 10 - 16 * j), add, 0)
        each(4, lambda k: s1_copy(j, k).start())

    def across_first(j):
        each(4, lambda k: s1_copy(j, k).wait_recv())
        own = half[j, x] if x_first(j) else half[j, :, y]
        mid[j] = total_of(4, own, lambda k: in_1[j, k - 1]).astype(BF16)
        each(4, lambda k: s2_copy(j, k).start())

    def across_second(j):
        each(4, lambda k: s2_copy(j, k).wait_recv())
        own = mid[j, y if x_first(j) else x]
        sum_f[j] = total_of(4, own, lambda k: in_2[j, k - 1]).astype(BF16)
        pl.when(z != j)(lambda: z_copy(lax.rem(j + 8 - z, 8)).start())

    half[SLICES - 1, 3, pl.ds(2, 2)] = jnp.zeros((2, 16, CHANNELS), BF16)
    pick = PickFour(img, row, s_all, s_give, s_got, s_img_sems, s_pair_sems)
    each(3, tap, 2)
    pick.start(row_sum.total().astype(BF16))
    across_cores(0, 0, 2)
    each(5, tap, 3)
    across_cores(1, 2, 4)
    each(6, tap, 5)
    across_cores(2, 4, 5)
    each(8, tap, 6)
    across_cores(3, 5, 7)
    each(9, tap, 8)
    across_cores(4, 7, 8)
    across_first(0)
    each(11, tap, 9)
    across_cores(5, 8, 10)
    across_cores(6, 10, 11)
    zi = lax.rem(z, 7)

    def kz_copy(k):
        to = at_z(k)
        return remote(
            k_quarter.at[:, lax.rem(to, 7)], k_z.at[k - 1], kz_sems, k - 1, device(to, x, y, core)
        )

    def g1_copy(j, k):
        mine = final.at[core, j, x, y]
        return remote(mine, mine, g1_sems, 3 * j + k - 1, at(not x_first(j), k))

    def g2_copy(j, k):
        mine = final.at[core, j, x] if x_first(j) else final.at[core, j, :, y]
        return remote(mine, mine, g2_sems, 3 * j + k - 1, at(x_first(j), k))

    def core_pass(j, k):
        mine = (
            final.at[core, j, lax.rem(x + 4 - k, 4)]
            if x_first(j)
            else final.at[core, j, :, lax.rem(y + 4 - k, 4)]
        )
        return remote(mine, mine, gcore_sems, 4 * j + k, partner)

    def spread_second(j):
        @pl.when(z != j)
        def _():
            gz_copy(lax.rem(z + 8 - j, 8)).wait_recv()

        each(4, lambda k: g1_copy(j, k).start())

    def spread_first(j):
        each(4, lambda k: g1_copy(j, k).wait_recv())
        each(4, lambda k: g2_copy(j, k).start())
        core_pass(j, 0).start()

    def spread_core(j):
        def go(k):
            g2_copy(j, k).wait_recv()
            core_pass(j, k).start()

        each(4, go)

    def kgz1_copy(k):
        mine = k_final.at[core, low, 0, zi]
        return remote(mine, mine, kgz1_sems, k - 1, device(at_z(k), x, y, core))

    def kgx1_copy():
        mine = k_final.at[core, low, 0]
        return remote(mine, mine, kgx1_sems, 0, across)

    def kgx2_copy():
        mine = k_final.at[core, low, 1, zi]
        return remote(mine, mine, kgx2_sems, 0, across)

    def kgz2_copy(k):
        mine = k_final.at[core, :, 1, zi]
        return remote(mine, mine, kgz2_sems, k - 1, device(at_z(k), x, y, core))

    def kgc_copy(k):
        part_x, turn_of = ((low, 0), (0, 1), (1, 1), (1 - low, 0))[k]
        mine = k_final.at[core, part_x, turn_of]
        return remote(mine, mine, kgc_sems, k, partner)


    def wanted(m):
        return group_ref[4 * z + m]

    pick.relay(wanted)
    across_first(1)

    def put(m, value):
        s_image[m, lax.rem(row, 2), rows16(lax.div(row, 2))] = value

    pick.result(wanted, put)
    share = Gather(
        ROWS, row, lambda j: (img, j),
        lambda j: s_image.at[:, lax.rem(j, 2), rows16(lax.div(j, 2))], s_row_sems,
    )
    share.start()
    across_first(2)
    across_second(0)
    across_first(3)
    across_second(1)
    share.wait()
    each(4, lambda k: quarter_copy(k).wait_recv())
    for side in range(2):
        total = jnp.zeros((224, CHANNELS), F32)
        for m in range(4):
            total = total + matmul(four_cond[m].reshape(224, SLOTS), s_image[m, side])
        k_quarter[:, :, :, side * CHANNELS : (side + 1) * CHANNELS] = total.astype(BF16).reshape(
            2, 7, 16, CHANNELS
        )
    each(8, lambda k: to_owner(k, lambda i: kz_copy(i).start()))
    across_first(4)
    across_second(2)
    across_first(5)
    across_second(3)
    across_first(6)
    across_second(4)
    across_second(5)
    across_second(6)
    @pl.when(z < 7)
    def _():
        each(8, lambda k: z_copy(k).wait_recv())
        done = total_of(8, sum_f[zi], lambda k: in_z[k - 1]) * weight_scale
        final[core, zi, x, y] = done.astype(BF16)

    def gz_copy(k):
        mine = final.at[core, zi, x, y]
        return remote(mine, mine, gz_sems, k - 1, device(at_z(k), x, y, core))

    @pl.when(z < 7)
    def _():
        each(8, lambda k: gz_copy(k).start())

    @pl.when(z < 7)
    def _():
        each(8, lambda k: kz_copy(k).wait_recv())
        done = (total_of(8, k_quarter[:, zi], lambda k: k_z[k - 1]) * kv_scale).astype(BF16)
        k_final[core, low, 0, zi] = done[0]
        k_final[core, low, 1, zi] = done[1]
        kgx2_copy().start()
        each(8, lambda k: kgz1_copy(k).start())

    image = jnp.concatenate([s_image[member, 0], s_image[member, 1]], axis=1)
    gcond = against(kvw_ref[...], image).astype(BF16)
    spot = lax.broadcasted_iota(jnp.int32, (SLOTS, tokens), 1)
    slot = lax.broadcasted_iota(jnp.int32, (SLOTS, tokens), 0) + slot_ref[0]
    ghidden_ref[...] = matmul(gcond, (spot == slot).astype(BF16)).astype(BF16)

    @pl.when(z < 7)
    def _():
        kgx2_copy().wait_recv()
        each(8, lambda k: kgz2_copy(k).start())

    each(5, unflatten, 0)
    for j in range(SLICES):
        spread_second(j)
    for j in range(SLICES):
        spread_first(j)
    each(8, lambda k: from_owner(k, lambda i: kgz1_copy(i).wait_recv()))
    kgx1_copy().start()
    kgc_copy(0).start()
    for j in range(0, 4):
        spread_core(j)
    each(8, lambda k: from_owner(k, lambda i: kgz2_copy(i).wait_recv()))
    kgc_copy(1).start()
    kgc_copy(2).start()
    for j in range(4, SLICES):
        spread_core(j)
    kgx1_copy().wait_recv()
    kgc_copy(3).start()

    for j in range(SLICES):
        each(4, lambda k, j=j: core_pass(j, k).wait_recv(), 0)

    for t in range(TAPS):
        target, base = ((query_ref, 0), (out_ref, 0))[t] if t < 2 else (res_ref, (t - 2) * CHANNELS)
        for c in range(2):
            for i in range(10):
                j, rest = divmod(t * 10 + i, 16)
                target[pl.ds(base + c * 160 + i * 16, 16)] = final[c, j, rest // 4, rest % 4]
    for k in range(4):
        kgc_copy(k).wait_recv()
    for unit in range(52):
        q, rest = divmod(unit, 14)
        kvout_ref[pl.ds(16 * unit, 16)] = k_final[q // 2, q % 2, rest // 7, rest % 7]

    pl.when(below)(lambda: halo_up().wait_send())
    pl.when(above)(lambda: halo_down().wait_send())
    for one in (f_sum, f_pick, f_share, row_sum, pick, share):
        one.finish()
    each(TAPS, lambda t: core_copy(t).wait_send(), 0)
    for j in range(SLICES):
        for copy in (s1_copy, s2_copy, g1_copy, g2_copy):
            each(4, lambda k, copy=copy, j=j: copy(j, k).wait_send())
        each(4, lambda k, j=j: core_pass(j, k).wait_send(), 0)
    each(8, lambda k: to_owner(k, lambda i: z_copy(i).wait_send()))
    each(8, lambda k: to_owner(k, lambda i: kz_copy(i).wait_send()))
    each(4, lambda k: quarter_copy(k).wait_send())

    @pl.when(z < 7)
    def _():
        for copy in (gz_copy, kgz1_copy, kgz2_copy):
            each(8, lambda k, copy=copy: copy(k).wait_send())
        kgx2_copy().wait_send()

    kgx1_copy().wait_send()
    for k in range(4):
        kgc_copy(k).wait_send()


def finish_kernel(*refs):
    count = (len(refs) - 1) // 3
    sems = refs[-1]
    loads = [pltpu.make_async_copy(refs[i], refs[2 * count + i], sems.at[0, i]) for i in range(count)]
    stores = [pltpu.make_async_copy(refs[2 * count + i], refs[count + i], sems.at[1, i]) for i in range(count)]
    for load in loads:
        load.start()
    for load, store in zip(loads, stores):
        load.wait()
        store.start()
    for store in stores:
        store.wait()


def finish(arrays):
    anywhere = pl.BlockSpec(memory_space=pl.ANY)
    return pl.pallas_call(
        finish_kernel,
        out_shape=tuple(jax.ShapeDtypeStruct(a.shape, a.dtype) for a in arrays),
        in_specs=[anywhere] * len(arrays),
        out_specs=(anywhere,) * len(arrays),
        scratch_shapes=[pltpu.VMEM(a.shape, a.dtype) for a in arrays]
        + [pltpu.SemaphoreType.DMA((2, len(arrays)))],
        compiler_params=pltpu.CompilerParams(vmem_limit_bytes=62 * 2**20),
        name="finish",
    )(*arrays)


def shards(
    llm_hidden,
    slot_start,
    image_group,
    timesteps,
    latents,
    noise,
    kv_weight,
    in_weight,
    res_weight,
    query_weight,
    out_weight,
    cotangent,
):
    width, features = CHANNELS, llm_hidden.shape[1]
    frequency = jnp.exp(-math.log(10000.0) * jnp.arange(width // 2, dtype=F32) / (width // 2))
    angles = timesteps[0].astype(F32) * frequency
    emb = jnp.concatenate([jnp.cos(angles), jnp.sin(angles)])[:, None]
    vmem, smem = pl.BlockSpec(memory_space=pltpu.VMEM), pl.BlockSpec(memory_space=pltpu.SMEM)
    anywhere = pl.BlockSpec(memory_space=pl.ANY)
    dma = lambda n: pltpu.SemaphoreType.DMA((2, n))
    low = lambda *shape: pltpu.VMEM(shape, BF16)
    field, square = low(width, 1024), low(width, width)
    out = lambda *shape: jax.ShapeDtypeStruct(shape, BF16)
    block, res, query, projection, grad_hidden, grad_kv_weight = pl.pallas_call(
        functools.partial(
            kernel,
            weight_scale=(IMGS * ROWS * 1024) ** (-0.5),
            kv_scale=(IMGS * SLOTS) ** (-0.5),
        ),
        out_shape=(
            out(width, 8, 128), out(9 * width, width), out(width, width), out(width, width),
            out(features, llm_hidden.shape[0]), out(*kv_weight.shape),
        ),
        in_specs=[smem] * 3 + [vmem] * 8 + [anywhere] * 2,
        out_specs=(vmem,) * 6,
        scratch_shapes=[
            low(9, width, width), low(width, 8, 128), pltpu.SemaphoreType.DMA((2,)),
            pltpu.VMEM((72, width), F32), low(width, 72), pltpu.VMEM((64, 8, 128), F32), field, field,
            pltpu.VMEM((4, 8, 128), F32), pltpu.VMEM((12, 8, 128), F32),
            low(features, SLOTS), pltpu.VMEM((2, SLOTS, width), F32),
            pltpu.VMEM((ROWS - 1, 16, width), F32), low(IMGS // 2, 16, width),
            low(16, width), low(16, width), low(2, SLOTS, width),
            low(3, width, 3 * width), square, square,
            low(3 * width, 1280), pltpu.VMEM((width, 1280), F32),
            field, field, field, field, field, field, field, field, square, square, square, square,
            low(2, SLOTS, width), low(ROWS - 1, 16, width), low(IMGS // 2, 16, width),
            low(4, 16, width), low(4, 16, width), low(4, 2, SLOTS, width),
            low(TAPS, width, width), low(TAPS, 160, width), low(SLICES, 4, 4, 16, width),
            low(SLICES, 3, 4, 16, width), low(SLICES, 4, 16, width), low(SLICES, 3, 16, width),
            low(SLICES, 16, width), low(7, 16, width), low(2, SLICES, 4, 4, 16, width),
            low(4, 14, 16, SLOTS), low(4, 14, 16, SLOTS), low(2, 7, 16, 2 * width),
            low(7, 2, 16, 2 * width), low(2, 2, 2, 7, 16, 2 * width),
            dma(2), dma(7), dma(15), dma(1), dma(7),
            dma(7), dma(15), dma(1), dma(7),
            dma(TAPS), dma(3 * SLICES), dma(3 * SLICES), dma(7),
            dma(7), dma(3 * SLICES), dma(3 * SLICES), dma(4 * SLICES),
            dma(3), dma(7),
            dma(7), dma(1), dma(1), dma(7), dma(4),
        ],
        compiler_params=pltpu.CompilerParams(
            collective_id=0, has_side_effects=True, vmem_limit_bytes=60 * 2**20
        ),
        name="block",
    )(
        image_group, slot_start, timesteps, llm_hidden.T, kv_weight, latents[0], noise[0], emb,
        in_weight.transpose(0, 1, 3, 2).reshape(9, 4, width), query_weight, out_weight,
        res_weight.reshape(9, width, width), cotangent[0],
    )
    query, projection, block, grad_hidden, grad_kv_weight, res = finish(
        (query, projection, block, grad_hidden, grad_kv_weight, res.reshape(3, 3, width, width))
    )
    return block[None], grad_hidden.T, grad_kv_weight, res, query, projection


def solution(mesh):
    return jax.shard_map(
        shards,
        mesh=mesh,
        in_specs=(
            P("img", "row"),
            P("img"),
            P(),
            P("img"),
            P("img", None, "row", None),
            P("img", None, "row", None),
            P("row", None),
            P(),
            P(),
            P(),
            P(),
            P("img", None, "row", None),
        ),
        out_specs=(P("img", None, "row", None), P("img", "row"), P("row", None), P(), P(), P()),
        check_vma=False,
    )
```

```python
import functools
import math

import jax
import jax.numpy as jnp
from jax import lax
from jax.experimental import pallas as pl
from jax.experimental.pallas import tpu as pltpu
from jax.sharding import PartitionSpec as P

HEAD_DIM = 64
SLOTS = 64
MESH = pl.DeviceIdType.MESH
CHANNELS = 320
HEADS = 5
IMGS, ROWS = 32, 8
TAPS = 11
SLICES = 7
F32, BF16 = jnp.float32, jnp.bfloat16


def place():
    img, row = lax.axis_index("img"), lax.axis_index("row")
    return img, row


def coords(img, row):
    z, low, core = lax.div(img, 4), lax.rem(lax.div(img, 2), 2), lax.rem(img, 2)
    return z, lax.div(row, 4) * 2 + low, lax.rem(row, 4), core


def device(z, x, y, core):
    return (z * 4 + lax.rem(x, 2) * 2 + core, lax.div(x, 2) * 4 + y)


def remote(src, dst, sems, slot, where):
    return pltpu.make_async_remote_copy(
        src_ref=src,
        dst_ref=dst,
        send_sem=sems.at[0, slot],
        recv_sem=sems.at[1, slot],
        device_id=where,
        device_id_type=MESH,
    )


def each(count, act, first=1):
    def body(k, carry):
        act(k)
        return carry

    lax.fori_loop(first, count, body, 0)


def rows16(index, count=16):
    return pl.ds(pl.multiple_of(index * 16, 16), count)


def greet(img, row):
    barrier = pltpu.get_barrier_semaphore()

    def call(where):
        pl.semaphore_signal(barrier, inc=1, device_id=where, device_id_type=MESH)

    each(ROWS, lambda k: call((img, lax.rem(row + k, ROWS))))
    each(IMGS // 2, lambda k: call((lax.rem(img + 2 * k, IMGS), row)))
    call((img + 1 - 2 * lax.rem(img, 2), row))
    call((img + 3 - 2 * lax.rem(img, 4), row))
    each(ROWS, lambda k: call((img + 1 - 2 * lax.rem(img, 2), lax.rem(row + k, ROWS))))
    z, x, y, core = coords(img, row)
    other = 2 * (1 - lax.div(x, 2)) + (1 - lax.rem(x, 2))
    call(device(z, other, y, core))
    return ROWS - 1 + IMGS // 2 - 1 + 1 + 1 + 1 + ROWS - 1


class RowSum:
    def __init__(self, img, row, part, inbox, sems):
        self.img, self.row, self.part, self.inbox, self.sems = img, row, part, inbox, sems

    def copy(self, k):
        r = lax.rem(self.row + k, ROWS)
        src = self.part.at[lax.rem(r, 2), rows16(lax.div(r, 2))]
        return remote(src, self.inbox.at[k - 1], self.sems, k - 1, (self.img, r))

    def start(self):
        each(ROWS, lambda k: self.copy(k).start())

    def total(self):
        own = self.part[lax.rem(self.row, 2), rows16(lax.div(self.row, 2))].astype(F32)

        def body(k, acc):
            self.copy(k).wait_recv()
            return acc + self.inbox[k - 1].astype(F32)

        return lax.fori_loop(1, ROWS, body, own)

    def finish(self):
        each(ROWS, lambda k: self.copy(k).wait_send())


class Gather:
    def __init__(self, count, me, where, target, sems):
        self.count, self.me, self.where, self.target, self.sems = count, me, where, target, sems

    def copy(self, k):
        to = lax.rem(self.me + k, self.count)
        return remote(
            self.target(self.me), self.target(self.me), self.sems, k - 1, self.where(to)
        )

    def start(self):
        each(self.count, lambda k: self.copy(k).start())

    def wait(self):
        each(self.count, lambda k: self.copy(k).wait_recv())

    def finish(self):
        each(self.count, lambda k: self.copy(k).wait_send())


class Pick:
    def __init__(self, img, row, everyone, give, got, sems, pair_sems):
        self.img, self.row, self.core = img, row, lax.rem(img, 2)
        self.everyone, self.give, self.got, self.pair_sems = everyone, give, got, pair_sems
        self.gather = Gather(
            IMGS // 2, lax.div(img, 2), lambda j: (2 * j + self.core, row),
            lambda j: everyone.at[j], sems,
        )

    def start(self, own):
        self.everyone[lax.div(self.img, 2)] = own
        self.gather.start()

    def pair(self):
        where = (self.img + 1 - 2 * self.core, self.row)
        return remote(self.give, self.got, self.pair_sems, 0, where)

    def relay(self, wanted):
        self.gather.wait()
        self.give[...] = self.everyone[lax.div(wanted, 2)]
        self.pair().start()

    def result(self, source):
        self.pair().wait_recv()
        own = self.everyone[lax.div(source, 2)].astype(F32)
        return jnp.where(lax.rem(source, 2) == self.core, own, self.got[...].astype(F32)).astype(BF16)

    def finish(self):
        self.gather.finish()
        self.pair().wait_send()


class PickFour(Pick):
    def relay(self, wanted):
        self.gather.wait()
        for m in range(4):
            self.give[m] = self.everyone[lax.div(wanted(m), 2)]
        self.pair().start()

    def result(self, wanted, put):
        self.pair().wait_recv()
        for m in range(4):
            own = self.give[m].astype(F32)
            put(m, jnp.where(lax.rem(wanted(m), 2) == self.core, own, self.got[m].astype(F32)).astype(BF16))


def total_of(count, base, piece):
    return lax.fori_loop(1, count, lambda k, acc: acc + piece(k).astype(F32), base.astype(F32))


def matmul(left, right):
    return jnp.dot(left, right, preferred_element_type=F32)


def against(left, right):
    return lax.dot_general(left, right, (((1,), (1,)), ((), ())), preferred_element_type=F32)


def against_first(left, right):
    return lax.dot_general(left, right, (((0,), (0,)), ((), ())), preferred_element_type=F32)


def shifted(field, step):
    lane = lax.broadcasted_iota(jnp.int32, (field.shape[0], 128), 1)
    edge = 127 if step > 0 else 0
    parts = []
    for start in range(0, field.shape[1], 128):
        turned = pltpu.roll(field[:, start : start + 128], (-step) % 128, 1)
        parts.append(jnp.where(lane == edge, 0.0, turned))
    return parts[0] if len(parts) == 1 else jnp.concatenate(parts, axis=1)


def spread(rows, target, flip):
    lane = lax.div(lax.broadcasted_iota(jnp.int32, rows.shape, 1), HEAD_DIM)
    wide = rows.astype(F32)
    full = jnp.concatenate([jnp.where(lane == h, wide, 0.0) for h in range(HEADS)], axis=0)
    target[...] = full.astype(BF16)
    flip[...] = full.T.astype(BF16)


def diagonal(full):
    lane = lax.div(lax.broadcasted_iota(jnp.int32, (SLOTS, CHANNELS), 1), HEAD_DIM)
    total = jnp.zeros((SLOTS, CHANNELS), F32)
    for h in range(HEADS):
        total = jnp.where(lane == h, full[h * SLOTS : (h + 1) * SLOTS], total)
    return total


def kernel(
    group_ref, slot_ref, time_ref,
    hidden_ref, kvw_ref, latent_ref, noise_ref, emb_ref, inw_ref, qw_ref, ow_ref, resw_hbm, up_hbm,
    block3_ref, res_ref, query_ref, out_ref, ghidden_ref, kvout_ref,
    resw_ref, up3_ref, load_sems, inw_f, inw_t, turn, up_ref, block_ref,
    noisy, band, cond, part, f_inbox, f_all, f_give, f_kv, wcat, qw_t, ow_t, taps, first,
    hid, query, att, prob, gatt, gscore, gquery, ghid, bk, bk_t, bv, bv_t,
    gkv, s_inbox, s_all, s_give, s_got, s_image,
    grads, in_core, half, in_1, mid, in_2, sum_f, in_z, final,
    quarters, four_cond, k_quarter, k_z, k_final,
    halo_sems, f_sum_sems, f_img_sems, f_pair_sems, f_row_sems,
    s_sum_sems, s_img_sems, s_pair_sems, s_row_sems,
    core_sems, s1_sems, s2_sems, z_sems,
    gz_sems, g1_sems, g2_sems, gcore_sems,
    q_sems, kz_sems,
    kgz1_sems, kgx1_sems, kgx2_sems, kgz2_sems, kgc_sems,
    *, weight_scale, kv_scale,
):
    loads = [
        pltpu.make_async_copy(resw_hbm, resw_ref, load_sems.at[0]),
        pltpu.make_async_copy(up_hbm, up3_ref, load_sems.at[1]),
    ]
    for load in loads:
        load.start()
    img, row = place()
    z, x, y, core = coords(img, row)
    partner = device(z, x, y, 1 - core)
    low = lax.rem(x, 2)
    across = device(z, x + 1 - 2 * low, y, core)

    band[...] = jnp.zeros_like(band)
    signals = greet(img, row)

    def at_x(k):
        return lax.rem(x + k, 4)

    def at_y(k):
        return lax.rem(y + k, 4)

    def at_z(k):
        return lax.rem(z + k, 8)

    tokens = hidden_ref.shape[1]
    token = lax.broadcasted_iota(jnp.int32, (SLOTS, tokens), 1)
    wanted = lax.broadcasted_iota(jnp.int32, (SLOTS, tokens), 0) + slot_ref[0]
    pick_rows = (token == wanted).astype(BF16)
    cond[...] = against(hidden_ref[...], pick_rows).astype(BF16)
    units = cond[...].reshape(cond.shape[0] // 16, 16, SLOTS)
    for q in range(4):
        count = min(14, units.shape[0] - 14 * q)
        quarters[q, pl.ds(0, count)] = units[14 * q : 14 * q + count]
    quarters[3, pl.ds(10, 4)] = jnp.zeros((4, 16, SLOTS), BF16)
    member = lax.rem(img, 4)
    four_cond[member] = quarters[2 * core + low]
    product = against_first(cond[...], kvw_ref[...])
    part[0] = product[:, :CHANNELS]
    part[1] = product[:, CHANNELS:]

    index = lax.broadcasted_iota(jnp.int32, (8, 128), 0) * 128 + lax.broadcasted_iota(
        jnp.int32, (8, 128), 1
    )
    share_of = index.astype(F32) / 999.0
    beta = (0.00085**0.5 * (1.0 - share_of) + 0.012**0.5 * share_of) ** 2
    logs = jnp.where(index <= time_ref[0], jnp.log(1.0 - jnp.where(index < 1000, beta, 0.0)), 0.0)
    level = jnp.exp(jnp.sum(logs, axis=(0, 1), keepdims=True))
    keep, add = jnp.sqrt(level), jnp.sqrt(1.0 - level)
    for c in range(4):
        noisy[c] = (keep * latent_ref[c] + add * noise_ref[c]).astype(BF16).astype(F32)
    for r in range(8):
        band[2 + r, pl.ds(0, 4)] = noisy[:, r, :]

    pl.semaphore_wait(pltpu.get_barrier_semaphore(), signals)

    def halo_up():
        return remote(band.at[pl.ds(8, 2)], band.at[pl.ds(0, 2)], halo_sems, 0, (img, lax.rem(row + 1, ROWS)))

    def halo_down():
        return remote(band.at[pl.ds(2, 2)], band.at[pl.ds(10, 2)], halo_sems, 1, (img, lax.rem(row + ROWS - 1, ROWS)))

    above, below = row > 0, row < ROWS - 1
    pl.when(below)(lambda: halo_up().start())
    pl.when(above)(lambda: halo_down().start())
    f_sum = RowSum(img, row, part, f_inbox, f_sum_sems)
    f_sum.start()

    def quarter_copy(k):
        to = lax.rem(member + k, 4)
        return remote(
            quarters.at[2 * lax.rem(to, 2) + lax.div(to, 2)], four_cond.at[member], q_sems, k - 1,
            (img - member + to, row),
        )

    each(4, lambda k: quarter_copy(k).start())

    inw_f[...] = jnp.zeros_like(inw_f)
    for t in range(9):
        inw_f[pl.ds(8 * t, 4)] = inw_ref[t].astype(F32)
    inw_t[...] = inw_f[...].T.astype(BF16)
    loads[0].wait()
    for a in range(3):
        for b in range(3):
            wcat[a, :, b * CHANNELS : (b + 1) * CHANNELS] = resw_ref[3 * a + b]
    qw_t[...] = qw_ref[...].astype(F32).T.astype(BF16)
    ow_t[...] = ow_ref[...].astype(F32).T.astype(BF16)

    def source_of(which):
        return lax.fori_loop(
            0, IMGS, lambda i, s: jnp.maximum(s, jnp.where(group_ref[i] == which, i, 0)), jnp.int32(0)
        )

    other = img + 1 - 2 * core
    source, other_source = source_of(img), source_of(other)
    half_img = lax.div(img, 2)
    f_gather = Gather(
        IMGS // 2, half_img, lambda j: (2 * j + core, row), lambda j: f_all.at[j], f_img_sems
    )
    f_all[half_img] = f_sum.total().astype(BF16)
    f_gather.start()

    pl.when(above)(lambda: halo_up().wait_recv())
    pl.when(below)(lambda: halo_down().wait_recv())

    def first_rows(j):
        fields = []
        for r in range(2):
            pieces = []
            for a in range(3):
                n = band[2 * j + r + a]
                pieces += [shifted(n, -1), n, shifted(n, 1)]
            fields.append(jnp.concatenate(pieces, axis=0))
        field = jnp.concatenate(fields, axis=1).astype(BF16)
        value = matmul(inw_t[...], field)
        lanes = pl.ds(pl.multiple_of(j * 256, 256), 256)
        first[:, lanes] = value
        v = value + emb_ref[...]
        line = row * 8 - 1 + 2 * j + lax.div(lax.broadcasted_iota(jnp.int32, v.shape, 1), 128)
        act = jnp.where((line >= 0) & (line < 64), v / (1.0 + jnp.exp(-v)), 0.0)
        act = act.astype(BF16).astype(F32)
        taps[pl.ds(0, CHANNELS), lanes] = shifted(act, -1).astype(BF16)
        taps[pl.ds(CHANNELS, CHANNELS), lanes] = act.astype(BF16)
        taps[pl.ds(2 * CHANNELS, CHANNELS), lanes] = shifted(act, 1).astype(BF16)

    each(5, first_rows, 0)

    def cells(n, more=0):
        return pl.ds(pl.multiple_of(n * 256 + more, 128), 256)

    def residual(n):
        acc = first[:, cells(n, 128)]
        for a in range(3):
            acc = acc + matmul(wcat[a], taps[:, cells(n, 128 * a)])
        hid[:, cells(n)] = acc.astype(BF16)

    each(4, residual, 0)


    def band_slot(which, j):
        return f_kv.at[which, lax.rem(j, 2), rows16(lax.div(j, 2))]

    f_gather.wait()
    f_kv[0, lax.rem(row, 2), rows16(lax.div(row, 2))] = f_all[lax.div(source, 2)]
    f_give[...] = f_all[lax.div(other_source, 2)]
    f_share = Gather(ROWS, row, lambda j: (img, j), lambda j: band_slot(0, j), f_row_sems)

    def f_cross(k):
        return remote(
            f_give, band_slot(1, row), f_pair_sems, k, (other, lax.rem(row + k, ROWS))
        )

    each(ROWS, lambda k: f_cross(k).start(), 0)
    f_share.start()

    loads[1].wait()

    def flatten(c):
        channels = rows16(4 * c, 64)
        turn[...] = up3_ref[channels].astype(F32)
        for r in range(8):
            up_ref[channels, r * 128 : (r + 1) * 128] = turn[:, r, :].astype(BF16)

    each(5, flatten, 0)

    def unflatten(c):
        channels = rows16(4 * c, 64)
        for r in range(8):
            turn[:, r, :] = block_ref[channels, r * 128 : (r + 1) * 128].astype(F32)
        block3_ref[channels] = turn[...].astype(BF16)

    def projections(n):
        query[:, cells(n)] = matmul(qw_ref[...], hid[:, cells(n)]).astype(BF16)
        gatt[:, cells(n)] = matmul(ow_t[...], up_ref[:, cells(n)]).astype(BF16)

    each(4, projections, 0)
    f_share.wait()
    each(ROWS, lambda k: f_cross(k).wait_recv(), 0)
    same = lax.rem(source, 2) == core
    for side, (wide, flip) in enumerate(((bk, bk_t), (bv, bv_t))):
        spread(jnp.where(same, f_kv[0, side].astype(F32), f_kv[1, side].astype(F32)), wide, flip)

    def attend(n):
        here = cells(n)
        score = matmul(bk[...], query[:, here]) * HEAD_DIM**-0.5
        score = score.reshape(HEADS, SLOTS, 256)
        top = jnp.max(score, axis=1, keepdims=True)
        grown = jnp.exp(score - top)
        soft = grown / jnp.sum(grown, axis=1, keepdims=True)
        soft_low = soft.reshape(CHANNELS, 256).astype(BF16)
        prob[:, here] = soft_low
        gprob = matmul(bv[...], gatt[:, here]).reshape(HEADS, SLOTS, 256)
        mean = jnp.sum(soft * gprob, axis=1, keepdims=True)
        gs = (HEAD_DIM**-0.5 * soft * (gprob - mean)).reshape(CHANNELS, 256).astype(BF16)
        gscore[:, here] = gs

    def attend_more(n):
        here = cells(n)
        attended = matmul(bv_t[...], prob[:, here]).astype(BF16)
        att[:, here] = attended
        block_ref[:, here] = (
            hid[:, here].astype(F32) + matmul(ow_ref[...], attended)
        ).astype(BF16)
        gq = matmul(bk_t[...], gscore[:, here]).astype(BF16)
        gquery[:, here] = gq
        ghid[:, here] = (up_ref[:, here].astype(F32) + matmul(qw_t[...], gq)).astype(BF16)

    each(4, attend, 0)

    gkv[0] = diagonal(against(gscore[...], query[...])).astype(BF16)
    gkv[1] = diagonal(against(prob[...], gatt[...])).astype(BF16)
    row_sum = RowSum(img, row, gkv, s_inbox, s_sum_sems)
    row_sum.start()

    each(4, attend_more, 0)

    def core_copy(t):
        return remote(
            grads.at[t, rows16((1 - core) * 10, 160)], in_core.at[t], core_sems, t, partner
        )

    grads[0] = against(gquery[...], hid[...]).astype(BF16)
    core_copy(0).start()
    grads[1] = against(up_ref[...], att[...]).astype(BF16)
    core_copy(1).start()

    def tap(t):
        a, b = lax.div(t - 2, 3), lax.rem(t - 2, 3)
        field = taps[
            pl.ds(pl.multiple_of(b * CHANNELS, CHANNELS), CHANNELS),
            pl.ds(pl.multiple_of(a * 128, 128), 1024),
        ]
        grads[t] = against(ghid[...], field).astype(BF16)
        core_copy(t).start()

    def x_first(j):
        return j % 2 == 1

    def at(axis_x, k):
        return device(z, at_x(k), y, core) if axis_x else device(z, x, at_y(k), core)

    def s1_copy(j, k):
        src = half.at[j, at_x(k)] if x_first(j) else half.at[j, :, at_y(k)]
        return remote(src, in_1.at[j, k - 1], s1_sems, 3 * j + k - 1, at(x_first(j), k))

    def s2_copy(j, k):
        src = mid.at[j, at_y(k) if x_first(j) else at_x(k)]
        return remote(src, in_2.at[j, k - 1], s2_sems, 3 * j + k - 1, at(not x_first(j), k))

    def z_copy(k):
        to = at_z(k)
        return remote(
            sum_f.at[lax.rem(to, 7)], in_z.at[k - 1], z_sems, k - 1, device(to, x, y, core)
        )

    def to_owner(k, act):
        pl.when(at_z(k) < 7)(lambda: act(k))

    def from_owner(k, act):
        pl.when(lax.rem(z + 8 - k, 8) < 7)(lambda: act(k))

    def across_cores(j, begin, end):
        each(end, lambda t: core_copy(t).wait_recv(), begin)

        def add(u):
            unit = 16 * j + u
            t, i = lax.div(unit, 10), lax.rem(unit, 10)
            half[j, lax.div(u, 4), lax.rem(u, 4)] = (
                grads[t, rows16(core * 10 + i)].astype(F32) + in_core[t, rows16(i)].astype(F32)
            ).astype(BF16)

        each(min(16, TAPS * 10 - 16 * j), add, 0)
        each(4, lambda k: s1_copy(j, k).start())

    def across_first(j):
        each(4, lambda k: s1_copy(j, k).wait_recv())
        own = half[j, x] if x_first(j) else half[j, :, y]
        mid[j] = total_of(4, own, lambda k: in_1[j, k - 1]).astype(BF16)
        each(4, lambda k: s2_copy(j, k).start())

    def across_second(j):
        each(4, lambda k: s2_copy(j, k).wait_recv())
        own = mid[j, y if x_first(j) else x]
        sum_f[j] = total_of(4, own, lambda k: in_2[j, k - 1]).astype(BF16)
        pl.when(z != j)(lambda: z_copy(lax.rem(j + 8 - z, 8)).start())

    half[SLICES - 1, 3, pl.ds(2, 2)] = jnp.zeros((2, 16, CHANNELS), BF16)
    pick = PickFour(img, row, s_all, s_give, s_got, s_img_sems, s_pair_sems)
    each(3, tap, 2)
    pick.start(row_sum.total().astype(BF16))
    across_cores(0, 0, 2)
    each(5, tap, 3)
    across_cores(1, 2, 4)
    each(6, tap, 5)
    across_cores(2, 4, 5)
    each(8, tap, 6)
    across_cores(3, 5, 7)
    each(9, tap, 8)
    across_cores(4, 7, 8)
    across_first(0)
    each(11, tap, 9)
    across_cores(5, 8, 10)
    across_cores(6, 10, 11)
    zi = lax.rem(z, 7)

    def kz_copy(k):
        to = at_z(k)
        return remote(
            k_quarter.at[:, lax.rem(to, 7)], k_z.at[k - 1], kz_sems, k - 1, device(to, x, y, core)
        )

    def g1_copy(j, k):
        mine = final.at[core, j, x, y]
        return remote(mine, mine, g1_sems, 3 * j + k - 1, at(not x_first(j), k))

    def g2_copy(j, k):
        mine = final.at[core, j, x] if x_first(j) else final.at[core, j, :, y]
        return remote(mine, mine, g2_sems, 3 * j + k - 1, at(x_first(j), k))

    def core_pass(j, k):
        mine = (
            final.at[core, j, lax.rem(x + 4 - k, 4)]
            if x_first(j)
            else final.at[core, j, :, lax.rem(y + 4 - k, 4)]
        )
        return remote(mine, mine, gcore_sems, 4 * j + k, partner)

    def spread_second(j):
        @pl.when(z != j)
        def _():
            gz_copy(lax.rem(z + 8 - j, 8)).wait_recv()

        each(4, lambda k: g1_copy(j, k).start())

    def spread_first(j):
        each(4, lambda k: g1_copy(j, k).wait_recv())
        each(4, lambda k: g2_copy(j, k).start())
        core_pass(j, 0).start()

    def spread_core(j):
        def go(k):
            g2_copy(j, k).wait_recv()
            core_pass(j, k).start()

        each(4, go)

    def kgz1_copy(k):
        mine = k_final.at[core, low, 0, zi]
        return remote(mine, mine, kgz1_sems, k - 1, device(at_z(k), x, y, core))

    def kgx1_copy():
        mine = k_final.at[core, low, 0]
        return remote(mine, mine, kgx1_sems, 0, across)

    def kgx2_copy():
        mine = k_final.at[core, low, 1, zi]
        return remote(mine, mine, kgx2_sems, 0, across)

    def kgz2_copy(k):
        mine = k_final.at[core, :, 1, zi]
        return remote(mine, mine, kgz2_sems, k - 1, device(at_z(k), x, y, core))

    def kgc_copy(k):
        part_x, turn_of = ((low, 0), (0, 1), (1, 1), (1 - low, 0))[k]
        mine = k_final.at[core, part_x, turn_of]
        return remote(mine, mine, kgc_sems, k, partner)


    def wanted(m):
        return group_ref[4 * z + m]

    pick.relay(wanted)
    across_first(1)

    def put(m, value):
        s_image[m, lax.rem(row, 2), rows16(lax.div(row, 2))] = value

    pick.result(wanted, put)
    share = Gather(
        ROWS, row, lambda j: (img, j),
        lambda j: s_image.at[:, lax.rem(j, 2), rows16(lax.div(j, 2))], s_row_sems,
    )
    share.start()
    across_first(2)
    across_second(0)
    across_first(3)
    across_second(1)
    share.wait()
    each(4, lambda k: quarter_copy(k).wait_recv())
    for side in range(2):
        total = jnp.zeros((224, CHANNELS), F32)
        for m in range(4):
            total = total + matmul(four_cond[m].reshape(224, SLOTS), s_image[m, side])
        k_quarter[:, :, :, side * CHANNELS : (side + 1) * CHANNELS] = total.astype(BF16).reshape(
            2, 7, 16, CHANNELS
        )
    each(8, lambda k: to_owner(k, lambda i: kz_copy(i).start()))
    across_first(4)
    across_second(2)
    across_first(5)
    across_second(3)
    across_first(6)
    across_second(4)
    across_second(5)
    across_second(6)
    @pl.when(z < 7)
    def _():
        each(8, lambda k: z_copy(k).wait_recv())
        done = total_of(8, sum_f[zi], lambda k: in_z[k - 1]) * weight_scale
        final[core, zi, x, y] = done.astype(BF16)

    def gz_copy(k):
        mine = final.at[core, zi, x, y]
        return remote(mine, mine, gz_sems, k - 1, device(at_z(k), x, y, core))

    @pl.when(z < 7)
    def _():
        each(8, lambda k: gz_copy(k).start())

    @pl.when(z < 7)
    def _():
        each(8, lambda k: kz_copy(k).wait_recv())
        done = (total_of(8, k_quarter[:, zi], lambda k: k_z[k - 1]) * kv_scale).astype(BF16)
        k_final[core, low, 0, zi] = done[0]
        k_final[core, low, 1, zi] = done[1]
        kgx2_copy().start()
        each(8, lambda k: kgz1_copy(k).start())

    image = jnp.concatenate([s_image[member, 0], s_image[member, 1]], axis=1)
    gcond = against(kvw_ref[...], image).astype(BF16)
    spot = lax.broadcasted_iota(jnp.int32, (SLOTS, tokens), 1)
    slot = lax.broadcasted_iota(jnp.int32, (SLOTS, tokens), 0) + slot_ref[0]
    ghidden_ref[...] = matmul(gcond, (spot == slot).astype(BF16)).astype(BF16)

    @pl.when(z < 7)
    def _():
        kgx2_copy().wait_recv()
        each(8, lambda k: kgz2_copy(k).start())

    each(5, unflatten, 0)
    for j in range(SLICES):
        spread_second(j)
    for j in range(SLICES):
        spread_first(j)
    each(8, lambda k: from_owner(k, lambda i: kgz1_copy(i).wait_recv()))
    kgx1_copy().start()
    kgc_copy(0).start()
    for j in range(0, 4):
        spread_core(j)
    each(8, lambda k: from_owner(k, lambda i: kgz2_copy(i).wait_recv()))
    kgc_copy(1).start()
    kgc_copy(2).start()
    for j in range(4, SLICES):
        spread_core(j)
    kgx1_copy().wait_recv()
    kgc_copy(3).start()

    for j in range(SLICES):
        each(4, lambda k, j=j: core_pass(j, k).wait_recv(), 0)

    for t in range(TAPS):
        target, base = ((query_ref, 0), (out_ref, 0))[t] if t < 2 else (res_ref, (t - 2) * CHANNELS)
        for c in range(2):
            for i in range(10):
                j, rest = divmod(t * 10 + i, 16)
                target[pl.ds(base + c * 160 + i * 16, 16)] = final[c, j, rest // 4, rest % 4]
    for k in range(4):
        kgc_copy(k).wait_recv()
    for unit in range(52):
        q, rest = divmod(unit, 14)
        kvout_ref[pl.ds(16 * unit, 16)] = k_final[q // 2, q % 2, rest // 7, rest % 7]

    pl.when(below)(lambda: halo_up().wait_send())
    pl.when(above)(lambda: halo_down().wait_send())
    for one in (f_sum, f_gather, f_share, row_sum, pick, share):
        one.finish()
    each(ROWS, lambda k: f_cross(k).wait_send(), 0)
    each(TAPS, lambda t: core_copy(t).wait_send(), 0)
    for j in range(SLICES):
        for copy in (s1_copy, s2_copy, g1_copy, g2_copy):
            each(4, lambda k, copy=copy, j=j: copy(j, k).wait_send())
        each(4, lambda k, j=j: core_pass(j, k).wait_send(), 0)
    each(8, lambda k: to_owner(k, lambda i: z_copy(i).wait_send()))
    each(8, lambda k: to_owner(k, lambda i: kz_copy(i).wait_send()))
    each(4, lambda k: quarter_copy(k).wait_send())

    @pl.when(z < 7)
    def _():
        for copy in (gz_copy, kgz1_copy, kgz2_copy):
            each(8, lambda k, copy=copy: copy(k).wait_send())
        kgx2_copy().wait_send()

    kgx1_copy().wait_send()
    for k in range(4):
        kgc_copy(k).wait_send()


def finish_kernel(*refs):
    count = (len(refs) - 1) // 3
    sems = refs[-1]
    loads = [pltpu.make_async_copy(refs[i], refs[2 * count + i], sems.at[0, i]) for i in range(count)]
    stores = [pltpu.make_async_copy(refs[2 * count + i], refs[count + i], sems.at[1, i]) for i in range(count)]
    for load in loads:
        load.start()
    for load, store in zip(loads, stores):
        load.wait()
        store.start()
    for store in stores:
        store.wait()


def finish(arrays):
    anywhere = pl.BlockSpec(memory_space=pl.ANY)
    return pl.pallas_call(
        finish_kernel,
        out_shape=tuple(jax.ShapeDtypeStruct(a.shape, a.dtype) for a in arrays),
        in_specs=[anywhere] * len(arrays),
        out_specs=(anywhere,) * len(arrays),
        scratch_shapes=[pltpu.VMEM(a.shape, a.dtype) for a in arrays]
        + [pltpu.SemaphoreType.DMA((2, len(arrays)))],
        compiler_params=pltpu.CompilerParams(vmem_limit_bytes=62 * 2**20),
        name="finish",
    )(*arrays)


def shards(
    llm_hidden,
    slot_start,
    image_group,
    timesteps,
    latents,
    noise,
    kv_weight,
    in_weight,
    res_weight,
    query_weight,
    out_weight,
    cotangent,
):
    width, features = CHANNELS, llm_hidden.shape[1]
    frequency = jnp.exp(-math.log(10000.0) * jnp.arange(width // 2, dtype=F32) / (width // 2))
    angles = timesteps[0].astype(F32) * frequency
    emb = jnp.concatenate([jnp.cos(angles), jnp.sin(angles)])[:, None]
    vmem, smem = pl.BlockSpec(memory_space=pltpu.VMEM), pl.BlockSpec(memory_space=pltpu.SMEM)
    anywhere = pl.BlockSpec(memory_space=pl.ANY)
    dma = lambda n: pltpu.SemaphoreType.DMA((2, n))
    low = lambda *shape: pltpu.VMEM(shape, BF16)
    field, square = low(width, 1024), low(width, width)
    out = lambda *shape: jax.ShapeDtypeStruct(shape, BF16)
    block, res, query, projection, grad_hidden, grad_kv_weight = pl.pallas_call(
        functools.partial(
            kernel,
            weight_scale=(IMGS * ROWS * 1024) ** (-0.5),
            kv_scale=(IMGS * SLOTS) ** (-0.5),
        ),
        out_shape=(
            out(width, 8, 128), out(9 * width, width), out(width, width), out(width, width),
            out(features, llm_hidden.shape[0]), out(*kv_weight.shape),
        ),
        in_specs=[smem] * 3 + [vmem] * 8 + [anywhere] * 2,
        out_specs=(vmem,) * 6,
        scratch_shapes=[
            low(9, width, width), low(width, 8, 128), pltpu.SemaphoreType.DMA((2,)),
            pltpu.VMEM((72, width), F32), low(width, 72), pltpu.VMEM((64, 8, 128), F32), field, field,
            pltpu.VMEM((4, 8, 128), F32), pltpu.VMEM((12, 8, 128), F32),
            low(features, SLOTS), pltpu.VMEM((2, SLOTS, width), F32),
            pltpu.VMEM((ROWS - 1, 16, width), F32), low(IMGS // 2, 16, width),
            low(16, width), low(2, 2, SLOTS, width),
            low(3, width, 3 * width), square, square,
            low(3 * width, 1280), pltpu.VMEM((width, 1280), F32),
            field, field, field, field, field, field, field, field, square, square, square, square,
            low(2, SLOTS, width), low(ROWS - 1, 16, width), low(IMGS // 2, 16, width),
            low(4, 16, width), low(4, 16, width), low(4, 2, SLOTS, width),
            low(TAPS, width, width), low(TAPS, 160, width), low(SLICES, 4, 4, 16, width),
            low(SLICES, 3, 4, 16, width), low(SLICES, 4, 16, width), low(SLICES, 3, 16, width),
            low(SLICES, 16, width), low(7, 16, width), low(2, SLICES, 4, 4, 16, width),
            low(4, 14, 16, SLOTS), low(4, 14, 16, SLOTS), low(2, 7, 16, 2 * width),
            low(7, 2, 16, 2 * width), low(2, 2, 2, 7, 16, 2 * width),
            dma(2), dma(7), dma(15), dma(ROWS), dma(7),
            dma(7), dma(15), dma(1), dma(7),
            dma(TAPS), dma(3 * SLICES), dma(3 * SLICES), dma(7),
            dma(7), dma(3 * SLICES), dma(3 * SLICES), dma(4 * SLICES),
            dma(3), dma(7),
            dma(7), dma(1), dma(1), dma(7), dma(4),
        ],
        compiler_params=pltpu.CompilerParams(
            collective_id=0, has_side_effects=True, vmem_limit_bytes=60 * 2**20
        ),
        name="block",
    )(
        image_group, slot_start, timesteps, llm_hidden.T, kv_weight, latents[0], noise[0], emb,
        in_weight.transpose(0, 1, 3, 2).reshape(9, 4, width), query_weight, out_weight,
        res_weight.reshape(9, width, width), cotangent[0],
    )
    query, projection, block, grad_hidden, grad_kv_weight, res = finish(
        (query, projection, block, grad_hidden, grad_kv_weight, res.reshape(3, 3, width, width))
    )
    return block[None], grad_hidden.T, grad_kv_weight, res, query, projection


def solution(mesh):
    return jax.shard_map(
        shards,
        mesh=mesh,
        in_specs=(
            P("img", "row"),
            P("img"),
            P(),
            P("img"),
            P("img", None, "row", None),
            P("img", None, "row", None),
            P("row", None),
            P(),
            P(),
            P(),
            P(),
            P("img", None, "row", None),
        ),
        out_specs=(P("img", None, "row", None), P("img", "row"), P("row", None), P(), P(), P()),
        check_vma=False,
    )
```

```python
import functools
import math

import jax
import jax.numpy as jnp
from jax import lax
from jax.experimental import pallas as pl
from jax.experimental.pallas import tpu as pltpu
from jax.sharding import PartitionSpec as P

HEAD_DIM = 64
SLOTS = 64
MESH = pl.DeviceIdType.MESH
CHANNELS = 320
HEADS = 5
IMGS, ROWS = 32, 8
TAPS = 11
SLICES = 7
F32, BF16 = jnp.float32, jnp.bfloat16


def place():
    img, row = lax.axis_index("img"), lax.axis_index("row")
    return img, row


def coords(img, row):
    z, low, core = lax.div(img, 4), lax.rem(lax.div(img, 2), 2), lax.rem(img, 2)
    return z, lax.div(row, 4) * 2 + low, lax.rem(row, 4), core


def device(z, x, y, core):
    return (z * 4 + lax.rem(x, 2) * 2 + core, lax.div(x, 2) * 4 + y)


def remote(src, dst, sems, slot, where):
    return pltpu.make_async_remote_copy(
        src_ref=src,
        dst_ref=dst,
        send_sem=sems.at[0, slot],
        recv_sem=sems.at[1, slot],
        device_id=where,
        device_id_type=MESH,
    )


def each(count, act, first=1):
    def body(k, carry):
        act(k)
        return carry

    lax.fori_loop(first, count, body, 0)


def rows16(index, count=16):
    return pl.ds(pl.multiple_of(index * 16, 16), count)


def greet(img, row):
    barrier = pltpu.get_barrier_semaphore()

    def call(where):
        pl.semaphore_signal(barrier, inc=1, device_id=where, device_id_type=MESH)

    each(ROWS, lambda k: call((img, lax.rem(row + k, ROWS))))
    each(IMGS // 2, lambda k: call((lax.rem(img + 2 * k, IMGS), row)))
    call((img + 1 - 2 * lax.rem(img, 2), row))
    call((img + 3 - 2 * lax.rem(img, 4), row))
    z, x, y, core = coords(img, row)
    other = 2 * (1 - lax.div(x, 2)) + (1 - lax.rem(x, 2))
    call(device(z, other, y, core))
    return ROWS - 1 + IMGS // 2 - 1 + 1 + 1 + 1


class RowSum:
    def __init__(self, img, row, part, inbox, sems):
        self.img, self.row, self.part, self.inbox, self.sems = img, row, part, inbox, sems

    def copy(self, k):
        r = lax.rem(self.row + k, ROWS)
        src = self.part.at[lax.rem(r, 2), rows16(lax.div(r, 2))]
        return remote(src, self.inbox.at[k - 1], self.sems, k - 1, (self.img, r))

    def start(self):
        each(ROWS, lambda k: self.copy(k).start())

    def total(self):
        own = self.part[lax.rem(self.row, 2), rows16(lax.div(self.row, 2))].astype(F32)

        def body(k, acc):
            self.copy(k).wait_recv()
            return acc + self.inbox[k - 1].astype(F32)

        return lax.fori_loop(1, ROWS, body, own)

    def finish(self):
        each(ROWS, lambda k: self.copy(k).wait_send())


class Gather:
    def __init__(self, count, me, where, target, sems):
        self.count, self.me, self.where, self.target, self.sems = count, me, where, target, sems

    def copy(self, k):
        to = lax.rem(self.me + k, self.count)
        return remote(
            self.target(self.me), self.target(self.me), self.sems, k - 1, self.where(to)
        )

    def start(self):
        each(self.count, lambda k: self.copy(k).start())

    def wait(self):
        each(self.count, lambda k: self.copy(k).wait_recv())

    def finish(self):
        each(self.count, lambda k: self.copy(k).wait_send())


class Pick:
    def __init__(self, img, row, everyone, give, got, sems, pair_sems):
        self.img, self.row, self.core = img, row, lax.rem(img, 2)
        self.everyone, self.give, self.got, self.pair_sems = everyone, give, got, pair_sems
        self.gather = Gather(
            IMGS // 2, lax.div(img, 2), lambda j: (2 * j + self.core, row),
            lambda j: everyone.at[j], sems,
        )

    def start(self, own):
        self.everyone[lax.div(self.img, 2)] = own
        self.gather.start()

    def pair(self):
        where = (self.img + 1 - 2 * self.core, self.row)
        return remote(self.give, self.got, self.pair_sems, 0, where)

    def relay(self, wanted):
        self.gather.wait()
        self.give[...] = self.everyone[lax.div(wanted, 2)]
        self.pair().start()

    def result(self, source):
        self.pair().wait_recv()
        own = self.everyone[lax.div(source, 2)].astype(F32)
        return jnp.where(lax.rem(source, 2) == self.core, own, self.got[...].astype(F32)).astype(BF16)

    def finish(self):
        self.gather.finish()
        self.pair().wait_send()


class PickFour(Pick):
    def relay(self, wanted):
        self.gather.wait()
        for m in range(4):
            self.give[m] = self.everyone[lax.div(wanted(m), 2)]
        self.pair().start()

    def result(self, wanted, put):
        self.pair().wait_recv()
        for m in range(4):
            own = self.give[m].astype(F32)
            put(m, jnp.where(lax.rem(wanted(m), 2) == self.core, own, self.got[m].astype(F32)).astype(BF16))


def total_of(count, base, piece):
    return lax.fori_loop(1, count, lambda k, acc: acc + piece(k).astype(F32), base.astype(F32))


def matmul(left, right):
    return jnp.dot(left, right, preferred_element_type=F32)


def against(left, right):
    return lax.dot_general(left, right, (((1,), (1,)), ((), ())), preferred_element_type=F32)


def against_first(left, right):
    return lax.dot_general(left, right, (((0,), (0,)), ((), ())), preferred_element_type=F32)


def shifted(field, step):
    lane = lax.broadcasted_iota(jnp.int32, (field.shape[0], 128), 1)
    edge = 127 if step > 0 else 0
    parts = []
    for start in range(0, field.shape[1], 128):
        turned = pltpu.roll(field[:, start : start + 128], (-step) % 128, 1)
        parts.append(jnp.where(lane == edge, 0.0, turned))
    return parts[0] if len(parts) == 1 else jnp.concatenate(parts, axis=1)


def spread(rows, target, flip):
    lane = lax.div(lax.broadcasted_iota(jnp.int32, rows.shape, 1), HEAD_DIM)
    wide = rows.astype(F32)
    full = jnp.concatenate([jnp.where(lane == h, wide, 0.0) for h in range(HEADS)], axis=0)
    target[...] = full.astype(BF16)
    flip[...] = full.T.astype(BF16)


def diagonal(full):
    lane = lax.div(lax.broadcasted_iota(jnp.int32, (SLOTS, CHANNELS), 1), HEAD_DIM)
    total = jnp.zeros((SLOTS, CHANNELS), F32)
    for h in range(HEADS):
        total = jnp.where(lane == h, full[h * SLOTS : (h + 1) * SLOTS], total)
    return total


def kernel(
    group_ref, slot_ref, time_ref,
    hidden_ref, kvw_ref, latent_ref, noise_ref, emb_ref, inw_ref, qw_ref, ow_ref, resw_hbm, up_hbm,
    block3_ref, res_ref, query_ref, out_ref, ghidden_ref, kvout_ref,
    resw_ref, up3_ref, load_sems, inw_f, inw_t, turn, up_ref, block_ref,
    noisy, band, cond, part, f_inbox, f_all, f_give, f_got, f_kv, wcat, qw_t, ow_t, taps, first,
    hid, query, att, prob, gatt, gscore, gquery, ghid, bk, bk_t, bv, bv_t,
    gkv, s_inbox, s_all, s_give, s_got, s_image,
    grads, in_core, half, in_1, mid, in_2, sum_f, in_z, final,
    quarters, four_cond, k_quarter, k_z, k_final,
    halo_sems, f_sum_sems, f_img_sems, f_pair_sems, f_row_sems,
    s_sum_sems, s_img_sems, s_pair_sems, s_row_sems,
    core_sems, s1_sems, s2_sems, z_sems,
    gz_sems, g1_sems, g2_sems, gcore_sems,
    q_sems, kz_sems,
    kgz1_sems, kgx1_sems, kgx2_sems, kgz2_sems, kgc_sems,
    *, weight_scale, kv_scale,
):
    loads = [
        pltpu.make_async_copy(resw_hbm, resw_ref, load_sems.at[0]),
        pltpu.make_async_copy(up_hbm, up3_ref, load_sems.at[1]),
    ]
    for load in loads:
        load.start()
    img, row = place()
    z, x, y, core = coords(img, row)
    partner = device(z, x, y, 1 - core)
    low = lax.rem(x, 2)
    across = device(z, x + 1 - 2 * low, y, core)

    band[...] = jnp.zeros_like(band)
    signals = greet(img, row)

    def at_x(k):
        return lax.rem(x + k, 4)

    def at_y(k):
        return lax.rem(y + k, 4)

    def at_z(k):
        return lax.rem(z + k, 8)

    tokens = hidden_ref.shape[1]
    token = lax.broadcasted_iota(jnp.int32, (SLOTS, tokens), 1)
    wanted = lax.broadcasted_iota(jnp.int32, (SLOTS, tokens), 0) + slot_ref[0]
    pick_rows = (token == wanted).astype(BF16)
    cond[...] = against(hidden_ref[...], pick_rows).astype(BF16)
    units = cond[...].reshape(cond.shape[0] // 16, 16, SLOTS)
    for q in range(4):
        count = min(14, units.shape[0] - 14 * q)
        quarters[q, pl.ds(0, count)] = units[14 * q : 14 * q + count]
    quarters[3, pl.ds(10, 4)] = jnp.zeros((4, 16, SLOTS), BF16)
    member = lax.rem(img, 4)
    four_cond[member] = quarters[2 * core + low]
    product = against_first(cond[...], kvw_ref[...])
    part[0] = product[:, :CHANNELS]
    part[1] = product[:, CHANNELS:]

    index = lax.broadcasted_iota(jnp.int32, (8, 128), 0) * 128 + lax.broadcasted_iota(
        jnp.int32, (8, 128), 1
    )
    share_of = index.astype(F32) / 999.0
    beta = (0.00085**0.5 * (1.0 - share_of) + 0.012**0.5 * share_of) ** 2
    logs = jnp.where(index <= time_ref[0], jnp.log(1.0 - jnp.where(index < 1000, beta, 0.0)), 0.0)
    level = jnp.exp(jnp.sum(logs, axis=(0, 1), keepdims=True))
    keep, add = jnp.sqrt(level), jnp.sqrt(1.0 - level)
    for c in range(4):
        noisy[c] = (keep * latent_ref[c] + add * noise_ref[c]).astype(BF16).astype(F32)
    for r in range(8):
        band[2 + r, pl.ds(0, 4)] = noisy[:, r, :]

    pl.semaphore_wait(pltpu.get_barrier_semaphore(), signals)

    def halo_up():
        return remote(band.at[pl.ds(8, 2)], band.at[pl.ds(0, 2)], halo_sems, 0, (img, lax.rem(row + 1, ROWS)))

    def halo_down():
        return remote(band.at[pl.ds(2, 2)], band.at[pl.ds(10, 2)], halo_sems, 1, (img, lax.rem(row + ROWS - 1, ROWS)))

    above, below = row > 0, row < ROWS - 1
    pl.when(below)(lambda: halo_up().start())
    pl.when(above)(lambda: halo_down().start())
    f_sum = RowSum(img, row, part, f_inbox, f_sum_sems)
    f_sum.start()

    def quarter_copy(k):
        to = lax.rem(member + k, 4)
        return remote(
            quarters.at[2 * lax.rem(to, 2) + lax.div(to, 2)], four_cond.at[member], q_sems, k - 1,
            (img - member + to, row),
        )

    each(4, lambda k: quarter_copy(k).start())

    inw_f[...] = jnp.zeros_like(inw_f)
    for t in range(9):
        inw_f[pl.ds(8 * t, 4)] = inw_ref[t].astype(F32)
    inw_t[...] = inw_f[...].T.astype(BF16)
    loads[0].wait()
    for a in range(3):
        for b in range(3):
            wcat[a, :, b * CHANNELS : (b + 1) * CHANNELS] = resw_ref[3 * a + b]
    qw_t[...] = qw_ref[...].astype(F32).T.astype(BF16)
    ow_t[...] = ow_ref[...].astype(F32).T.astype(BF16)

    def source_of(which):
        return lax.fori_loop(
            0, IMGS, lambda i, s: jnp.maximum(s, jnp.where(group_ref[i] == which, i, 0)), jnp.int32(0)
        )

    other = img + 1 - 2 * core
    source, other_source = source_of(img), source_of(other)
    f_pick = Pick(img, row, f_all, f_give, f_got, f_img_sems, f_pair_sems)
    f_pick.start(f_sum.total().astype(BF16))

    pl.when(above)(lambda: halo_up().wait_recv())
    pl.when(below)(lambda: halo_down().wait_recv())

    def first_rows(j):
        fields = []
        for r in range(2):
            pieces = []
            for a in range(3):
                n = band[2 * j + r + a]
                pieces += [shifted(n, -1), n, shifted(n, 1)]
            fields.append(jnp.concatenate(pieces, axis=0))
        field = jnp.concatenate(fields, axis=1).astype(BF16)
        value = matmul(inw_t[...], field)
        lanes = pl.ds(pl.multiple_of(j * 256, 256), 256)
        first[:, lanes] = value
        v = value + emb_ref[...]
        line = row * 8 - 1 + 2 * j + lax.div(lax.broadcasted_iota(jnp.int32, v.shape, 1), 128)
        act = jnp.where((line >= 0) & (line < 64), v / (1.0 + jnp.exp(-v)), 0.0)
        act = act.astype(BF16).astype(F32)
        taps[pl.ds(0, CHANNELS), lanes] = shifted(act, -1).astype(BF16)
        taps[pl.ds(CHANNELS, CHANNELS), lanes] = act.astype(BF16)
        taps[pl.ds(2 * CHANNELS, CHANNELS), lanes] = shifted(act, 1).astype(BF16)

    each(5, first_rows, 0)

    def cells(n, more=0):
        return pl.ds(pl.multiple_of(n * 256 + more, 128), 256)

    def residual(n):
        acc = first[:, cells(n, 128)]
        for a in range(3):
            acc = acc + matmul(wcat[a], taps[:, cells(n, 128 * a)])
        hid[:, cells(n)] = acc.astype(BF16)

    each(2, residual, 0)
    f_pick.relay(other_source)
    each(4, residual, 2)

    f_kv[lax.rem(row, 2), rows16(lax.div(row, 2))] = f_pick.result(source)
    f_share = Gather(
        ROWS, row, lambda j: (img, j),
        lambda j: f_kv.at[lax.rem(j, 2), rows16(lax.div(j, 2))], f_row_sems,
    )
    f_share.start()

    loads[1].wait()

    def flatten(c):
        channels = rows16(4 * c, 64)
        turn[...] = up3_ref[channels].astype(F32)
        for r in range(8):
            up_ref[channels, r * 128 : (r + 1) * 128] = turn[:, r, :].astype(BF16)

    each(5, flatten, 0)

    def unflatten(c):
        channels = rows16(4 * c, 64)
        for r in range(8):
            turn[:, r, :] = block_ref[channels, r * 128 : (r + 1) * 128].astype(F32)
        block3_ref[channels] = turn[...].astype(BF16)

    def projections(n):
        query[:, cells(n)] = matmul(qw_ref[...], hid[:, cells(n)]).astype(BF16)
        gatt[:, cells(n)] = matmul(ow_t[...], up_ref[:, cells(n)]).astype(BF16)

    each(4, projections, 0)
    f_share.wait()
    spread(f_kv[0], bk, bk_t)
    spread(f_kv[1], bv, bv_t)

    def attend(n):
        here = cells(n)
        score = matmul(bk[...], query[:, here]) * HEAD_DIM**-0.5
        score = score.reshape(HEADS, SLOTS, 256)
        top = jnp.max(score, axis=1, keepdims=True)
        grown = jnp.exp(score - top)
        soft = grown / jnp.sum(grown, axis=1, keepdims=True)
        soft_low = soft.reshape(CHANNELS, 256).astype(BF16)
        prob[:, here] = soft_low
        gprob = matmul(bv[...], gatt[:, here]).reshape(HEADS, SLOTS, 256)
        mean = jnp.sum(soft * gprob, axis=1, keepdims=True)
        gs = (HEAD_DIM**-0.5 * soft * (gprob - mean)).reshape(CHANNELS, 256).astype(BF16)
        gscore[:, here] = gs

    def attend_more(n):
        here = cells(n)
        attended = matmul(bv_t[...], prob[:, here]).astype(BF16)
        att[:, here] = attended
        block_ref[:, here] = (
            hid[:, here].astype(F32) + matmul(ow_ref[...], attended)
        ).astype(BF16)
        gq = matmul(bk_t[...], gscore[:, here]).astype(BF16)
        gquery[:, here] = gq
        ghid[:, here] = (up_ref[:, here].astype(F32) + matmul(qw_t[...], gq)).astype(BF16)

    each(4, attend, 0)

    gkv[0] = diagonal(against(gscore[...], query[...])).astype(BF16)
    gkv[1] = diagonal(against(prob[...], gatt[...])).astype(BF16)
    row_sum = RowSum(img, row, gkv, s_inbox, s_sum_sems)
    row_sum.start()

    each(4, attend_more, 0)

    def core_copy(t):
        return remote(
            grads.at[t, rows16((1 - core) * 10, 160)], in_core.at[t], core_sems, t, partner
        )

    grads[0] = against(gquery[...], hid[...]).astype(BF16)
    core_copy(0).start()
    grads[1] = against(up_ref[...], att[...]).astype(BF16)
    core_copy(1).start()

    def tap(t):
        a, b = lax.div(t - 2, 3), lax.rem(t - 2, 3)
        field = taps[
            pl.ds(pl.multiple_of(b * CHANNELS, CHANNELS), CHANNELS),
            pl.ds(pl.multiple_of(a * 128, 128), 1024),
        ]
        grads[t] = against(ghid[...], field).astype(BF16)
        core_copy(t).start()

    def x_first(j):
        return j % 2 == 1

    def at(axis_x, k):
        return device(z, at_x(k), y, core) if axis_x else device(z, x, at_y(k), core)

    def s1_copy(j, k):
        src = half.at[j, at_x(k)] if x_first(j) else half.at[j, :, at_y(k)]
        return remote(src, in_1.at[j, k - 1], s1_sems, 3 * j + k - 1, at(x_first(j), k))

    def s2_copy(j, k):
        src = mid.at[j, at_y(k) if x_first(j) else at_x(k)]
        return remote(src, in_2.at[j, k - 1], s2_sems, 3 * j + k - 1, at(not x_first(j), k))

    def z_copy(k):
        to = at_z(k)
        return remote(
            sum_f.at[lax.rem(to, 7)], in_z.at[k - 1], z_sems, k - 1, device(to, x, y, core)
        )

    def to_owner(k, act):
        pl.when(at_z(k) < 7)(lambda: act(k))

    def from_owner(k, act):
        pl.when(lax.rem(z + 8 - k, 8) < 7)(lambda: act(k))

    def across_cores(j, begin, end):
        each(end, lambda t: core_copy(t).wait_recv(), begin)

        def add(u):
            unit = 16 * j + u
            t, i = lax.div(unit, 10), lax.rem(unit, 10)
            half[j, lax.div(u, 4), lax.rem(u, 4)] = (
                grads[t, rows16(core * 10 + i)].astype(F32) + in_core[t, rows16(i)].astype(F32)
            ).astype(BF16)

        each(min(16, TAPS * 10 - 16 * j), add, 0)
        each(4, lambda k: s1_copy(j, k).start())

    def across_first(j):
        each(4, lambda k: s1_copy(j, k).wait_recv())
        own = half[j, x] if x_first(j) else half[j, :, y]
        mid[j] = total_of(4, own, lambda k: in_1[j, k - 1]).astype(BF16)
        each(4, lambda k: s2_copy(j, k).start())

    def across_second(j):
        each(4, lambda k: s2_copy(j, k).wait_recv())
        own = mid[j, y if x_first(j) else x]
        sum_f[j] = total_of(4, own, lambda k: in_2[j, k - 1]).astype(BF16)
        pl.when(z != j)(lambda: z_copy(lax.rem(j + 8 - z, 8)).start())

    half[SLICES - 1, 3, pl.ds(2, 2)] = jnp.zeros((2, 16, CHANNELS), BF16)
    pick = PickFour(img, row, s_all, s_give, s_got, s_img_sems, s_pair_sems)
    each(3, tap, 2)
    pick.start(row_sum.total().astype(BF16))
    across_cores(0, 0, 2)
    each(5, tap, 3)
    across_cores(1, 2, 4)
    each(6, tap, 5)
    across_cores(2, 4, 5)
    each(8, tap, 6)
    across_cores(3, 5, 7)
    each(9, tap, 8)
    across_cores(4, 7, 8)
    across_first(0)
    each(11, tap, 9)
    across_cores(5, 8, 10)
    across_cores(6, 10, 11)
    zi = lax.rem(z, 7)

    def kz_copy(k):
        to = at_z(k)
        return remote(
            k_quarter.at[:, lax.rem(to, 7)], k_z.at[k - 1], kz_sems, k - 1, device(to, x, y, core)
        )

    def g1_copy(j, k):
        mine = final.at[core, j, x, y]
        return remote(mine, mine, g1_sems, 3 * j + k - 1, at(not x_first(j), k))

    def g2_copy(j, k):
        mine = final.at[core, j, x] if x_first(j) else final.at[core, j, :, y]
        return remote(mine, mine, g2_sems, 3 * j + k - 1, at(x_first(j), k))

    def core_pass(j, k):
        mine = (
            final.at[core, j, lax.rem(x + 4 - k, 4)]
            if x_first(j)
            else final.at[core, j, :, lax.rem(y + 4 - k, 4)]
        )
        return remote(mine, mine, gcore_sems, 4 * j + k, partner)

    def spread_second(j):
        @pl.when(z != j)
        def _():
            gz_copy(lax.rem(z + 8 - j, 8)).wait_recv()

        each(4, lambda k: g1_copy(j, k).start())

    def spread_first(j):
        each(4, lambda k: g1_copy(j, k).wait_recv())
        each(4, lambda k: g2_copy(j, k).start())
        core_pass(j, 0).start()

    def spread_core(j):
        def go(k):
            g2_copy(j, k).wait_recv()
            core_pass(j, k).start()

        each(4, go)

    def kgz1_copy(k):
        mine = k_final.at[core, low, 0, zi]
        return remote(mine, mine, kgz1_sems, k - 1, device(at_z(k), x, y, core))

    def kgx1_copy():
        mine = k_final.at[core, low, 0]
        return remote(mine, mine, kgx1_sems, 0, across)

    def kgx2_copy():
        mine = k_final.at[core, low, 1, zi]
        return remote(mine, mine, kgx2_sems, 0, across)

    def kgz2_copy(k):
        mine = k_final.at[core, :, 1, zi]
        return remote(mine, mine, kgz2_sems, k - 1, device(at_z(k), x, y, core))

    def kgc_copy(k):
        part_x, turn_of = ((low, 0), (0, 1), (1, 1), (1 - low, 0))[k]
        mine = k_final.at[core, part_x, turn_of]
        return remote(mine, mine, kgc_sems, k, partner)


    def wanted(m):
        return group_ref[4 * z + m]

    pick.relay(wanted)
    across_first(1)

    def put(m, value):
        s_image[m, lax.rem(row, 2), rows16(lax.div(row, 2))] = value

    pick.result(wanted, put)
    share = Gather(
        ROWS, row, lambda j: (img, j),
        lambda j: s_image.at[:, lax.rem(j, 2), rows16(lax.div(j, 2))], s_row_sems,
    )
    share.start()
    across_first(2)
    across_second(0)
    across_first(3)
    across_second(1)
    share.wait()
    each(4, lambda k: quarter_copy(k).wait_recv())
    for side in range(2):
        total = jnp.zeros((224, CHANNELS), F32)
        for m in range(4):
            total = total + matmul(four_cond[m].reshape(224, SLOTS), s_image[m, side])
        k_quarter[:, :, :, side * CHANNELS : (side + 1) * CHANNELS] = total.astype(BF16).reshape(
            2, 7, 16, CHANNELS
        )
    each(8, lambda k: to_owner(k, lambda i: kz_copy(i).start()))
    across_first(4)
    across_second(2)
    across_first(5)
    across_second(3)
    across_first(6)
    across_second(4)
    across_second(5)
    across_second(6)
    @pl.when(z < 7)
    def _():
        each(8, lambda k: z_copy(k).wait_recv())
        done = total_of(8, sum_f[zi], lambda k: in_z[k - 1]) * weight_scale
        final[core, zi, x, y] = done.astype(BF16)

    def gz_copy(k):
        mine = final.at[core, zi, x, y]
        return remote(mine, mine, gz_sems, k - 1, device(at_z(k), x, y, core))

    @pl.when(z < 7)
    def _():
        each(8, lambda k: gz_copy(k).start())

    @pl.when(z < 7)
    def _():
        each(8, lambda k: kz_copy(k).wait_recv())
        done = (total_of(8, k_quarter[:, zi], lambda k: k_z[k - 1]) * kv_scale).astype(BF16)
        k_final[core, low, 0, zi] = done[0]
        k_final[core, low, 1, zi] = done[1]
        kgx2_copy().start()
        each(8, lambda k: kgz1_copy(k).start())

    image = jnp.concatenate([s_image[member, 0], s_image[member, 1]], axis=1)
    gcond = against(kvw_ref[...], image).astype(BF16)
    spot = lax.broadcasted_iota(jnp.int32, (SLOTS, tokens), 1)
    slot = lax.broadcasted_iota(jnp.int32, (SLOTS, tokens), 0) + slot_ref[0]
    ghidden_ref[...] = matmul(gcond, (spot == slot).astype(BF16)).astype(BF16)

    @pl.when(z < 7)
    def _():
        kgx2_copy().wait_recv()
        each(8, lambda k: kgz2_copy(k).start())

    each(5, unflatten, 0)
    for j in range(SLICES):
        spread_second(j)
    for j in range(SLICES):
        spread_first(j)
    each(8, lambda k: from_owner(k, lambda i: kgz1_copy(i).wait_recv()))
    kgx1_copy().start()
    kgc_copy(0).start()
    for j in range(0, 4):
        spread_core(j)
    each(8, lambda k: from_owner(k, lambda i: kgz2_copy(i).wait_recv()))
    kgc_copy(1).start()
    kgc_copy(2).start()
    for j in range(4, SLICES):
        spread_core(j)
    kgx1_copy().wait_recv()
    kgc_copy(3).start()

    for j in range(SLICES):
        each(4, lambda k, j=j: core_pass(j, k).wait_recv(), 0)

    for t in range(TAPS):
        target, base = ((query_ref, 0), (out_ref, 0))[t] if t < 2 else (res_ref, (t - 2) * CHANNELS)
        for c in range(2):
            for i in range(10):
                j, rest = divmod(t * 10 + i, 16)
                target[pl.ds(base + c * 160 + i * 16, 16)] = final[c, j, rest // 4, rest % 4]
    for k in range(4):
        kgc_copy(k).wait_recv()
    for unit in range(52):
        q, rest = divmod(unit, 14)
        kvout_ref[pl.ds(16 * unit, 16)] = k_final[q // 2, q % 2, rest // 7, rest % 7]

    pl.when(below)(lambda: halo_up().wait_send())
    pl.when(above)(lambda: halo_down().wait_send())
    for one in (f_sum, f_pick, f_share, row_sum, pick, share):
        one.finish()
    each(TAPS, lambda t: core_copy(t).wait_send(), 0)
    for j in range(SLICES):
        for copy in (s1_copy, s2_copy, g1_copy, g2_copy):
            each(4, lambda k, copy=copy, j=j: copy(j, k).wait_send())
        each(4, lambda k, j=j: core_pass(j, k).wait_send(), 0)
    each(8, lambda k: to_owner(k, lambda i: z_copy(i).wait_send()))
    each(8, lambda k: to_owner(k, lambda i: kz_copy(i).wait_send()))
    each(4, lambda k: quarter_copy(k).wait_send())

    @pl.when(z < 7)
    def _():
        for copy in (gz_copy, kgz1_copy, kgz2_copy):
            each(8, lambda k, copy=copy: copy(k).wait_send())
        kgx2_copy().wait_send()

    kgx1_copy().wait_send()
    for k in range(4):
        kgc_copy(k).wait_send()


FINISH_PARTS = (1, 1, 4, 4, 4, 3)


def finish_kernel(*refs):
    count = (len(refs) - 1) // 3
    sems = refs[-1]
    loads, stores = [], []
    for i in range(count):
        rows = refs[i].shape[0]
        pieces = FINISH_PARTS[i]
        for p in range(pieces):
            here = pl.ds(p * (rows // pieces), rows // pieces)
            slot = len(loads)
            held = refs[2 * count + i].at[here]
            loads.append(pltpu.make_async_copy(refs[i].at[here], held, sems.at[0, slot]))
            stores.append(pltpu.make_async_copy(held, refs[count + i].at[here], sems.at[1, slot]))
    for load in loads:
        load.start()
    for load, store in zip(loads, stores):
        load.wait()
        store.start()
    for store in stores:
        store.wait()


def finish(arrays):
    anywhere = pl.BlockSpec(memory_space=pl.ANY)
    return pl.pallas_call(
        finish_kernel,
        out_shape=tuple(jax.ShapeDtypeStruct(a.shape, a.dtype) for a in arrays),
        in_specs=[anywhere] * len(arrays),
        out_specs=(anywhere,) * len(arrays),
        scratch_shapes=[pltpu.VMEM(a.shape, a.dtype) for a in arrays]
        + [pltpu.SemaphoreType.DMA((2, sum(FINISH_PARTS)))],
        compiler_params=pltpu.CompilerParams(vmem_limit_bytes=62 * 2**20),
        name="finish",
    )(*arrays)


def shards(
    llm_hidden,
    slot_start,
    image_group,
    timesteps,
    latents,
    noise,
    kv_weight,
    in_weight,
    res_weight,
    query_weight,
    out_weight,
    cotangent,
):
    width, features = CHANNELS, llm_hidden.shape[1]
    frequency = jnp.exp(-math.log(10000.0) * jnp.arange(width // 2, dtype=F32) / (width // 2))
    angles = timesteps[0].astype(F32) * frequency
    emb = jnp.concatenate([jnp.cos(angles), jnp.sin(angles)])[:, None]
    vmem, smem = pl.BlockSpec(memory_space=pltpu.VMEM), pl.BlockSpec(memory_space=pltpu.SMEM)
    anywhere = pl.BlockSpec(memory_space=pl.ANY)
    dma = lambda n: pltpu.SemaphoreType.DMA((2, n))
    low = lambda *shape: pltpu.VMEM(shape, BF16)
    field, square = low(width, 1024), low(width, width)
    out = lambda *shape: jax.ShapeDtypeStruct(shape, BF16)
    block, res, query, projection, grad_hidden, grad_kv_weight = pl.pallas_call(
        functools.partial(
            kernel,
            weight_scale=(IMGS * ROWS * 1024) ** (-0.5),
            kv_scale=(IMGS * SLOTS) ** (-0.5),
        ),
        out_shape=(
            out(width, 8, 128), out(9 * width, width), out(width, width), out(width, width),
            out(features, llm_hidden.shape[0]), out(*kv_weight.shape),
        ),
        in_specs=[smem] * 3 + [vmem] * 8 + [anywhere] * 2,
        out_specs=(vmem,) * 6,
        scratch_shapes=[
            low(9, width, width), low(width, 8, 128), pltpu.SemaphoreType.DMA((2,)),
            pltpu.VMEM((72, width), F32), low(width, 72), pltpu.VMEM((64, 8, 128), F32), field, field,
            pltpu.VMEM((4, 8, 128), F32), pltpu.VMEM((12, 8, 128), F32),
            low(features, SLOTS), pltpu.VMEM((2, SLOTS, width), F32),
            pltpu.VMEM((ROWS - 1, 16, width), F32), low(IMGS // 2, 16, width),
            low(16, width), low(16, width), low(2, SLOTS, width),
            low(3, width, 3 * width), square, square,
            low(3 * width, 1280), pltpu.VMEM((width, 1280), F32),
            field, field, field, field, field, field, field, field, square, square, square, square,
            low(2, SLOTS, width), low(ROWS - 1, 16, width), low(IMGS // 2, 16, width),
            low(4, 16, width), low(4, 16, width), low(4, 2, SLOTS, width),
            low(TAPS, width, width), low(TAPS, 160, width), low(SLICES, 4, 4, 16, width),
            low(SLICES, 3, 4, 16, width), low(SLICES, 4, 16, width), low(SLICES, 3, 16, width),
            low(SLICES, 16, width), low(7, 16, width), low(2, SLICES, 4, 4, 16, width),
            low(4, 14, 16, SLOTS), low(4, 14, 16, SLOTS), low(2, 7, 16, 2 * width),
            low(7, 2, 16, 2 * width), low(2, 2, 2, 7, 16, 2 * width),
            dma(2), dma(7), dma(15), dma(1), dma(7),
            dma(7), dma(15), dma(1), dma(7),
            dma(TAPS), dma(3 * SLICES), dma(3 * SLICES), dma(7),
            dma(7), dma(3 * SLICES), dma(3 * SLICES), dma(4 * SLICES),
            dma(3), dma(7),
            dma(7), dma(1), dma(1), dma(7), dma(4),
        ],
        compiler_params=pltpu.CompilerParams(
            collective_id=0, has_side_effects=True, vmem_limit_bytes=60 * 2**20
        ),
        name="block",
    )(
        image_group, slot_start, timesteps, llm_hidden.T, kv_weight, latents[0], noise[0], emb,
        in_weight.transpose(0, 1, 3, 2).reshape(9, 4, width), query_weight, out_weight,
        res_weight.reshape(9, width, width), cotangent[0],
    )
    query, projection, block, grad_hidden, grad_kv_weight, res = finish(
        (query, projection, block, grad_hidden, grad_kv_weight, res.reshape(3, 3, width, width))
    )
    return block[None], grad_hidden.T, grad_kv_weight, res, query, projection


def solution(mesh):
    return jax.shard_map(
        shards,
        mesh=mesh,
        in_specs=(
            P("img", "row"),
            P("img"),
            P(),
            P("img"),
            P("img", None, "row", None),
            P("img", None, "row", None),
            P("row", None),
            P(),
            P(),
            P(),
            P(),
            P("img", None, "row", None),
        ),
        out_specs=(P("img", None, "row", None), P("img", "row"), P("row", None), P(), P(), P()),
        check_vma=False,
    )
```
